32 devices in a mesh: seq: 8 (over z, x), tp: 4 (over y, core).
Axes of the slice: x: 2, y: 2, z: 4, core: 2. Of those that a mesh axis runs over, the one named last changes fastest.
Arguments:
- stream: float32 [8192, 2048], P('seq', 'tp')
- norm1_gain: float32 [2048], P('tp'), may hold values from 0.25 to 1.75
- in_weight: bfloat16 [2048, 3, 2048], P('seq', None, 'tp'), may hold values from -0.125 to 0.125
- conv_weight: float32 [3, 2048], P(None, 'tp'), may hold values from -3 to 3
- out_weight: bfloat16 [2048, 2048], P('seq', 'tp'), may hold values from -0.125 to 0.125
- norm2_gain: float32 [2048], P('tp'), may hold values from 0.25 to 1.75
- gate_weight: bfloat16 [2048, 8192], P('seq', 'tp'), may hold values from -0.125 to 0.125
- up_weight: bfloat16 [2048, 8192], P('seq', 'tp'), may hold values from -0.125 to 0.125
- down_weight: bfloat16 [2048, 8192], P('seq', 'tp'), may hold values from -0.09375 to 0.09375
- doc_starts: int32 [4], replicated, may hold values from 0 to 7167, as said below
- out_grad: float32 [8192, 2048], P('seq', 'tp'), may hold values from -6 to 6
Outputs:
- result: float32 [8192, 2048], P('seq', 'tp')
- stream_grad: float32 [8192, 2048], P('seq', 'tp')
- norm1_gain_grad: float32 [2048], P('tp')
- in_weight_grad: float32 [2048, 3, 2048], P('seq', None, 'tp')
- conv_weight_grad: float32 [3, 2048], P(None, 'tp')
- out_weight_grad: float32 [2048, 2048], P('seq', 'tp')
- norm2_gain_grad: float32 [2048], P('tp')
- gate_weight_grad: float32 [2048, 8192], P('seq', 'tp')
- up_weight_grad: float32 [2048, 8192], P('seq', 'tp')
- down_weight_grad: float32 [2048, 8192], P('seq', 'tp')
- rms_values: float32 [2, 8192], P(None, 'seq')
The draws below stay inside these ranges and needn't reach their ends.
Inputs may be any that keep to these rules, and one draw needn't show every extreme that they name: doc_starts[0] = 0; for 1 <= j < 3, doc_starts[j] lies between 2 j * 1024 + 2 and 2 j * 1024 + 1023; when 4 > 1 the last entry is exactly 2 (3) * 1024 + 1023; so the entries rise.
All inputs are finite; a program needn't handle non-finite values.
Results may differ from the reference program's by a relative error of at most 0.0094.
Values may be sent and summed in bfloat16 or wider, within the bound.
A program may use at most 320 MiB of HBM per device.

```python
import math
from functools import partial
import jax
import jax.numpy as jnp
from jax import lax

D = 2048
FF = 8192
TAPS = 3
TOK = 1024
TOKENS = 8192
DOCS = 4


def draw_stream(key, part):
    key = jax.random.fold_in(key, 3)
    key_rows, key_cols, key_base = jax.random.split(key, 3)
    row_scale = 0.3 * jnp.exp(jax.random.uniform(key_rows, (TOKENS, 1), jnp.float32) * math.log(10.0))
    rough = jnp.exp(jax.random.uniform(key_cols, (1, D), jnp.float32, minval=-0.4, maxval=0.4))
    rising = jnp.exp(jnp.linspace(math.log(0.5), math.log(1.5), D, dtype=jnp.float32))[None, :]
    base = jax.random.normal(key_base, (TOKENS, D), jnp.float32)
    return (base * row_scale * rising * rough).astype(jnp.float32)


def draw_doc_starts(key, part):
    key = jax.random.fold_in(key, 7)
    offsets = jax.random.randint(key, (DOCS,), 2, TOK, dtype=jnp.int32)
    index = jnp.arange(DOCS, dtype=jnp.int32)
    offsets = jnp.where(index == DOCS - 1, TOK - 1, offsets)
    firsts = index * (2 * TOK)
    starts = firsts + offsets
    return jnp.where(index == 0, 0, starts).astype(jnp.int32)


def levels(rng, shape, cuts, smallest, high):
    def one(axis_at, blocks):
        draws = jax.random.uniform(jax.random.fold_in(jax.random.fold_in(rng, 6), axis_at), (blocks,), jnp.float32, smallest / len(cuts), high / len(cuts))
        return jnp.repeat(jnp.exp(draws), shape[axis_at] // blocks).reshape((-1,) + (1,) * (len(shape) - axis_at - 1))

    factor_of = one(*cuts[0])
    for cut in cuts[1:]:
        factor_of = factor_of * one(*cut)
    return factor_of


def gaussian(stream_key, shape, scale, bound, cuts=(), kind=jnp.bfloat16):
    values = jax.random.normal(stream_key, shape, jnp.float32) * scale
    if len(cuts) > 0:
        values = levels(stream_key, shape, cuts, -0.22, 0.18) * values
    return jnp.clip(values, min=-bound, max=bound).astype(kind)


def setup_inputs(seed: int = 0) -> dict:
    seeds = jax.random.split(jax.random.key(seed), 12)
    stream = draw_stream(jax.random.fold_in(seeds[11], 71), 0)
    norm1_gain = jnp.clip(1.0 + 0.15 * jax.random.normal(seeds[1], (D,), jnp.float32), 0.25, 1.75)
    in_weight = gaussian(seeds[2], (D, 3, D), D ** -0.5, 0.125, ((0, 8), (2, 4)))
    conv_weight = gaussian(seeds[3], (TAPS, D), 0.6, 3.0, ((1, 4),), jnp.float32)
    out_weight = gaussian(seeds[4], (D, D), D ** -0.5, 0.125, ((0, 8), (1, 4)))
    norm2_gain = jnp.clip(1.0 + 0.15 * jax.random.normal(seeds[5], (D,), jnp.float32), 0.25, 1.75)
    gate_weight = gaussian(seeds[6], (D, FF), D ** -0.5, 0.125, ((0, 8), (1, 4)))
    up_weight = gaussian(seeds[7], (D, FF), D ** -0.5, 0.125, ((0, 8), (1, 4)))
    down_weight = gaussian(seeds[8], (D, FF), (FF // 2) ** -0.5, 0.09375, ((0, 8), (1, 4)))
    doc_starts = draw_doc_starts(jax.random.fold_in(seeds[11], 71), 0)
    out_grad = gaussian(seeds[10], (TOKENS, D), 1.0, 6.0, ((0, 8), (1, 4)), jnp.float32)
    return dict(stream=stream, norm1_gain=norm1_gain, in_weight=in_weight, conv_weight=conv_weight, out_weight=out_weight, norm2_gain=norm2_gain, gate_weight=gate_weight, up_weight=up_weight, down_weight=down_weight, doc_starts=doc_starts, out_grad=out_grad)


epsilon = 1e-05

@jax.custom_vjp
def low(v):
    return lax.optimization_barrier(v.astype(jnp.bfloat16)).astype(jnp.float32)

@jax.custom_vjp
def low_back(v):
    return v

def low_keep(v):
    return (low(v), None)

def low_pass(kept, grad):
    return (grad,)

def back_keep(v):
    return (v, None)

def back_low(kept, grad):
    return (low(grad),)
low.defvjp(low_keep, low_pass)
low_back.defvjp(back_keep, back_low)

def product(left, right):
    return jnp.dot(left, right, precision=lax.Precision.HIGHEST, preferred_element_type=jnp.float32)

def doc_count(doc_starts, positions):
    return lax.optimization_barrier(jnp.sum((doc_starts[None, :] <= positions[:, None]).astype(jnp.int32), axis=1))

def lag_masks(doc_starts, positions):
    current = doc_count(doc_starts, positions)
    one = (positions >= 1) & (doc_count(doc_starts, positions - 1) == current)
    two = (positions >= 2) & (doc_count(doc_starts, positions - 2) == current)
    return (one.astype(jnp.float32)[:, None], two.astype(jnp.float32)[:, None])

def rms_norm(values, gain):
    mean_square = lax.optimization_barrier(jnp.mean(values * values, axis=1, keepdims=True))
    return (values * lax.rsqrt(mean_square + epsilon) * gain, jnp.sqrt(mean_square[:, 0] + epsilon))

def block_step(weights_all, doc_starts, carry, inputs):
    block_rows, first = inputs
    norm1_gain, in_weight, conv_weight, out_weight, norm2_gain, gate_weight, up_weight, down_weight = weights_all
    length = block_rows.shape[0]
    width = block_rows.shape[1]
    positions = first + jnp.arange(length, dtype=jnp.int32)
    mask_one, mask_two = lag_masks(doc_starts, positions)
    normed_in, rms_in = rms_norm(block_rows, norm1_gain)
    normed_in = low(normed_in)
    projected = low_back(product(normed_in, in_weight.reshape(width, 3 * width)))
    in_gate = projected[:, :width]
    out_gate = projected[:, width:2 * width]
    carried = projected[:, 2 * width:]
    mixed = in_gate * carried
    extended = jnp.concatenate([carry, mixed], axis=0)
    convolved = conv_weight[0] * mixed + mask_one * conv_weight[1] * extended[1:-1] + mask_two * conv_weight[2] * extended[:-2]
    gated = low(out_gate * convolved)
    middle = block_rows + low_back(product(gated, out_weight.T))
    normed_mid, rms_mid = rms_norm(middle, norm2_gain)
    normed_mid = low(normed_mid)
    gate = low_back(product(normed_mid, gate_weight))
    upward = low_back(product(normed_mid, up_weight))
    hidden = low(jax.nn.silu(gate) * upward)
    result = middle + low_back(product(hidden, down_weight.T))
    return (mixed[-2:], (result, jnp.stack([rms_in, rms_mid])))

def reference(stream, norm1_gain, in_weight, conv_weight, out_weight, norm2_gain, gate_weight, up_weight, down_weight, doc_starts, out_grad):
    span = 2 * TOK
    blocks = TOKENS // span
    weights_all = tuple((w.astype(jnp.float32) for w in (norm1_gain, in_weight, conv_weight, out_weight, norm2_gain, gate_weight, up_weight, down_weight)))

    def forward(rows_all, weights_given):
        stepper = jax.checkpoint(partial(block_step, weights_given, doc_starts))
        carry = jnp.zeros((2, D), jnp.float32)
        firsts = jnp.arange(blocks, dtype=jnp.int32) * span
        unused, (results, rms_blocks) = lax.scan(stepper, carry, (rows_all.reshape(blocks, span, D), firsts))
        rms_values = jnp.transpose(rms_blocks, (1, 0, 2)).reshape(2, TOKENS)
        return (results.reshape(TOKENS, D), rms_values)
    result, pullback, rms_values = jax.vjp(forward, stream.astype(jnp.float32), weights_all, has_aux=True)
    stream_grad, weight_grads = pullback(out_grad.astype(jnp.float32))
    return (result, stream_grad, weight_grads[0], weight_grads[1], weight_grads[2], weight_grads[3], weight_grads[4], weight_grads[5], weight_grads[6], weight_grads[7], rms_values)
```

```python
import jax
import jax.numpy as jnp
from jax import lax
from jax.sharding import PartitionSpec as P

epsilon = 1e-05


def from_behind(shard, axis, by):
    count = lax.axis_size(axis)
    pairs = [(i, i + by) for i in range(count) if 0 <= i + by < count]
    return lax.ppermute(shard, axis, pairs)


def doc_count(doc_starts, positions):
    return jnp.sum((doc_starts[None, :] <= positions[:, None]).astype(jnp.int32), axis=1)


def lag_masks(doc_starts, positions):
    current = doc_count(doc_starts, positions)
    one = (positions >= 1) & (doc_count(doc_starts, positions - 1) == current)
    two = (positions >= 2) & (doc_count(doc_starts, positions - 2) == current)
    return (one.astype(jnp.float32)[:, None], two.astype(jnp.float32)[:, None])


def contract_rows(left, right):
    return lax.dot_general(
        left, right, (((0,), (0,)), ((), ())), preferred_element_type=jnp.float32
    )


def contract_cols(left, right):
    return lax.dot_general(
        left, right, (((1,), (1,)), ((), ())), preferred_element_type=jnp.float32
    )


def reduce_tp(partial_rows):
    return lax.psum_scatter(
        partial_rows.astype(jnp.bfloat16), "tp", scatter_dimension=1, tiled=True
    ).astype(jnp.float32)


def reduce_seq(partial_grad):
    return lax.psum_scatter(
        partial_grad.astype(jnp.bfloat16), "seq", scatter_dimension=0, tiled=True
    ).astype(jnp.float32)


def gather_grads(grad_rows):
    return lax.all_gather(grad_rows, "tp", axis=1, tiled=True)


def normalize(values, gain):
    width = gain.shape[0] * lax.axis_size("tp")
    squares = lax.psum(jnp.sum(values * values, axis=1, keepdims=True), "tp")
    inverse = lax.rsqrt(squares / width + epsilon)
    normed = lax.all_gather(
        (values * inverse * gain).astype(jnp.bfloat16), "tp", axis=1, tiled=True
    )
    return (normed, inverse, jnp.sqrt(squares[:, 0] / width + epsilon))


def norm_backward(values, gain, inverse, grad_rows):
    width = gain.shape[0] * lax.axis_size("tp")
    gained = gain * grad_rows
    total = lax.psum(jnp.sum(values * gained, axis=1, keepdims=True), "tp")
    grad_values = inverse * gained - values * inverse**3 * (total / width)
    grad_gain = jnp.sum(grad_rows * values * inverse, axis=0)
    return (grad_values, grad_gain)


def on_device(
    stream,
    norm1_gain,
    in_weight,
    conv_weight,
    out_weight,
    norm2_gain,
    gate_weight,
    up_weight,
    down_weight,
    doc_starts,
    out_grad,
):
    tokens = stream.shape[0]
    local = stream.shape[1]
    rows_here = in_weight.shape[0]
    whole_in, whole_out, whole_gate, whole_up, whole_down = (
        lax.all_gather(in_weight, "seq", axis=0, tiled=True),
        lax.all_gather(out_weight, "seq", axis=0, tiled=True),
        lax.all_gather(gate_weight, "seq", axis=0, tiled=True),
        lax.all_gather(up_weight, "seq", axis=0, tiled=True),
        lax.all_gather(down_weight, "seq", axis=0, tiled=True),
    )
    width = whole_out.shape[0]
    in_matrix = whole_in.reshape(width, 3 * local)
    positions = lax.axis_index("seq") * tokens + jnp.arange(tokens, dtype=jnp.int32)
    mask_one, mask_two = lag_masks(doc_starts, positions)
    normed_in, inverse_in, rms_in = normalize(stream, norm1_gain)
    projected = jnp.dot(normed_in, in_matrix, preferred_element_type=jnp.float32)
    in_gate = projected[:, :local]
    out_gate = projected[:, local : 2 * local]
    carried = projected[:, 2 * local :]
    mixed = in_gate * carried
    previous = from_behind(mixed[-2:], "seq", 1)
    extended = jnp.concatenate([previous, mixed], axis=0)
    convolved = (
        conv_weight[0] * mixed
        + mask_one * conv_weight[1] * extended[1:-1]
        + mask_two * conv_weight[2] * extended[:-2]
    )
    gated = (out_gate * convolved).astype(jnp.bfloat16)
    middle = stream + reduce_tp(contract_cols(gated, whole_out))
    normed_mid, inverse_mid, rms_mid = normalize(middle, norm2_gain)
    gate = jnp.dot(normed_mid, whole_gate, preferred_element_type=jnp.float32)
    upward = jnp.dot(normed_mid, whole_up, preferred_element_type=jnp.float32)
    hidden = (jax.nn.silu(gate) * upward).astype(jnp.bfloat16)
    result = middle + reduce_tp(contract_cols(hidden, whole_down))
    out_full = gather_grads(out_grad.astype(jnp.bfloat16))
    hidden_grad = jnp.dot(out_full, whole_down, preferred_element_type=jnp.float32)
    sigmoid_gate = jax.nn.sigmoid(gate)
    gate_rows = (hidden_grad * upward * sigmoid_gate * (1.0 + gate * (1.0 - sigmoid_gate))).astype(
        jnp.bfloat16
    )
    up_rows = (hidden_grad * gate * sigmoid_gate).astype(jnp.bfloat16)
    normed_mid_grad = reduce_tp(
        contract_cols(gate_rows, whole_gate) + contract_cols(up_rows, whole_up)
    )
    middle_norm_grad, gain_mid_grad = norm_backward(
        middle, norm2_gain, inverse_mid, normed_mid_grad
    )
    middle_grad = out_grad + middle_norm_grad
    branch_full = gather_grads(middle_grad.astype(jnp.bfloat16))
    gated_grad = jnp.dot(branch_full, whole_out, preferred_element_type=jnp.float32)
    out_gate_grad = gated_grad * convolved
    conv_grad = gated_grad * out_gate
    lag_one = mask_one * conv_grad
    lag_two = mask_two * conv_grad
    next_one, next_two = from_behind((lag_one[:2], lag_two[:2]), "seq", -1)
    after_one = jnp.concatenate([lag_one, next_one], axis=0)
    after_two = jnp.concatenate([lag_two, next_two], axis=0)
    mixed_grad = (
        conv_weight[0] * conv_grad
        + conv_weight[1] * after_one[1 : tokens + 1]
        + conv_weight[2] * after_two[2:]
    )
    tap_grads = jnp.stack(
        [
            jnp.sum(conv_grad * mixed, axis=0),
            jnp.sum(lag_one * extended[1:-1], axis=0),
            jnp.sum(lag_two * extended[:-2], axis=0),
        ]
    )
    projected_grad = jnp.concatenate(
        [mixed_grad * carried, out_gate_grad, mixed_grad * in_gate], axis=1
    ).astype(jnp.bfloat16)
    normed_in_grad = reduce_tp(contract_cols(projected_grad, in_matrix))
    stream_norm_grad, gain_in_grad = norm_backward(stream, norm1_gain, inverse_in, normed_in_grad)
    stream_grad = middle_grad + stream_norm_grad
    conv_total, gain_in_total, gain_mid_total = lax.psum(
        (tap_grads, gain_in_grad, gain_mid_grad), "seq"
    )
    down_weight_grad = reduce_seq(contract_rows(out_full, hidden))
    gate_weight_grad = reduce_seq(contract_rows(normed_mid, gate_rows))
    up_weight_grad = reduce_seq(contract_rows(normed_mid, up_rows))
    out_weight_grad = reduce_seq(contract_rows(branch_full, gated))
    in_weight_grad = reduce_seq(contract_rows(normed_in, projected_grad)).reshape(
        rows_here, 3, local
    )
    rms_values = jnp.stack([rms_in, rms_mid])
    return (
        result,
        stream_grad,
        gain_in_total,
        in_weight_grad,
        conv_total,
        out_weight_grad,
        gain_mid_total,
        gate_weight_grad,
        up_weight_grad,
        down_weight_grad,
        rms_values,
    )


def solution(mesh):
    return jax.shard_map(
        on_device,
        mesh=mesh,
        in_specs=(
            P("seq", "tp"),
            P("tp"),
            P("seq", None, "tp"),
            P(None, "tp"),
            P("seq", "tp"),
            P("tp"),
            P("seq", "tp"),
            P("seq", "tp"),
            P("seq", "tp"),
            P(),
            P("seq", "tp"),
        ),
        out_specs=(
            P("seq", "tp"),
            P("seq", "tp"),
            P("tp"),
            P("seq", None, "tp"),
            P(None, "tp"),
            P("seq", "tp"),
            P("tp"),
            P("seq", "tp"),
            P("seq", "tp"),
            P("seq", "tp"),
            P(None, "seq"),
        ),
        check_vma=False,
    )
```

```python
import jax
import jax.numpy as jnp
from jax import lax
from jax.experimental import pallas as pl
from jax.experimental.pallas import tpu as pltpu
from jax.sharding import Mesh, PartitionSpec as P

epsilon = 1e-05


def from_behind(shard, axis, by):
    count = lax.axis_size(axis)
    pairs = [(i, i + by) for i in range(count) if 0 <= i + by < count]
    return lax.ppermute(shard, axis, pairs)


def doc_count(doc_starts, positions):
    return jnp.sum((doc_starts[None, :] <= positions[:, None]).astype(jnp.int32), axis=1)


def lag_masks(doc_starts, positions):
    current = doc_count(doc_starts, positions)
    one = (positions >= 1) & (doc_count(doc_starts, positions - 1) == current)
    two = (positions >= 2) & (doc_count(doc_starts, positions - 2) == current)
    return (one.astype(jnp.float32)[:, None], two.astype(jnp.float32)[:, None])


def contract_rows(left, right):
    return lax.dot_general(
        left, right, (((0,), (0,)), ((), ())), preferred_element_type=jnp.float32
    )


def contract_cols(left, right):
    return lax.dot_general(
        left, right, (((1,), (1,)), ((), ())), preferred_element_type=jnp.float32
    )


def reduce_tp(partial_rows):
    return lax.psum_scatter(
        partial_rows.astype(jnp.bfloat16), "tp", scatter_dimension=1, tiled=True
    ).astype(jnp.float32)


def reduce_seq(partial_grad):
    return lax.psum_scatter(
        partial_grad.astype(jnp.bfloat16), "seq", scatter_dimension=0, tiled=True
    ).astype(jnp.float32)


def gather_grads(grad_rows):
    return lax.all_gather(grad_rows, "tp", axis=1, tiled=True)


def normalize(values, gain):
    width = gain.shape[0] * lax.axis_size("tp")
    squares = lax.psum(jnp.sum(values * values, axis=1, keepdims=True), "tp")
    inverse = lax.rsqrt(squares / width + epsilon)
    normed = lax.all_gather(
        (values * inverse * gain).astype(jnp.bfloat16), "tp", axis=1, tiled=True
    )
    return (normed, inverse, jnp.sqrt(squares[:, 0] / width + epsilon))


def norm_backward(values, gain, inverse, grad_rows):
    width = gain.shape[0] * lax.axis_size("tp")
    gained = gain * grad_rows
    total = lax.psum(jnp.sum(values * gained, axis=1, keepdims=True), "tp")
    grad_values = inverse * gained - values * inverse**3 * (total / width)
    grad_gain = jnp.sum(grad_rows * values * inverse, axis=0)
    return (grad_values, grad_gain)


def on_device(
    stream,
    norm1_gain,
    in_weight,
    conv_weight,
    out_weight,
    norm2_gain,
    gate_weight,
    up_weight,
    down_weight,
    doc_starts,
    out_grad,
):
    tokens = stream.shape[0]
    local = stream.shape[1]
    rows_here = in_weight.shape[0]
    whole_in, whole_out, whole_gate, whole_up, whole_down = (
        lax.all_gather(in_weight, "seq", axis=0, tiled=True),
        lax.all_gather(out_weight, "seq", axis=0, tiled=True),
        lax.all_gather(gate_weight, "seq", axis=0, tiled=True),
        lax.all_gather(up_weight, "seq", axis=0, tiled=True),
        lax.all_gather(down_weight, "seq", axis=0, tiled=True),
    )
    width = whole_out.shape[0]
    in_matrix = whole_in.reshape(width, 3 * local)
    positions = lax.axis_index("seq") * tokens + jnp.arange(tokens, dtype=jnp.int32)
    mask_one, mask_two = lag_masks(doc_starts, positions)
    normed_in, inverse_in, rms_in = normalize(stream, norm1_gain)
    projected = jnp.dot(normed_in, in_matrix, preferred_element_type=jnp.float32)
    in_gate = projected[:, :local]
    out_gate = projected[:, local : 2 * local]
    carried = projected[:, 2 * local :]
    mixed = in_gate * carried
    previous = from_behind(mixed[-2:], "seq", 1)
    extended = jnp.concatenate([previous, mixed], axis=0)
    convolved = (
        conv_weight[0] * mixed
        + mask_one * conv_weight[1] * extended[1:-1]
        + mask_two * conv_weight[2] * extended[:-2]
    )
    gated = (out_gate * convolved).astype(jnp.bfloat16)
    middle = stream + reduce_tp(contract_cols(gated, whole_out))
    normed_mid, inverse_mid, rms_mid = normalize(middle, norm2_gain)
    gate = jnp.dot(normed_mid, whole_gate, preferred_element_type=jnp.float32)
    upward = jnp.dot(normed_mid, whole_up, preferred_element_type=jnp.float32)
    hidden = (jax.nn.silu(gate) * upward).astype(jnp.bfloat16)
    result = middle + reduce_tp(contract_cols(hidden, whole_down))
    out_full = gather_grads(out_grad.astype(jnp.bfloat16))
    hidden_grad = jnp.dot(out_full, whole_down, preferred_element_type=jnp.float32)
    sigmoid_gate = jax.nn.sigmoid(gate)
    gate_rows = (hidden_grad * upward * sigmoid_gate * (1.0 + gate * (1.0 - sigmoid_gate))).astype(
        jnp.bfloat16
    )
    up_rows = (hidden_grad * gate * sigmoid_gate).astype(jnp.bfloat16)
    normed_mid_grad = reduce_tp(
        contract_cols(gate_rows, whole_gate) + contract_cols(up_rows, whole_up)
    )
    middle_norm_grad, gain_mid_grad = norm_backward(
        middle, norm2_gain, inverse_mid, normed_mid_grad
    )
    middle_grad = out_grad + middle_norm_grad
    branch_full = gather_grads(middle_grad.astype(jnp.bfloat16))
    gated_grad = jnp.dot(branch_full, whole_out, preferred_element_type=jnp.float32)
    out_gate_grad = gated_grad * convolved
    conv_grad = gated_grad * out_gate
    lag_one = mask_one * conv_grad
    lag_two = mask_two * conv_grad
    next_one, next_two = from_behind((lag_one[:2], lag_two[:2]), "seq", -1)
    after_one = jnp.concatenate([lag_one, next_one], axis=0)
    after_two = jnp.concatenate([lag_two, next_two], axis=0)
    mixed_grad = (
        conv_weight[0] * conv_grad
        + conv_weight[1] * after_one[1 : tokens + 1]
        + conv_weight[2] * after_two[2:]
    )
    tap_grads = jnp.stack(
        [
            jnp.sum(conv_grad * mixed, axis=0),
            jnp.sum(lag_one * extended[1:-1], axis=0),
            jnp.sum(lag_two * extended[:-2], axis=0),
        ]
    )
    projected_grad = jnp.concatenate(
        [mixed_grad * carried, out_gate_grad, mixed_grad * in_gate], axis=1
    ).astype(jnp.bfloat16)
    normed_in_grad = reduce_tp(contract_cols(projected_grad, in_matrix))
    stream_norm_grad, gain_in_grad = norm_backward(stream, norm1_gain, inverse_in, normed_in_grad)
    stream_grad = middle_grad + stream_norm_grad
    conv_total, gain_in_total, gain_mid_total = lax.psum(
        (tap_grads, gain_in_grad, gain_mid_grad), "seq"
    )
    down_weight_grad = reduce_seq(contract_rows(out_full, hidden))
    gate_weight_grad = reduce_seq(contract_rows(normed_mid, gate_rows))
    up_weight_grad = reduce_seq(contract_rows(normed_mid, up_rows))
    out_weight_grad = reduce_seq(contract_rows(branch_full, gated))
    in_weight_grad = reduce_seq(contract_rows(normed_in, projected_grad)).reshape(
        rows_here, 3, local
    )
    rms_values = jnp.stack([rms_in, rms_mid])
    return (
        result,
        stream_grad,
        gain_in_total,
        in_weight_grad,
        conv_total,
        out_weight_grad,
        gain_mid_total,
        gate_weight_grad,
        up_weight_grad,
        down_weight_grad,
        rms_values,
    )


MESH = pl.DeviceIdType.MESH
BF = jnp.bfloat16
F32 = jnp.float32
ANY = pl.BlockSpec(memory_space=pl.ANY)
VMEM = pl.BlockSpec(memory_space=pltpu.VMEM)
OWN, MATE, NEAR, FAR = 0, 1, 2, 3


def remote(src, dst, send_sem, recv_sem, device):
    return pltpu.make_async_remote_copy(
        src_ref=src,
        dst_ref=dst,
        send_sem=send_sem,
        recv_sem=recv_sem,
        device_id=device,
        device_id_type=MESH,
    )


class Place:
    def __init__(self):
        self.zh, self.zl = lax.axis_index("zh"), lax.axis_index("zl")
        self.x, self.y, self.c = lax.axis_index("x"), lax.axis_index("y"), lax.axis_index("c")
        self.z = 2 * self.zh + self.zl
        self.inner = (self.z == 1) | (self.z == 2)
        self.outer = (self.z == 0) | (self.z == 3)
        self.rows = [self.z, 2 * self.zh + 1 - self.zl, 2 - self.zh, 3 - 3 * self.zh]
        self.mate = (self.zh, 1 - self.zl, self.x, self.y, self.c)
        self.mid = (1 - self.zh, 1 - self.zl, self.x, self.y, self.c)
        self.across = (self.zh, self.zl, 1 - self.x, self.y, self.c)

    def block(self, which, x):
        return self.rows[which] * 2 + x

    def enter(self):
        barrier = pltpu.get_barrier_semaphore()

        def greet(device):
            pl.semaphore_signal(barrier, inc=1, device_id=device, device_id_type=MESH)

        greet(self.mate)
        greet(self.across)

        @pl.when(self.inner)
        def _():
            greet(self.mid)

        @pl.when(self.inner)
        def _():
            pl.semaphore_wait(barrier, 3)

        @pl.when(self.outer)
        def _():
            pl.semaphore_wait(barrier, 2)


def in_stages(chunks):
    stages = len(chunks[0])
    for step in range(len(chunks) + stages - 1):
        for stage in range(stages):
            if 0 <= step - stage < len(chunks):
                chunks[step - stage][stage]()


def pair_gather_chunk(p, weight, out, relay, ss, rs, first, count, rows):
    half = out.shape[1]
    here = pl.ds(first, count)
    own = weight.at[here, pl.ds(pl.multiple_of(p.zl * half, half), half)]
    other = weight.at[here, pl.ds(pl.multiple_of((1 - p.zl) * half, half), half)]

    def block(which, x):
        return out.at[pl.ds(pl.multiple_of(p.block(which, x) * rows + first, count), count), :]

    held = [relay.at[i, here, :] for i in range(3)]

    def send(slot, src, dst, recv, device):
        return remote(src, dst, ss.at[slot], rs.at[recv], device)

    def arrived(recv, dst):
        remote(dst, dst, ss.at[0], rs.at[recv], p.mate).wait_recv()

    local = pltpu.make_async_copy(own, block(OWN, p.x), ss.at[11])
    across = [
        send(7 + k, own if k == OWN else block(k, p.x), block(k, p.x), 6 + k, p.across)
        for k in range(4)
    ]
    to_mate = send(0, other, block(OWN, p.x), 0, p.mate)
    outer_own = send(1, own, held[0], 3, p.mate)
    mid_other = send(3, other, block(OWN, p.x), 1, p.mid)
    mid_own = send(4, own, held[1], 4, p.mid)
    mid_far = send(5, held[0], block(MATE, p.x), 2, p.mid)
    mid_far_own = send(6, block(MATE, p.x), held[2], 5, p.mid)
    back_near = send(1, held[1], block(NEAR, p.x), 1, p.mate)
    back_far = send(2, held[2], block(FAR, p.x), 2, p.mate)

    def begin():
        @pl.when(p.inner)
        def _():
            mid_other.start()
            mid_own.start()

        to_mate.start()

        @pl.when(p.outer)
        def _():
            outer_own.start()

        across[OWN].start()
        local.start()

    def mate_here():
        arrived(0, block(MATE, p.x))

        @pl.when(p.inner)
        def _():
            arrived(3, held[0])
            mid_far.start()
            mid_far_own.start()
            arrived(4, held[1])
            back_near.start()

        across[MATE].start()

    def near_here():
        arrived(1, block(NEAR, p.x))
        across[NEAR].start()

        @pl.when(p.inner)
        def _():
            arrived(5, held[2])
            back_far.start()

    def far_here():
        arrived(2, block(FAR, p.x))
        across[FAR].start()

    def finish():
        for k in range(4):
            arrived(6 + k, block(k, 1 - p.x))
            across[k].wait_send()
        local.wait()
        to_mate.wait_send()

        @pl.when(p.inner)
        def _():
            for copy in (mid_other, mid_own, mid_far, mid_far_own, back_near, back_far):
                copy.wait_send()

        @pl.when(p.outer)
        def _():
            outer_own.wait_send()

    return [begin, mate_here, near_here, far_here, finish]


def gather_pair(weights, collective, split=4):
    n = len(weights)
    rows, width = weights[0].shape
    half = width // 2
    count = rows // split

    def kernel(*refs):
        ins, outs = refs[:n], refs[n : 2 * n]
        relay, ss, rs = refs[2 * n :]
        p = Place()
        p.enter()
        in_stages(
            [
                pair_gather_chunk(
                    p, ins[i], outs[i], relay.at[i], ss.at[i * split + c], rs.at[i * split + c],
                    c * count, count, rows,
                )
                for i in range(n)
                for c in range(split)
            ]
        )

    return pl.pallas_call(
        kernel,
        out_shape=[jax.ShapeDtypeStruct((8 * rows, half), BF)] * n,
        in_specs=[ANY] * n,
        out_specs=[ANY] * n,
        scratch_shapes=[
            pltpu.VMEM((n, 3, rows, half), BF),
            pltpu.SemaphoreType.DMA((n * split, 12)),
            pltpu.SemaphoreType.DMA((n * split, 10)),
        ],
        compiler_params=pltpu.CompilerParams(
            collective_id=collective, has_side_effects=True, vmem_limit_bytes=32 << 20
        ),
        cost_estimate=pl.CostEstimate(flops=0, bytes_accessed=n * (100 << 20), transcendentals=0),
        name="gather_pair",
    )(*weights)


def line_gather_chunk(p, weight, out, ss, rs, first, count, rows):
    own = weight.at[pl.ds(first, count), :]

    def block(which, x):
        return out.at[pl.ds(pl.multiple_of(p.block(which, x) * rows + first, count), count), :]

    def send(slot, src, dst, recv, device):
        return remote(src, dst, ss.at[slot], rs.at[recv], device)

    def arrived(recv, dst):
        remote(dst, dst, ss.at[0], rs.at[recv], p.mate).wait_recv()

    local = pltpu.make_async_copy(own, block(OWN, p.x), ss.at[9])
    across = [
        send(k, own if k == OWN else block(k, p.x), block(k, p.x), 3 + k, p.across)
        for k in range(4)
    ]
    to_mate = send(4, own, block(OWN, p.x), MATE - 1, p.mate)
    to_mid = send(5, own, block(OWN, p.x), NEAR - 1, p.mid)
    mid_far = send(6, block(MATE, p.x), block(MATE, p.x), FAR - 1, p.mid)
    back_near = send(7, block(NEAR, p.x), block(NEAR, p.x), NEAR - 1, p.mate)
    back_far = send(8, block(FAR, p.x), block(FAR, p.x), FAR - 1, p.mate)

    def begin():
        @pl.when(p.inner)
        def _():
            to_mid.start()

        to_mate.start()
        across[OWN].start()
        local.start()

    def mate_here():
        arrived(MATE - 1, block(MATE, p.x))

        @pl.when(p.inner)
        def _():
            mid_far.start()

        across[MATE].start()

    def near_here():
        arrived(NEAR - 1, block(NEAR, p.x))

        @pl.when(p.inner)
        def _():
            back_near.start()

        across[NEAR].start()

    def far_here():
        arrived(FAR - 1, block(FAR, p.x))

        @pl.when(p.inner)
        def _():
            back_far.start()

        across[FAR].start()

    def finish():
        for k in range(4):
            arrived(3 + k, block(k, 1 - p.x))
            across[k].wait_send()
        local.wait()
        to_mate.wait_send()

        @pl.when(p.inner)
        def _():
            for copy in (to_mid, mid_far, back_near, back_far):
                copy.wait_send()

    return [begin, mate_here, near_here, far_here, finish]


def gather_line(weights, collective, split=2):
    n = len(weights)
    rows = weights[0].shape[0]
    count = rows // split

    def kernel(*refs):
        ins, outs = refs[:n], refs[n : 2 * n]
        ss, rs = refs[2 * n :]
        p = Place()
        p.enter()
        in_stages(
            [
                line_gather_chunk(
                    p, ins[i], outs[i], ss.at[i * split + c], rs.at[i * split + c],
                    c * count, count, rows,
                )
                for i in range(n)
                for c in range(split)
            ]
        )

    return pl.pallas_call(
        kernel,
        out_shape=[jax.ShapeDtypeStruct((8 * rows, w.shape[1]), BF) for w in weights],
        in_specs=[ANY] * n,
        out_specs=[ANY] * n,
        scratch_shapes=[
            pltpu.SemaphoreType.DMA((n * split, 10)),
            pltpu.SemaphoreType.DMA((n * split, 7)),
        ],
        compiler_params=pltpu.CompilerParams(
            collective_id=collective, has_side_effects=True, vmem_limit_bytes=32 << 20
        ),
        cost_estimate=pl.CostEstimate(flops=0, bytes_accessed=n * (100 << 20), transcendentals=0),
        name="gather_line",
    )(*weights)


def contract_tokens(left, right):
    return lax.dot_general(left, right, (((0,), (0,)), ((), ())), preferred_element_type=F32)


def scatter_pair(lefts, rights, which, collective):
    n, nx = len(rights), len(lefts)
    half = rights[0].shape[1]
    rows = lefts[0].shape[1] // 8

    def kernel(*refs):
        left, right, out = refs[:nx], refs[nx : nx + n], refs[nx + n : nx + 2 * n]
        sx, rx, sz, rz, rm, own, ss, rs = refs[nx + 2 * n :]
        p = Place()
        p.enter()

        def product(i, k, x):
            cols = pl.ds(pl.multiple_of(p.block(k, x) * rows, rows), rows)
            return contract_tokens(left[which[i]][:, cols], right[i][...])

        def across(i, k):
            return remote(sx.at[i, k], rx.at[i, k], ss.at[i, k], rs.at[i, k], p.across)

        def outward(i, j):
            return remote(sz.at[i, j], rz.at[i, j], ss.at[i, 4 + j], rs.at[i, 4 + j], p.mate)

        def middle(i, j):
            return remote(sz.at[i, j], rm.at[i, j], ss.at[i, 7 + j], rs.at[i, 7 + j], p.mid)

        def relay(i, j):
            return remote(rz.at[i, j], rm.at[i, 2 + j], ss.at[i, 9 + j], rs.at[i, 9 + j], p.mid)

        def forward(i):
            return remote(rm.at[i, 0], rz.at[i, 0], ss.at[i, 4], rs.at[i, 4], p.mate)

        def back(i):
            return remote(sz.at[i, 2], rz.at[i, 1], ss.at[i, 5], rs.at[i, 5], p.mate)

        def cols_of(place):
            return pl.ds(pl.multiple_of(place * half, half), half)

        def send_across(i):
            for k in (FAR, NEAR, MATE, OWN):
                sx[i, k] = product(i, k, 1 - p.x).astype(BF)
                across(i, k).start()

        def send_on(i, k, j):
            total = product(i, k, p.x)
            across(i, k).wait_recv()
            sz[i, j] = (total + rx[i, k].astype(F32)).astype(BF)

            @pl.when(p.outer)
            def _():
                outward(i, j).start()

            @pl.when(p.inner)
            def _():
                middle(i, j).start()

        def send_relay(i, j):
            @pl.when(p.inner)
            def _():
                outward(i, j).wait_recv()
                relay(i, j).start()

        def mate_rows(i):
            total = product(i, MATE, p.x)
            across(i, MATE).wait_recv()
            total = total + rx[i, MATE].astype(F32)

            @pl.when(p.outer)
            def _():
                sz[i, 2] = total.astype(BF)
                outward(i, 2).start()

            @pl.when(p.inner)
            def _():
                own[i, 0] = total

        def send_forward(i):
            @pl.when(p.inner)
            def _():
                middle(i, 0).wait_recv()
                forward(i).start()

        def own_rows(i):
            total = product(i, OWN, p.x)
            across(i, OWN).wait_recv()
            own[i, 1] = total + rx[i, OWN].astype(F32)

        def finish(i):
            @pl.when(p.inner)
            def _():
                relay(i, 0).wait_recv()
                sz[i, 2] = (own[i, 0] + rm[i, 2].astype(F32)).astype(BF)
                back(i).start()
                relay(i, 1).wait_recv()
                out[i][:, cols_of(p.zl)] = own[i, 1] + rm[i, 3].astype(F32)
                outward(i, 2).wait_recv()
                middle(i, 1).wait_recv()
                out[i][:, cols_of(1 - p.zl)] = rz[i, 2].astype(F32) + rm[i, 1].astype(F32)

            @pl.when(p.outer)
            def _():
                forward(i).wait_recv()
                out[i][:, cols_of(p.zl)] = own[i, 1] + rz[i, 0].astype(F32)
                back(i).wait_recv()
                out[i][:, cols_of(1 - p.zl)] = rz[i, 1].astype(F32)
                for j in range(3):
                    outward(i, j).wait_send()

            for k in range(4):
                across(i, k).wait_send()

            @pl.when(p.inner)
            def _():
                for j in range(2):
                    middle(i, j).wait_send()
                    relay(i, j).wait_send()
                forward(i).wait_send()
                back(i).wait_send()

        send_across(0)
        for i in range(n):
            if i + 1 < n:
                send_across(i + 1)
            send_on(i, FAR, 0)
            send_on(i, NEAR, 1)
            send_relay(i, 0)
            mate_rows(i)
            send_relay(i, 1)
            send_forward(i)
            own_rows(i)
            if i > 0:
                finish(i - 1)
        finish(n - 1)

    return pl.pallas_call(
        kernel,
        out_shape=[jax.ShapeDtypeStruct((rows, 2 * half), F32)] * n,
        in_specs=[VMEM] * (nx + n),
        out_specs=[VMEM] * n,
        scratch_shapes=[
            pltpu.VMEM((n, 4, rows, half), BF),
            pltpu.VMEM((n, 4, rows, half), BF),
            pltpu.VMEM((n, 3, rows, half), BF),
            pltpu.VMEM((n, 3, rows, half), BF),
            pltpu.VMEM((n, 4, rows, half), BF),
            pltpu.VMEM((n, 2, rows, half), F32),
            pltpu.SemaphoreType.DMA((n, 11)),
            pltpu.SemaphoreType.DMA((n, 11)),
        ],
        compiler_params=pltpu.CompilerParams(
            collective_id=collective, has_side_effects=True, vmem_limit_bytes=60 << 20
        ),
        cost_estimate=pl.CostEstimate(flops=0, bytes_accessed=n * (150 << 20), transcendentals=0),
        name="scatter_pair",
    )(*lefts, *rights)


def scatter_line(lefts, rights, which, collective):
    n, nx, ny = len(which), len(lefts), len(rights)
    rows = lefts[0].shape[1] // 8
    width = min(r.shape[1] for r in rights)

    def kernel(*refs):
        left, right, out = refs[:nx], refs[nx : nx + ny], refs[nx + ny : nx + 2 * ny]
        sx, rx, sz, rz, rm, own, ss, rs = refs[nx + 2 * ny :]
        p = Place()
        p.enter()

        def product(i, k, x):
            a, b, group = which[i]
            cols = pl.ds(pl.multiple_of(p.block(k, x) * rows, rows), rows)
            return contract_tokens(
                left[a][:, cols], right[b][:, group * width : (group + 1) * width]
            )

        def across(i, k):
            return remote(sx.at[i, k], rx.at[i, k], ss.at[i, k], rs.at[i, k], p.across)

        def outward(i, j):
            return remote(sz.at[i, j], rz.at[i, j], ss.at[i, 4 + j], rs.at[i, 4 + j], p.mate)

        def middle(i, j):
            return remote(sz.at[i, j], rm.at[i, j], ss.at[i, 7 + j], rs.at[i, 7 + j], p.mid)

        def back(i):
            return remote(sz.at[i, 2], rz.at[i, 0], ss.at[i, 4], rs.at[i, 4], p.mate)

        def send_across(i):
            for k in (FAR, NEAR, MATE, OWN):
                sx[i, k] = product(i, k, 1 - p.x).astype(BF)
                across(i, k).start()

        def summed(i, k):
            total = product(i, k, p.x)
            across(i, k).wait_recv()
            return total + rx[i, k].astype(F32)

        def send_on(i, k, j):
            total = summed(i, k)

            @pl.when(p.outer)
            def _():
                sz[i, j] = total.astype(BF)
                outward(i, j).start()

            @pl.when(p.inner)
            def _():
                outward(i, j).wait_recv()
                sz[i, j] = (total + rz[i, j].astype(F32)).astype(BF)
                middle(i, j).start()

        def mate_rows(i):
            total = summed(i, MATE)

            @pl.when(p.outer)
            def _():
                sz[i, 2] = total.astype(BF)
                outward(i, 2).start()

            @pl.when(p.inner)
            def _():
                own[i, 0] = total

        def own_rows(i):
            own[i, 1] = summed(i, OWN)

        def finish(i):
            b, group = which[i][1:]
            here = pl.ds(group * width, width)

            @pl.when(p.inner)
            def _():
                middle(i, 0).wait_recv()
                sz[i, 2] = (own[i, 0] + rm[i, 0].astype(F32)).astype(BF)
                back(i).start()
                outward(i, 2).wait_recv()
                middle(i, 1).wait_recv()
                out[b][:, here] = own[i, 1] + rz[i, 2].astype(F32) + rm[i, 1].astype(F32)

            @pl.when(p.outer)
            def _():
                back(i).wait_recv()
                out[b][:, here] = own[i, 1] + rz[i, 0].astype(F32)
                for j in range(3):
                    outward(i, j).wait_send()

            for k in range(4):
                across(i, k).wait_send()

            @pl.when(p.inner)
            def _():
                for j in range(2):
                    middle(i, j).wait_send()
                back(i).wait_send()

        send_across(0)
        for i in range(n):
            if i + 1 < n:
                send_across(i + 1)
            send_on(i, FAR, 0)
            send_on(i, NEAR, 1)
            mate_rows(i)
            own_rows(i)
            if i > 0:
                finish(i - 1)
        finish(n - 1)

    return pl.pallas_call(
        kernel,
        out_shape=[jax.ShapeDtypeStruct((rows, r.shape[1]), F32) for r in rights],
        in_specs=[VMEM] * (nx + ny),
        out_specs=[VMEM] * ny,
        scratch_shapes=[
            pltpu.VMEM((n, 4, rows, width), BF),
            pltpu.VMEM((n, 4, rows, width), BF),
            pltpu.VMEM((n, 3, rows, width), BF),
            pltpu.VMEM((n, 3, rows, width), BF),
            pltpu.VMEM((n, 2, rows, width), BF),
            pltpu.VMEM((n, 2, rows, width), F32),
            pltpu.SemaphoreType.DMA((n, 9)),
            pltpu.SemaphoreType.DMA((n, 9)),
        ],
        compiler_params=pltpu.CompilerParams(
            collective_id=collective, has_side_effects=True, vmem_limit_bytes=60 << 20
        ),
        cost_estimate=pl.CostEstimate(flops=0, bytes_accessed=n * (80 << 20), transcendentals=0),
        name="scatter_line",
    )(*lefts, *rights)


SEQ = ("zh", "zl", "x")
TP = ("y", "c")
PAIR = ("zl", "y", "c")


def after(value, *others):
    return lax.optimization_barrier((value, *others))[0]


def gather_pair_rows(rows):
    tokens, local = rows.shape
    pair, parts = lax.axis_size("zl"), lax.axis_size(TP)
    blocks = lax.all_gather(rows, PAIR, axis=0).reshape(pair, parts, tokens, local)
    return blocks.transpose(0, 2, 1, 3).reshape(pair * tokens, parts * local)


def reduce_pair_rows(partial_rows):
    pair, parts = lax.axis_size("zl"), lax.axis_size(TP)
    tokens, local = partial_rows.shape[0] // pair, partial_rows.shape[1] // parts
    blocks = partial_rows.astype(BF).reshape(pair, tokens, parts, local).transpose(0, 2, 1, 3)
    return lax.psum_scatter(
        blocks.reshape(pair * parts * tokens, local), PAIR, scatter_dimension=0, tiled=True
    ).astype(F32)


def reduce_features(partial_rows):
    return lax.psum_scatter(
        partial_rows.astype(BF), TP, scatter_dimension=1, tiled=True
    ).astype(F32)


def rms_scale(values, gain):
    width = gain.shape[0] * lax.axis_size(TP)
    squares = lax.psum(jnp.sum(values * values, axis=1, keepdims=True), TP)
    inverse = lax.rsqrt(squares / width + epsilon)
    return (values * inverse * gain).astype(BF), inverse, jnp.sqrt(squares[:, 0] / width + epsilon)


def scale_backward(values, gain, inverse, grad_rows):
    width = gain.shape[0] * lax.axis_size(TP)
    gained = gain * grad_rows
    total = lax.psum(jnp.sum(values * gained, axis=1, keepdims=True), TP)
    grad_values = inverse * gained - values * inverse**3 * (total / width)
    return grad_values, jnp.sum(grad_rows * values * inverse, axis=0)


def dot(left, right):
    return jnp.dot(left, right, preferred_element_type=F32)


def paired_on_device(
    stream,
    norm1_gain,
    in_weight,
    conv_weight,
    out_weight,
    norm2_gain,
    gate_weight,
    up_weight,
    down_weight,
    doc_starts,
    out_grad,
):
    tokens, local = stream.shape
    rows_here = in_weight.shape[0]
    positions = lax.axis_index(SEQ) * tokens + jnp.arange(tokens, dtype=jnp.int32)
    mask_one, mask_two = lag_masks(doc_starts, positions)
    normed_here, inverse_in, rms_in = rms_scale(stream, norm1_gain)
    normed_in = lax.all_gather(normed_here, TP, axis=1, tiled=True)
    in_matrix, whole_out = gather_line(
        [after(in_weight.reshape(rows_here, 3 * local), normed_here), out_weight], 0
    )
    out_full = gather_pair_rows(after(out_grad.astype(BF), normed_in))
    projected = dot(normed_in, in_matrix)
    in_gate = projected[:, :local]
    out_gate = projected[:, local : 2 * local]
    carried = projected[:, 2 * local :]
    mixed = in_gate * carried
    previous = from_behind(mixed[-2:], SEQ, 1)
    extended = jnp.concatenate([previous, mixed], axis=0)
    convolved = (
        conv_weight[0] * mixed
        + mask_one * conv_weight[1] * extended[1:-1]
        + mask_two * conv_weight[2] * extended[:-2]
    )
    gated = (out_gate * convolved).astype(BF)
    mixer_partial = contract_cols(gated, whole_out).astype(BF)
    mixer_out = reduce_features(mixer_partial)
    (whole_gate,) = gather_pair([after(gate_weight, mixer_partial)], 1)
    mixer_out = after(mixer_out, whole_gate)
    middle = stream + mixer_out
    normed_mid_here, inverse_mid, rms_mid = rms_scale(middle, norm2_gain)
    normed_mid = gather_pair_rows(normed_mid_here)
    (whole_up,) = gather_pair([after(up_weight, normed_mid_here)], 2)
    normed_mid = after(normed_mid, whole_up)
    gate = dot(normed_mid, whole_gate)
    upward = dot(normed_mid, whole_up)
    (whole_down,) = gather_pair([after(down_weight, whole_up)], 3)
    sigmoid_gate = jax.nn.sigmoid(gate)
    hidden = (gate * sigmoid_gate * upward).astype(BF)
    hidden_grad = dot(out_full, whole_down)
    gate_rows = (
        hidden_grad * upward * sigmoid_gate * (1.0 + gate * (1.0 - sigmoid_gate))
    ).astype(BF)
    up_rows = (hidden_grad * gate * sigmoid_gate).astype(BF)
    mid_partial = (contract_cols(gate_rows, whole_gate) + contract_cols(up_rows, whole_up)).astype(BF)
    normed_mid_grad = reduce_pair_rows(mid_partial)
    (down_weight_grad,) = scatter_pair([out_full], [after(hidden, mid_partial)], [0], 4)
    normed_mid_grad = after(normed_mid_grad, down_weight_grad)
    middle_norm_grad, gain_mid_grad = scale_backward(
        middle, norm2_gain, inverse_mid, normed_mid_grad
    )
    middle_grad = out_grad + middle_norm_grad
    branch_here = middle_grad.astype(BF)
    branch_full = lax.all_gather(branch_here, TP, axis=1, tiled=True)
    ffn_partial = contract_cols(hidden, whole_down)
    result = middle + reduce_pair_rows(after(ffn_partial, branch_here))
    gate_weight_grad, up_weight_grad = scatter_pair(
        [normed_mid], [after(gate_rows, branch_here), up_rows], [0, 0], 5
    )
    branch_full = after(branch_full, gate_weight_grad)
    gated_grad = dot(branch_full, whole_out)
    out_gate_grad = gated_grad * convolved
    conv_grad = gated_grad * out_gate
    lag_one = mask_one * conv_grad
    lag_two = mask_two * conv_grad
    next_one, next_two = from_behind((lag_one[:2], lag_two[:2]), SEQ, -1)
    after_one = jnp.concatenate([lag_one, next_one], axis=0)
    after_two = jnp.concatenate([lag_two, next_two], axis=0)
    mixed_grad = (
        conv_weight[0] * conv_grad
        + conv_weight[1] * after_one[1 : tokens + 1]
        + conv_weight[2] * after_two[2:]
    )
    tap_grads = jnp.stack(
        [
            jnp.sum(conv_grad * mixed, axis=0),
            jnp.sum(lag_one * extended[1:-1], axis=0),
            jnp.sum(lag_two * extended[:-2], axis=0),
        ]
    )
    projected_grad = jnp.concatenate(
        [mixed_grad * carried, out_gate_grad, mixed_grad * in_gate], axis=1
    ).astype(BF)
    in_partial = contract_cols(projected_grad, in_matrix).astype(BF)
    normed_in_grad = reduce_features(in_partial)
    out_weight_grad, in_weight_grad = scatter_line(
        [normed_in, branch_full],
        [after(gated, in_partial), projected_grad],
        [(1, 0, 0), (0, 1, 0), (0, 1, 1), (0, 1, 2)],
        6,
    )
    normed_in_grad = after(normed_in_grad, in_weight_grad)
    stream_norm_grad, gain_in_grad = scale_backward(stream, norm1_gain, inverse_in, normed_in_grad)
    stream_grad = middle_grad + stream_norm_grad
    conv_total, gain_in_total, gain_mid_total = lax.psum(
        (tap_grads, gain_in_grad, gain_mid_grad), SEQ
    )
    return (
        result,
        stream_grad,
        gain_in_total,
        in_weight_grad.reshape(rows_here, 3, local),
        conv_total,
        out_weight_grad,
        gain_mid_total,
        gate_weight_grad,
        up_weight_grad,
        down_weight_grad,
        jnp.stack([rms_in, rms_mid]),
    )


def solution(mesh):
    seq, tp = mesh.shape["seq"], mesh.shape["tp"]
    if (seq, tp) == (8, 4):
        shape, names = (2, 2, 2, 2, 2), ("zh", "zl", "x", "y", "c")
        mesh = Mesh(mesh.devices.reshape(shape), names)
        body, rows, cols = paired_on_device, SEQ, TP
    else:
        body, rows, cols = on_device, "seq", "tp"
    return jax.shard_map(
        body,
        mesh=mesh,
        in_specs=(
            P(rows, cols),
            P(cols),
            P(rows, None, cols),
            P(None, cols),
            P(rows, cols),
            P(cols),
            P(rows, cols),
            P(rows, cols),
            P(rows, cols),
            P(),
            P(rows, cols),
        ),
        out_specs=(
            P(rows, cols),
            P(rows, cols),
            P(cols),
            P(rows, None, cols),
            P(None, cols),
            P(rows, cols),
            P(cols),
            P(rows, cols),
            P(rows, cols),
            P(rows, cols),
            P(None, rows),
        ),
        check_vma=False,
    )
```

```python
import jax
import jax.numpy as jnp
from jax import lax
from jax.experimental import pallas as pl
from jax.experimental.pallas import tpu as pltpu
from jax.sharding import Mesh, PartitionSpec as P

epsilon = 1e-05


def from_behind(shard, axis, by):
    count = lax.axis_size(axis)
    pairs = [(i, i + by) for i in range(count) if 0 <= i + by < count]
    return lax.ppermute(shard, axis, pairs)


def doc_count(doc_starts, positions):
    return jnp.sum((doc_starts[None, :] <= positions[:, None]).astype(jnp.int32), axis=1)


def lag_masks(doc_starts, positions):
    current = doc_count(doc_starts, positions)
    one = (positions >= 1) & (doc_count(doc_starts, positions - 1) == current)
    two = (positions >= 2) & (doc_count(doc_starts, positions - 2) == current)
    return (one.astype(jnp.float32)[:, None], two.astype(jnp.float32)[:, None])


def contract_rows(left, right):
    return lax.dot_general(
        left, right, (((0,), (0,)), ((), ())), preferred_element_type=jnp.float32
    )


def contract_cols(left, right):
    return lax.dot_general(
        left, right, (((1,), (1,)), ((), ())), preferred_element_type=jnp.float32
    )


def reduce_tp(partial_rows):
    return lax.psum_scatter(
        partial_rows.astype(jnp.bfloat16), "tp", scatter_dimension=1, tiled=True
    ).astype(jnp.float32)


def reduce_seq(partial_grad):
    return lax.psum_scatter(
        partial_grad.astype(jnp.bfloat16), "seq", scatter_dimension=0, tiled=True
    ).astype(jnp.float32)


def gather_grads(grad_rows):
    return lax.all_gather(grad_rows, "tp", axis=1, tiled=True)


def normalize(values, gain):
    width = gain.shape[0] * lax.axis_size("tp")
    squares = lax.psum(jnp.sum(values * values, axis=1, keepdims=True), "tp")
    inverse = lax.rsqrt(squares / width + epsilon)
    normed = lax.all_gather(
        (values * inverse * gain).astype(jnp.bfloat16), "tp", axis=1, tiled=True
    )
    return (normed, inverse, jnp.sqrt(squares[:, 0] / width + epsilon))


def norm_backward(values, gain, inverse, grad_rows):
    width = gain.shape[0] * lax.axis_size("tp")
    gained = gain * grad_rows
    total = lax.psum(jnp.sum(values * gained, axis=1, keepdims=True), "tp")
    grad_values = inverse * gained - values * inverse**3 * (total / width)
    grad_gain = jnp.sum(grad_rows * values * inverse, axis=0)
    return (grad_values, grad_gain)


def on_device(
    stream,
    norm1_gain,
    in_weight,
    conv_weight,
    out_weight,
    norm2_gain,
    gate_weight,
    up_weight,
    down_weight,
    doc_starts,
    out_grad,
):
    tokens = stream.shape[0]
    local = stream.shape[1]
    rows_here = in_weight.shape[0]
    whole_in, whole_out, whole_gate, whole_up, whole_down = (
        lax.all_gather(in_weight, "seq", axis=0, tiled=True),
        lax.all_gather(out_weight, "seq", axis=0, tiled=True),
        lax.all_gather(gate_weight, "seq", axis=0, tiled=True),
        lax.all_gather(up_weight, "seq", axis=0, tiled=True),
        lax.all_gather(down_weight, "seq", axis=0, tiled=True),
    )
    width = whole_out.shape[0]
    in_matrix = whole_in.reshape(width, 3 * local)
    positions = lax.axis_index("seq") * tokens + jnp.arange(tokens, dtype=jnp.int32)
    mask_one, mask_two = lag_masks(doc_starts, positions)
    normed_in, inverse_in, rms_in = normalize(stream, norm1_gain)
    projected = jnp.dot(normed_in, in_matrix, preferred_element_type=jnp.float32)
    in_gate = projected[:, :local]
    out_gate = projected[:, local : 2 * local]
    carried = projected[:, 2 * local :]
    mixed = in_gate * carried
    previous = from_behind(mixed[-2:], "seq", 1)
    extended = jnp.concatenate([previous, mixed], axis=0)
    convolved = (
        conv_weight[0] * mixed
        + mask_one * conv_weight[1] * extended[1:-1]
        + mask_two * conv_weight[2] * extended[:-2]
    )
    gated = (out_gate * convolved).astype(jnp.bfloat16)
    middle = stream + reduce_tp(contract_cols(gated, whole_out))
    normed_mid, inverse_mid, rms_mid = normalize(middle, norm2_gain)
    gate = jnp.dot(normed_mid, whole_gate, preferred_element_type=jnp.float32)
    upward = jnp.dot(normed_mid, whole_up, preferred_element_type=jnp.float32)
    hidden = (jax.nn.silu(gate) * upward).astype(jnp.bfloat16)
    result = middle + reduce_tp(contract_cols(hidden, whole_down))
    out_full = gather_grads(out_grad.astype(jnp.bfloat16))
    hidden_grad = jnp.dot(out_full, whole_down, preferred_element_type=jnp.float32)
    sigmoid_gate = jax.nn.sigmoid(gate)
    gate_rows = (hidden_grad * upward * sigmoid_gate * (1.0 + gate * (1.0 - sigmoid_gate))).astype(
        jnp.bfloat16
    )
    up_rows = (hidden_grad * gate * sigmoid_gate).astype(jnp.bfloat16)
    normed_mid_grad = reduce_tp(
        contract_cols(gate_rows, whole_gate) + contract_cols(up_rows, whole_up)
    )
    middle_norm_grad, gain_mid_grad = norm_backward(
        middle, norm2_gain, inverse_mid, normed_mid_grad
    )
    middle_grad = out_grad + middle_norm_grad
    branch_full = gather_grads(middle_grad.astype(jnp.bfloat16))
    gated_grad = jnp.dot(branch_full, whole_out, preferred_element_type=jnp.float32)
    out_gate_grad = gated_grad * convolved
    conv_grad = gated_grad * out_gate
    lag_one = mask_one * conv_grad
    lag_two = mask_two * conv_grad
    next_one, next_two = from_behind((lag_one[:2], lag_two[:2]), "seq", -1)
    after_one = jnp.concatenate([lag_one, next_one], axis=0)
    after_two = jnp.concatenate([lag_two, next_two], axis=0)
    mixed_grad = (
        conv_weight[0] * conv_grad
        + conv_weight[1] * after_one[1 : tokens + 1]
        + conv_weight[2] * after_two[2:]
    )
    tap_grads = jnp.stack(
        [
            jnp.sum(conv_grad * mixed, axis=0),
            jnp.sum(lag_one * extended[1:-1], axis=0),
            jnp.sum(lag_two * extended[:-2], axis=0),
        ]
    )
    projected_grad = jnp.concatenate(
        [mixed_grad * carried, out_gate_grad, mixed_grad * in_gate], axis=1
    ).astype(jnp.bfloat16)
    normed_in_grad = reduce_tp(contract_cols(projected_grad, in_matrix))
    stream_norm_grad, gain_in_grad = norm_backward(stream, norm1_gain, inverse_in, normed_in_grad)
    stream_grad = middle_grad + stream_norm_grad
    conv_total, gain_in_total, gain_mid_total = lax.psum(
        (tap_grads, gain_in_grad, gain_mid_grad), "seq"
    )
    down_weight_grad = reduce_seq(contract_rows(out_full, hidden))
    gate_weight_grad = reduce_seq(contract_rows(normed_mid, gate_rows))
    up_weight_grad = reduce_seq(contract_rows(normed_mid, up_rows))
    out_weight_grad = reduce_seq(contract_rows(branch_full, gated))
    in_weight_grad = reduce_seq(contract_rows(normed_in, projected_grad)).reshape(
        rows_here, 3, local
    )
    rms_values = jnp.stack([rms_in, rms_mid])
    return (
        result,
        stream_grad,
        gain_in_total,
        in_weight_grad,
        conv_total,
        out_weight_grad,
        gain_mid_total,
        gate_weight_grad,
        up_weight_grad,
        down_weight_grad,
        rms_values,
    )


MESH = pl.DeviceIdType.MESH
BF = jnp.bfloat16
F32 = jnp.float32
ANY = pl.BlockSpec(memory_space=pl.ANY)
VMEM = pl.BlockSpec(memory_space=pltpu.VMEM)
OWN, MATE, NEAR, FAR = 0, 1, 2, 3


def dot(left, right):
    return jnp.dot(left, right, preferred_element_type=F32)


def remote(src, dst, send_sem, recv_sem, device):
    return pltpu.make_async_remote_copy(
        src_ref=src,
        dst_ref=dst,
        send_sem=send_sem,
        recv_sem=recv_sem,
        device_id=device,
        device_id_type=MESH,
    )


class Place:
    def __init__(self):
        self.zh, self.zl = lax.axis_index("zh"), lax.axis_index("zl")
        self.x, self.y, self.c = lax.axis_index("x"), lax.axis_index("y"), lax.axis_index("c")
        self.z = 2 * self.zh + self.zl
        self.inner = (self.z == 1) | (self.z == 2)
        self.outer = (self.z == 0) | (self.z == 3)
        self.rows = [self.z, 2 * self.zh + 1 - self.zl, 2 - self.zh, 3 - 3 * self.zh]
        self.mate = (self.zh, 1 - self.zl, self.x, self.y, self.c)
        self.mid = (1 - self.zh, 1 - self.zl, self.x, self.y, self.c)
        self.across = (self.zh, self.zl, 1 - self.x, self.y, self.c)

    def block(self, which, x):
        return self.rows[which] * 2 + x

    def enter(self, *others):
        barrier = pltpu.get_barrier_semaphore()

        def greet(device):
            pl.semaphore_signal(barrier, inc=1, device_id=device, device_id_type=MESH)

        greet(self.mate)
        greet(self.across)
        for device in others:
            greet(device)

        @pl.when(self.inner)
        def _():
            greet(self.mid)

        @pl.when(self.inner)
        def _():
            pl.semaphore_wait(barrier, 3 + len(others))

        @pl.when(self.outer)
        def _():
            pl.semaphore_wait(barrier, 2 + len(others))


def in_stages(chunks):
    stages = len(chunks[0])
    for step in range(len(chunks) + stages - 1):
        for stage in range(stages):
            if 0 <= step - stage < len(chunks):
                chunks[step - stage][stage]()


def pair_gather_chunk(p, weight, out, relay, ss, rs, first, count, rows):
    half = out.shape[1]
    here = pl.ds(first, count)
    own = weight.at[here, pl.ds(pl.multiple_of(p.zl * half, half), half)]
    other = weight.at[here, pl.ds(pl.multiple_of((1 - p.zl) * half, half), half)]

    def block(which, x):
        return out.at[pl.ds(pl.multiple_of(p.block(which, x) * rows + first, count), count), :]

    held = [relay.at[i, here, :] for i in range(3)]

    def send(slot, src, dst, recv, device):
        return remote(src, dst, ss.at[slot], rs.at[recv], device)

    def arrived(recv, dst):
        remote(dst, dst, ss.at[0], rs.at[recv], p.mate).wait_recv()

    local = pltpu.make_async_copy(own, block(OWN, p.x), ss.at[11])
    across = [
        send(7 + k, own if k == OWN else block(k, p.x), block(k, p.x), 6 + k, p.across)
        for k in range(4)
    ]
    to_mate = send(0, other, block(OWN, p.x), 0, p.mate)
    outer_own = send(1, own, held[0], 3, p.mate)
    mid_other = send(3, other, block(OWN, p.x), 1, p.mid)
    mid_own = send(4, own, held[1], 4, p.mid)
    mid_far = send(5, held[0], block(MATE, p.x), 2, p.mid)
    mid_far_own = send(6, block(MATE, p.x), held[2], 5, p.mid)
    back_near = send(1, held[1], block(NEAR, p.x), 1, p.mate)
    back_far = send(2, held[2], block(FAR, p.x), 2, p.mate)

    def begin():
        @pl.when(p.inner)
        def _():
            mid_other.start()
            mid_own.start()

        to_mate.start()

        @pl.when(p.outer)
        def _():
            outer_own.start()

        across[OWN].start()
        local.start()

    def mate_here():
        arrived(0, block(MATE, p.x))

        @pl.when(p.inner)
        def _():
            arrived(3, held[0])
            mid_far.start()
            mid_far_own.start()
            arrived(4, held[1])
            back_near.start()

        across[MATE].start()

    def near_here():
        arrived(1, block(NEAR, p.x))
        across[NEAR].start()

        @pl.when(p.inner)
        def _():
            arrived(5, held[2])
            back_far.start()

    def far_here():
        arrived(2, block(FAR, p.x))
        across[FAR].start()

    def finish():
        for k in range(4):
            arrived(6 + k, block(k, 1 - p.x))
            across[k].wait_send()
        local.wait()
        to_mate.wait_send()

        @pl.when(p.inner)
        def _():
            for copy in (mid_other, mid_own, mid_far, mid_far_own, back_near, back_far):
                copy.wait_send()

        @pl.when(p.outer)
        def _():
            outer_own.wait_send()

    return [begin, mate_here, near_here, far_here, finish]


def gather_pair(weights, collective, split=4):
    n = len(weights)
    rows, width = weights[0].shape
    half = width // 2
    count = rows // split

    def kernel(*refs):
        ins, outs = refs[:n], refs[n : 2 * n]
        relay, ss, rs = refs[2 * n :]
        p = Place()
        p.enter()
        in_stages(
            [
                pair_gather_chunk(
                    p, ins[i], outs[i], relay.at[i], ss.at[i * split + c], rs.at[i * split + c],
                    c * count, count, rows,
                )
                for i in range(n)
                for c in range(split)
            ]
        )

    return pl.pallas_call(
        kernel,
        out_shape=[jax.ShapeDtypeStruct((8 * rows, half), BF)] * n,
        in_specs=[ANY] * n,
        out_specs=[ANY] * n,
        scratch_shapes=[
            pltpu.VMEM((n, 3, rows, half), BF),
            pltpu.SemaphoreType.DMA((n * split, 12)),
            pltpu.SemaphoreType.DMA((n * split, 10)),
        ],
        compiler_params=pltpu.CompilerParams(
            collective_id=collective, has_side_effects=True, vmem_limit_bytes=32 << 20
        ),
        cost_estimate=pl.CostEstimate(flops=0, bytes_accessed=n * (100 << 20), transcendentals=0),
        name="gather_pair",
    )(*weights)


def gather_down_and_hidden(weight, normed, gate, up, collective, split=4):
    rows, width = weight.shape
    half = width // 2
    pair, owners, tokens, local = normed.shape
    count = rows // split
    tile = pair * tokens // 8

    def kernel(*refs):
        weight_ref, normed_ref, gate_ref, up_ref = refs[:4]
        down_ref, hidden_ref, silu_ref, slope_ref = refs[4:8]
        relay, x, results, ss, rs, x_sem, result_sem = refs[8:]

        def loads(m, act):
            start = m % (8 // pair) * tile
            for j in range(owners):
                copy = pltpu.make_async_copy(
                    normed_ref.at[m // (8 // pair), j, pl.ds(start, tile), :],
                    x.at[m % 2, :, pl.ds(j * local, local)],
                    x_sem.at[m % 2, j],
                )
                getattr(copy, act)()

        def stores(m, act):
            for i, ref in enumerate((hidden_ref, silu_ref, slope_ref)):
                copy = pltpu.make_async_copy(
                    results.at[m % 2, i], ref.at[pl.ds(m * tile, tile), :], result_sem.at[m % 2, i]
                )
                getattr(copy, act)()

        loads(0, "start")
        loads(1, "start")
        p = Place()
        p.enter()
        chunks = [
            pair_gather_chunk(
                p, weight_ref, down_ref, relay.at[0], ss.at[c], rs.at[c], c * count, count, rows
            )
            for c in range(split)
        ]

        def compute(m):
            loads(m, "wait")
            if m >= 2:
                stores(m - 2, "wait")
            for part in range(2):
                here = pl.ds(part * half // 2, half // 2)
                value = dot(x[m % 2], gate_ref[:, here])
                upward = dot(x[m % 2], up_ref[:, here])
                sigmoid = jax.nn.sigmoid(value)
                silu = value * sigmoid
                results[m % 2, 0, :, here] = (silu * upward).astype(BF)
                results[m % 2, 1, :, here] = silu.astype(BF)
                results[m % 2, 2, :, here] = (
                    upward * (sigmoid + silu * (1.0 - sigmoid))
                ).astype(BF)
            stores(m, "start")
            if m + 2 < 8:
                loads(m + 2, "start")

        for step in range(split + 4):
            for stage in range(5):
                if 0 <= step - stage < split:
                    chunks[step - stage][stage]()
            for m in range(step * 8 // (split + 4), (step + 1) * 8 // (split + 4)):
                compute(m)
        stores(6, "wait")
        stores(7, "wait")

    units = jax.ShapeDtypeStruct((pair * tokens, half), BF)
    return pl.pallas_call(
        kernel,
        out_shape=[jax.ShapeDtypeStruct((8 * rows, half), BF), units, units, units],
        in_specs=[ANY, ANY, VMEM, VMEM],
        out_specs=[ANY] * 4,
        scratch_shapes=[
            pltpu.VMEM((1, 3, rows, half), BF),
            pltpu.VMEM((2, tile, owners * local), BF),
            pltpu.VMEM((2, 3, tile, half), BF),
            pltpu.SemaphoreType.DMA((split, 12)),
            pltpu.SemaphoreType.DMA((split, 10)),
            pltpu.SemaphoreType.DMA((2, owners)),
            pltpu.SemaphoreType.DMA((2, 3)),
        ],
        compiler_params=pltpu.CompilerParams(
            collective_id=collective, has_side_effects=True, vmem_limit_bytes=48 << 20
        ),
        cost_estimate=pl.CostEstimate(flops=0, bytes_accessed=100 << 20, transcendentals=0),
        name="gather_down_and_hidden",
    )(weight, normed, gate, up)


def line_gather_chunk(p, weight, out, ss, rs, first, count, rows):
    own = weight.at[pl.ds(first, count), :]

    def block(which, x):
        return out.at[pl.ds(pl.multiple_of(p.block(which, x) * rows + first, count), count), :]

    def send(slot, src, dst, recv, device):
        return remote(src, dst, ss.at[slot], rs.at[recv], device)

    def arrived(recv, dst):
        remote(dst, dst, ss.at[0], rs.at[recv], p.mate).wait_recv()

    local = pltpu.make_async_copy(own, block(OWN, p.x), ss.at[9])
    across = [
        send(k, own if k == OWN else block(k, p.x), block(k, p.x), 3 + k, p.across)
        for k in range(4)
    ]
    to_mate = send(4, own, block(OWN, p.x), MATE - 1, p.mate)
    to_mid = send(5, own, block(OWN, p.x), NEAR - 1, p.mid)
    mid_far = send(6, block(MATE, p.x), block(MATE, p.x), FAR - 1, p.mid)
    back_near = send(7, block(NEAR, p.x), block(NEAR, p.x), NEAR - 1, p.mate)
    back_far = send(8, block(FAR, p.x), block(FAR, p.x), FAR - 1, p.mate)

    def begin():
        @pl.when(p.inner)
        def _():
            to_mid.start()

        to_mate.start()
        across[OWN].start()
        local.start()

    def mate_here():
        arrived(MATE - 1, block(MATE, p.x))

        @pl.when(p.inner)
        def _():
            mid_far.start()

        across[MATE].start()

    def near_here():
        arrived(NEAR - 1, block(NEAR, p.x))

        @pl.when(p.inner)
        def _():
            back_near.start()

        across[NEAR].start()

    def far_here():
        arrived(FAR - 1, block(FAR, p.x))

        @pl.when(p.inner)
        def _():
            back_far.start()

        across[FAR].start()

    def finish():
        for k in range(4):
            arrived(3 + k, block(k, 1 - p.x))
            across[k].wait_send()
        local.wait()
        to_mate.wait_send()

        @pl.when(p.inner)
        def _():
            for copy in (to_mid, mid_far, back_near, back_far):
                copy.wait_send()

    return [begin, mate_here, near_here, far_here, finish]


def gather_line(weights, collective, split=2):
    n = len(weights)
    rows = weights[0].shape[0]
    count = rows // split

    def kernel(*refs):
        ins, outs = refs[:n], refs[n : 2 * n]
        ss, rs = refs[2 * n :]
        p = Place()
        p.enter()
        in_stages(
            [
                line_gather_chunk(
                    p, ins[i], outs[i], ss.at[i * split + c], rs.at[i * split + c],
                    c * count, count, rows,
                )
                for i in range(n)
                for c in range(split)
            ]
        )

    return pl.pallas_call(
        kernel,
        out_shape=[jax.ShapeDtypeStruct((8 * rows, w.shape[1]), BF) for w in weights],
        in_specs=[ANY] * n,
        out_specs=[ANY] * n,
        scratch_shapes=[
            pltpu.SemaphoreType.DMA((n * split, 10)),
            pltpu.SemaphoreType.DMA((n * split, 7)),
        ],
        compiler_params=pltpu.CompilerParams(
            collective_id=collective, has_side_effects=True, vmem_limit_bytes=32 << 20
        ),
        cost_estimate=pl.CostEstimate(flops=0, bytes_accessed=n * (100 << 20), transcendentals=0),
        name="gather_line",
    )(*weights)


def contract_tokens(left, right):
    return lax.dot_general(left, right, (((0,), (0,)), ((), ())), preferred_element_type=F32)


class PairScatter:
    def __init__(self, p, product, sx, rx, sz, rz, rm, held, out, ss, rs):
        self.p, self.product = p, product
        self.sx, self.rx, self.sz, self.rz, self.rm = sx, rx, sz, rz, rm
        self.held, self.out, self.ss, self.rs = held, out, ss, rs
        self.half = held.shape[1]

    def across(self, k):
        return remote(self.sx.at[k], self.rx.at[k], self.ss.at[k], self.rs.at[k], self.p.across)

    def outward(self, j):
        return remote(self.sz.at[j], self.rz.at[j], self.ss.at[4 + j], self.rs.at[4 + j], self.p.mate)

    def middle(self, j):
        return remote(self.sz.at[j], self.rm.at[j], self.ss.at[7 + j], self.rs.at[7 + j], self.p.mid)

    def relay(self, j):
        return remote(
            self.rz.at[j], self.rm.at[2 + j], self.ss.at[9 + j], self.rs.at[9 + j], self.p.mid
        )

    def forward(self):
        return remote(self.rm.at[0], self.rz.at[0], self.ss.at[4], self.rs.at[4], self.p.mate)

    def back(self):
        return remote(self.sz.at[2], self.rz.at[1], self.ss.at[5], self.rs.at[5], self.p.mate)

    def cols_of(self, place):
        return pl.ds(pl.multiple_of(place * self.half, self.half), self.half)

    def send_across(self, k, *sent):
        self.sx[k] = self.product(k, 1 - self.p.x).astype(BF)
        self.sent(*sent)
        self.across(k).start()

    def summed(self, k):
        total = self.product(k, self.p.x)
        self.across(k).wait_recv()
        return total + self.rx[k].astype(F32)

    def send_on(self, k, j):
        self.sz[j] = self.summed(k).astype(BF)

        @pl.when(self.p.outer)
        def _():
            self.outward(j).start()

        @pl.when(self.p.inner)
        def _():
            self.middle(j).start()

    def send_relay(self, j):
        @pl.when(self.p.inner)
        def _():
            self.outward(j).wait_recv()
            self.relay(j).start()

    def mate_rows(self):
        total = self.summed(MATE)

        @pl.when(self.p.outer)
        def _():
            self.sz[2] = total.astype(BF)
            self.outward(2).start()

        @pl.when(self.p.inner)
        def _():
            self.held[...] = total

    def send_forward(self):
        @pl.when(self.p.inner)
        def _():
            self.middle(0).wait_recv()
            self.forward().start()

    def own_rows(self):
        self.out[:, self.cols_of(self.p.zl)] = self.summed(OWN)

    def send_back(self):
        @pl.when(self.p.inner)
        def _():
            self.relay(0).wait_recv()
            self.sz[2] = (self.held[...] + self.rm[2].astype(F32)).astype(BF)
            self.back().start()

    def finish(self):
        p, out = self.p, self.out
        here, there = self.cols_of(p.zl), self.cols_of(1 - p.zl)

        @pl.when(p.inner)
        def _():
            self.relay(1).wait_recv()
            out[:, here] = out[:, here] + self.rm[3].astype(F32)
            self.outward(2).wait_recv()
            self.middle(1).wait_recv()
            out[:, there] = self.rz[2].astype(F32) + self.rm[1].astype(F32)

        @pl.when(p.outer)
        def _():
            self.forward().wait_recv()
            out[:, here] = out[:, here] + self.rz[0].astype(F32)
            self.back().wait_recv()
            out[:, there] = self.rz[1].astype(F32)

        @pl.when(p.inner)
        def _():
            for j in range(2):
                self.relay(j).wait_send()
            self.forward().wait_send()

    def sent_on(self):
        @pl.when(self.p.outer)
        def _():
            for j in range(3):
                self.outward(j).wait_send()

        @pl.when(self.p.inner)
        def _():
            for j in range(2):
                self.middle(j).wait_send()
            self.back().wait_send()

    def sent(self, *which):
        for k in which:
            self.across(k).wait_send()


def pair_scatter_scratch(n, rows, half):
    return [
        pltpu.VMEM((4, rows, half), BF),
        pltpu.VMEM((n, 4, rows, half), BF),
        pltpu.VMEM((3, rows, half), BF),
        pltpu.VMEM((n, 3, rows, half), BF),
        pltpu.VMEM((n, 4, rows, half), BF),
        pltpu.VMEM((rows, half), F32),
        pltpu.SemaphoreType.DMA((n, 11)),
        pltpu.SemaphoreType.DMA((n, 11)),
    ]


class Columns:
    def __init__(self, p, jobs, buffer, sems):
        self.p, self.jobs, self.buffer, self.sems, self.at = p, jobs, buffer, sems, 0
        for n in range(min(2, len(jobs))):
            self.copies(n, "start")

    def copies(self, n, act):
        array, k, flip = self.jobs[n]
        pair, _, tokens, local = array.shape
        rows = self.buffer.shape[2]
        start = self.p.block(k, 1 - self.p.x if flip else self.p.x) * rows
        cols = pl.ds(pl.multiple_of(start % local, rows), rows)
        for q in range(pair):
            copy = pltpu.make_async_copy(
                array.at[q, start // local, :, cols],
                self.buffer.at[n % 2, pl.ds(q * tokens, tokens), :],
                self.sems.at[n % 2, q],
            )
            getattr(copy, act)()

    def times(self, right):
        n = self.at
        self.at += 1
        self.copies(n, "wait")
        product = contract_tokens(self.buffer[n % 2], right)
        if n + 2 < len(self.jobs):
            self.copies(n + 2, "start")
        return product


ORDER = (FAR, NEAR, MATE, OWN)


def scatter_pair(left, right, collective):
    tokens, half = right.shape
    rows = left.shape[1] * left.shape[3] // 8

    def kernel(left_ref, right_ref, out, *scratch):
        sx, rx, sz, rz, rm, held, ss, rs, cols, cols_sem = scratch
        p = Place()
        p.enter()
        feed = Columns(
            p, [(left_ref, k, flip) for flip in (True, False) for k in ORDER], cols, cols_sem
        )
        m = PairScatter(
            p, lambda k, x: feed.times(right_ref[...]), sx, rx.at[0], sz, rz.at[0], rm.at[0],
            held, out, ss.at[0], rs.at[0],
        )
        m.send_across(FAR)
        m.send_across(NEAR)
        m.send_across(MATE, FAR)
        m.send_across(OWN, NEAR)
        m.send_on(FAR, 0)
        m.send_on(NEAR, 1)
        m.send_relay(0)
        m.mate_rows()
        m.send_relay(1)
        m.send_forward()
        m.own_rows()
        m.send_back()
        m.finish()
        m.sent_on()
        m.sent(MATE, OWN)

    return pl.pallas_call(
        kernel,
        out_shape=jax.ShapeDtypeStruct((rows, 2 * half), F32),
        in_specs=[ANY, VMEM],
        out_specs=VMEM,
        scratch_shapes=pair_scatter_scratch(1, rows, half)
        + [pltpu.VMEM((2, tokens, rows), BF), pltpu.SemaphoreType.DMA((2, 2))],
        compiler_params=pltpu.CompilerParams(
            collective_id=collective, has_side_effects=True, vmem_limit_bytes=40 << 20
        ),
        cost_estimate=pl.CostEstimate(flops=0, bytes_accessed=150 << 20, transcendentals=0),
        name="scatter_pair",
    )(left, right)


def scatter_line(lefts, rights, which, collective):
    n, nx, ny = len(which), len(lefts), len(rights)
    rows = lefts[0].shape[1] // 8
    width = min(r.shape[1] for r in rights)

    def kernel(*refs):
        left, right, out = refs[:nx], refs[nx : nx + ny], refs[nx + ny : nx + 2 * ny]
        sx, rx, sz, rz, rm, own, ss, rs = refs[nx + 2 * ny :]
        p = Place()
        p.enter()

        def product(i, k, x):
            a, b, group = which[i]
            cols = pl.ds(pl.multiple_of(p.block(k, x) * rows, rows), rows)
            return contract_tokens(
                left[a][:, cols], right[b][:, group * width : (group + 1) * width]
            )

        def across(i, k):
            return remote(sx.at[i, k], rx.at[i, k], ss.at[i, k], rs.at[i, k], p.across)

        def outward(i, j):
            return remote(sz.at[i, j], rz.at[i, j], ss.at[i, 4 + j], rs.at[i, 4 + j], p.mate)

        def middle(i, j):
            return remote(sz.at[i, j], rm.at[i, j], ss.at[i, 7 + j], rs.at[i, 7 + j], p.mid)

        def back(i):
            return remote(sz.at[i, 2], rz.at[i, 0], ss.at[i, 4], rs.at[i, 4], p.mate)

        def send_across(i):
            for k in (FAR, NEAR, MATE, OWN):
                sx[i, k] = product(i, k, 1 - p.x).astype(BF)
                across(i, k).start()

        def summed(i, k):
            total = product(i, k, p.x)
            across(i, k).wait_recv()
            return total + rx[i, k].astype(F32)

        def send_on(i, k, j):
            total = summed(i, k)

            @pl.when(p.outer)
            def _():
                sz[i, j] = total.astype(BF)
                outward(i, j).start()

            @pl.when(p.inner)
            def _():
                outward(i, j).wait_recv()
                sz[i, j] = (total + rz[i, j].astype(F32)).astype(BF)
                middle(i, j).start()

        def mate_rows(i):
            total = summed(i, MATE)

            @pl.when(p.outer)
            def _():
                sz[i, 2] = total.astype(BF)
                outward(i, 2).start()

            @pl.when(p.inner)
            def _():
                own[i, 0] = total

        def own_rows(i):
            own[i, 1] = summed(i, OWN)

        def finish(i):
            b, group = which[i][1:]
            here = pl.ds(group * width, width)

            @pl.when(p.inner)
            def _():
                middle(i, 0).wait_recv()
                sz[i, 2] = (own[i, 0] + rm[i, 0].astype(F32)).astype(BF)
                back(i).start()
                outward(i, 2).wait_recv()
                middle(i, 1).wait_recv()
                out[b][:, here] = own[i, 1] + rz[i, 2].astype(F32) + rm[i, 1].astype(F32)

            @pl.when(p.outer)
            def _():
                back(i).wait_recv()
                out[b][:, here] = own[i, 1] + rz[i, 0].astype(F32)
                for j in range(3):
                    outward(i, j).wait_send()

            for k in range(4):
                across(i, k).wait_send()

            @pl.when(p.inner)
            def _():
                for j in range(2):
                    middle(i, j).wait_send()
                back(i).wait_send()

        send_across(0)
        for i in range(n):
            if i + 1 < n:
                send_across(i + 1)
            send_on(i, FAR, 0)
            send_on(i, NEAR, 1)
            mate_rows(i)
            own_rows(i)
            if i > 0:
                finish(i - 1)
        finish(n - 1)

    return pl.pallas_call(
        kernel,
        out_shape=[jax.ShapeDtypeStruct((rows, r.shape[1]), F32) for r in rights],
        in_specs=[VMEM] * (nx + ny),
        out_specs=[VMEM] * ny,
        scratch_shapes=[
            pltpu.VMEM((n, 4, rows, width), BF),
            pltpu.VMEM((n, 4, rows, width), BF),
            pltpu.VMEM((n, 3, rows, width), BF),
            pltpu.VMEM((n, 3, rows, width), BF),
            pltpu.VMEM((n, 2, rows, width), BF),
            pltpu.VMEM((n, 2, rows, width), F32),
            pltpu.SemaphoreType.DMA((n, 9)),
            pltpu.SemaphoreType.DMA((n, 9)),
        ],
        compiler_params=pltpu.CompilerParams(
            collective_id=collective, has_side_effects=True, vmem_limit_bytes=60 << 20
        ),
        cost_estimate=pl.CostEstimate(flops=0, bytes_accessed=n * (80 << 20), transcendentals=0),
        name="scatter_line",
    )(*lefts, *rights)


def feed_forward_backward(out_rows, normed, hidden, silu, slope, gate, up, down, collective):
    pair, owners, tokens, local = normed.shape
    total, half = hidden.shape
    rows = owners * local // 8
    tile = total // 8
    piece = total // 4

    def kernel(*refs):
        out_ref, normed_ref, hidden_ref, silu_ref, slope_ref, gate_ref, up_ref, down_ref = refs[:8]
        normed_grad, down_grad, gate_grad, up_rows = refs[8:12]
        gate_rows, weights, cols, outs, factors, to_core, sums, from_y, from_mate = refs[12:21]
        cols_sem, outs_sem, factors_sem, weights_sem, move_ss, move_rs = refs[21:27]
        sx, rx, sz, rz, rm, held, ss, rs = refs[27:]
        p = Place()
        core = (p.zh, p.zl, p.x, p.y, 1 - p.c)
        side = (p.zh, p.zl, p.x, 1 - p.y, p.c)

        down_load = pltpu.make_async_copy(down_ref, weights, weights_sem.at[0])
        down_load.start()

        def tile_loads(m, act):
            start = m % (8 // pair) * tile
            for j in range(owners):
                copy = pltpu.make_async_copy(
                    out_ref.at[m // (8 // pair), j, pl.ds(start, tile), :],
                    outs.at[m % 2, :, pl.ds(j * local, local)],
                    outs_sem.at[m % 2, j],
                )
                getattr(copy, act)()
            for i, ref in enumerate((silu_ref, slope_ref)):
                copy = pltpu.make_async_copy(
                    ref.at[pl.ds(m * tile, tile), :], factors.at[m % 2, i], factors_sem.at[m % 2, i]
                )
                getattr(copy, act)()

        D = (out_ref, normed_ref)
        jobs = [(D[0], k, True) for k in ORDER] + [(D[0], FAR, False), (D[0], NEAR, False)]
        jobs += [(D[1], FAR, True), (D[1], NEAR, True), (D[0], MATE, False), (D[0], OWN, False)]
        jobs += [(D[1], MATE, True), (D[1], OWN, True)]
        jobs += [(D[1], k, False) for k in ORDER]
        feed = Columns(p, jobs, cols, cols_sem)
        tile_loads(0, "start")
        tile_loads(1, "start")
        p.enter(core, side)

        dm = PairScatter(
            p, lambda k, x: feed.times(hidden_ref[...]), sx, rx.at[0], sz, rz.at[0],
            rm.at[0], held, down_grad, ss.at[0], rs.at[0],
        )
        gm = PairScatter(
            p, lambda k, x: feed.times(gate_rows[...]), sx, rx.at[1], sz, rz.at[1],
            rm.at[1], held, gate_grad, ss.at[1], rs.at[1],
        )

        def rows_backward(m):
            tile_loads(m, "wait")
            here = pl.ds(m * tile, tile)
            hidden_grad = dot(outs[m % 2], weights[...])
            up_rows[here, :] = (hidden_grad * factors[m % 2, 0].astype(F32)).astype(BF)
            gate_rows[here, :] = (hidden_grad * factors[m % 2, 1].astype(F32)).astype(BF)
            if m + 2 < 8:
                tile_loads(m + 2, "start")

        owner = [
            2 * (1 - p.y) + 1 - p.c, 2 * (1 - p.y) + p.c, 2 * p.y + 1 - p.c, 2 * p.y + p.c
        ]

        def weight_loads(n, act):
            start = pl.multiple_of(owner[n] * local, local)
            for i, ref in enumerate((gate_ref, up_ref)):
                copy = pltpu.make_async_copy(
                    ref.at[pl.ds(start, local), :],
                    weights.at[pl.ds((n % 2 * 2 + i) * local, local), :],
                    weights_sem.at[1 + n % 2 * 2 + i],
                )
                getattr(copy, act)()

        def piece_rows(t):
            place = p.zl if t >= 2 else 1 - p.zl
            return pl.ds(pl.multiple_of(place * tokens + t % 2 * piece, piece), piece)

        def core_copy(b, t):
            return remote(
                to_core.at[b, t], sums.at[b, t], move_ss.at[b, t], move_rs.at[b, t], core
            )

        def side_copy(t):
            return remote(sums.at[0, t], from_y.at[t], move_ss.at[2, t], move_rs.at[2, t], side)

        def mate_copy(t):
            return remote(sums.at[1, t], from_mate.at[t], move_ss.at[3, t], move_rs.at[3, t], p.mate)

        def partial_sum(n, t):
            here = piece_rows(t)
            first = n % 2 * 2 * local
            return contract_cols(gate_rows[here, :], weights[first : first + local, :]) + contract_cols(
                up_rows[here, :], weights[first + local : first + 2 * local, :]
            )

        def partial_block(n):
            weight_loads(n, "wait")
            for t in range(4):
                value = partial_sum(n, t)
                b = n // 2
                if n % 2 == 0:
                    to_core[b, t] = value.astype(BF)
                    core_copy(b, t).start()
                else:
                    core_copy(b, t).wait_recv()
                    sums[b, t] = (value + sums[b, t].astype(F32)).astype(BF)
                    if b == 0 and t < 2:
                        side_copy(t).start()
            if n + 2 < 4:
                weight_loads(n + 2, "start")

        def side_next():
            for t in range(2):
                side_copy(t).wait_send()
                side_copy(t + 2).start()

        def to_mate(t):
            side_copy(t).wait_recv()
            sums[1, t] = (sums[1, t].astype(F32) + from_y[t].astype(F32)).astype(BF)
            mate_copy(t).start()

        def final(t):
            side_copy(t).wait_recv()
            mate_copy(t - 2).wait_recv()
            normed_grad[pl.ds((t - 2) * piece, piece), :] = (
                sums[1, t].astype(F32) + from_y[t].astype(F32) + from_mate[t - 2].astype(F32)
            )

        dm.send_across(FAR)
        dm.send_across(NEAR)
        down_load.wait()
        for m in range(8):
            rows_backward(m)
        weight_loads(0, "start")
        weight_loads(1, "start")
        dm.send_across(MATE, FAR)
        dm.send_across(OWN, NEAR)
        dm.send_on(FAR, 0)
        dm.send_on(NEAR, 1)
        partial_block(0)
        partial_block(1)
        dm.send_relay(0)
        partial_block(2)
        dm.sent(MATE)
        gm.send_across(FAR)
        dm.sent(OWN)
        gm.send_across(NEAR)
        dm.mate_rows()
        dm.send_relay(1)
        dm.send_forward()
        dm.own_rows()
        partial_block(3)
        side_next()
        dm.send_back()
        to_mate(0)
        gm.send_across(MATE, FAR)
        gm.send_across(OWN, NEAR)
        to_mate(1)
        dm.sent_on()
        gm.send_on(FAR, 0)
        gm.send_on(NEAR, 1)
        gm.send_relay(0)
        final(2)
        final(3)
        gm.mate_rows()
        gm.send_relay(1)
        gm.send_forward()
        gm.own_rows()
        gm.send_back()
        dm.finish()
        gm.finish()
        gm.sent_on()
        gm.sent(MATE, OWN)
        for t in range(4):
            core_copy(0, t).wait_send()
            core_copy(1, t).wait_send()
        for t in range(2):
            side_copy(t + 2).wait_send()
            mate_copy(t).wait_send()

    grad = jax.ShapeDtypeStruct((rows, 2 * half), F32)
    return pl.pallas_call(
        kernel,
        out_shape=[
            jax.ShapeDtypeStruct((tokens, local), F32),
            grad,
            grad,
            jax.ShapeDtypeStruct((total, half), BF),
        ],
        in_specs=[ANY, ANY, VMEM, ANY, ANY, ANY, ANY, ANY],
        out_specs=[VMEM] * 4,
        scratch_shapes=[
            pltpu.VMEM((total, half), BF),
            pltpu.VMEM((owners * local, half), BF),
            pltpu.VMEM((2, total, rows), BF),
            pltpu.VMEM((2, tile, owners * local), BF),
            pltpu.VMEM((2, 2, tile, half), BF),
            pltpu.VMEM((2, 4, piece, local), BF),
            pltpu.VMEM((2, 4, piece, local), BF),
            pltpu.VMEM((4, piece, local), BF),
            pltpu.VMEM((2, piece, local), BF),
            pltpu.SemaphoreType.DMA((2, pair)),
            pltpu.SemaphoreType.DMA((2, owners)),
            pltpu.SemaphoreType.DMA((2, 2)),
            pltpu.SemaphoreType.DMA((5,)),
            pltpu.SemaphoreType.DMA((4, 4)),
            pltpu.SemaphoreType.DMA((4, 4)),
        ]
        + pair_scatter_scratch(2, rows, half),
        compiler_params=pltpu.CompilerParams(
            collective_id=collective, has_side_effects=True, vmem_limit_bytes=62 << 20
        ),
        cost_estimate=pl.CostEstimate(flops=0, bytes_accessed=300 << 20, transcendentals=0),
        name="feed_forward_backward",
    )(out_rows, normed, hidden, silu, slope, gate, up, down)


SEQ = ("zh", "zl", "x")
TP = ("y", "c")
PAIR = ("zl", "y", "c")


def after(value, *others):
    return lax.optimization_barrier((value, *others))[0]


def gather_pair_rows(rows):
    blocks = lax.all_gather(rows, PAIR, axis=0)
    return blocks.reshape(lax.axis_size("zl"), lax.axis_size(TP), *rows.shape)


def reduce_pair_product(left, right):
    pair, parts = lax.axis_size("zl"), lax.axis_size(TP)
    tokens, local = left.shape[0] // pair, right.shape[0] // parts
    blocks = jnp.concatenate(
        [
            contract_cols(
                left[q * tokens : (q + 1) * tokens], right[j * local : (j + 1) * local]
            ).astype(BF)
            for q in range(pair)
            for j in range(parts)
        ]
    )
    return lax.psum_scatter(blocks, PAIR, scatter_dimension=0, tiled=True).astype(F32)


def reduce_features(partial_rows):
    return lax.psum_scatter(
        partial_rows.astype(BF), TP, scatter_dimension=1, tiled=True
    ).astype(F32)


def rms_scale(values, gain):
    width = gain.shape[0] * lax.axis_size(TP)
    squares = lax.psum(jnp.sum(values * values, axis=1, keepdims=True), TP)
    inverse = lax.rsqrt(squares / width + epsilon)
    return (values * inverse * gain).astype(BF), inverse, jnp.sqrt(squares[:, 0] / width + epsilon)


def scale_backward(values, gain, inverse, grad_rows):
    width = gain.shape[0] * lax.axis_size(TP)
    gained = gain * grad_rows
    total = lax.psum(jnp.sum(values * gained, axis=1, keepdims=True), TP)
    grad_values = inverse * gained - values * inverse**3 * (total / width)
    return grad_values, jnp.sum(grad_rows * values * inverse, axis=0)


def paired_on_device(
    stream,
    norm1_gain,
    in_weight,
    conv_weight,
    out_weight,
    norm2_gain,
    gate_weight,
    up_weight,
    down_weight,
    doc_starts,
    out_grad,
):
    tokens, local = stream.shape
    rows_here = in_weight.shape[0]
    positions = lax.axis_index(SEQ) * tokens + jnp.arange(tokens, dtype=jnp.int32)
    mask_one, mask_two = lag_masks(doc_starts, positions)
    normed_here, inverse_in, rms_in = rms_scale(stream, norm1_gain)
    normed_in = lax.all_gather(normed_here, TP, axis=1, tiled=True)
    in_matrix, whole_out = gather_line(
        [after(in_weight.reshape(rows_here, 3 * local), normed_here), out_weight], 0
    )
    out_full = gather_pair_rows(after(out_grad.astype(BF), normed_here))
    in_matrix = after(in_matrix, out_full)
    projected = dot(normed_in, in_matrix)
    in_gate = projected[:, :local]
    out_gate = projected[:, local : 2 * local]
    carried = projected[:, 2 * local :]
    mixed = in_gate * carried
    previous = from_behind(mixed[-2:], SEQ, 1)
    extended = jnp.concatenate([previous, mixed], axis=0)
    convolved = (
        conv_weight[0] * mixed
        + mask_one * conv_weight[1] * extended[1:-1]
        + mask_two * conv_weight[2] * extended[:-2]
    )
    gated = (out_gate * convolved).astype(BF)
    mixer_partial = contract_cols(gated, whole_out).astype(BF)
    mixer_out = reduce_features(mixer_partial)
    (whole_gate,) = gather_pair([after(gate_weight, mixer_partial)], 1)
    mixer_out = after(mixer_out, whole_gate)
    middle = stream + mixer_out
    normed_mid_here, inverse_mid, rms_mid = rms_scale(middle, norm2_gain)
    normed_mid = gather_pair_rows(normed_mid_here)
    (whole_up,) = gather_pair([after(up_weight, normed_mid_here)], 2)
    normed_mid = after(normed_mid, whole_up)
    whole_down, hidden, silu, slope = gather_down_and_hidden(
        down_weight, normed_mid, whole_gate, whole_up, 3
    )
    result = middle + reduce_pair_product(hidden, whole_down)
    normed_mid_grad, down_weight_grad, gate_weight_grad, up_rows = feed_forward_backward(
        out_full, normed_mid, hidden, silu, slope, whole_gate, whole_up, whole_down, 4
    )
    middle_norm_grad, gain_mid_grad = scale_backward(
        middle, norm2_gain, inverse_mid, normed_mid_grad
    )
    middle_grad = out_grad + middle_norm_grad
    branch_here = middle_grad.astype(BF)
    branch_full = lax.all_gather(branch_here, TP, axis=1, tiled=True)
    up_weight_grad = scatter_pair(normed_mid, after(up_rows, branch_here), 5)
    branch_full = after(branch_full, up_weight_grad)
    gated_grad = dot(branch_full, whole_out)
    out_gate_grad = gated_grad * convolved
    conv_grad = gated_grad * out_gate
    lag_one = mask_one * conv_grad
    lag_two = mask_two * conv_grad
    next_one, next_two = from_behind((lag_one[:2], lag_two[:2]), SEQ, -1)
    after_one = jnp.concatenate([lag_one, next_one], axis=0)
    after_two = jnp.concatenate([lag_two, next_two], axis=0)
    mixed_grad = (
        conv_weight[0] * conv_grad
        + conv_weight[1] * after_one[1 : tokens + 1]
        + conv_weight[2] * after_two[2:]
    )
    tap_grads = jnp.stack(
        [
            jnp.sum(conv_grad * mixed, axis=0),
            jnp.sum(lag_one * extended[1:-1], axis=0),
            jnp.sum(lag_two * extended[:-2], axis=0),
        ]
    )
    projected_grad = jnp.concatenate(
        [mixed_grad * carried, out_gate_grad, mixed_grad * in_gate], axis=1
    ).astype(BF)
    in_partial = contract_cols(projected_grad, in_matrix).astype(BF)
    normed_in_grad = reduce_features(in_partial)
    out_weight_grad, in_weight_grad = scatter_line(
        [normed_in, branch_full],
        [after(gated, in_partial), projected_grad],
        [(1, 0, 0), (0, 1, 0), (0, 1, 1), (0, 1, 2)],
        6,
    )
    normed_in_grad = after(normed_in_grad, in_weight_grad)
    stream_norm_grad, gain_in_grad = scale_backward(stream, norm1_gain, inverse_in, normed_in_grad)
    stream_grad = middle_grad + stream_norm_grad
    conv_total, gain_in_total, gain_mid_total = lax.psum(
        (tap_grads, gain_in_grad, gain_mid_grad), SEQ
    )
    return (
        result,
        stream_grad,
        gain_in_total,
        in_weight_grad.reshape(rows_here, 3, local),
        conv_total,
        out_weight_grad,
        gain_mid_total,
        gate_weight_grad,
        up_weight_grad,
        down_weight_grad,
        jnp.stack([rms_in, rms_mid]),
    )


def solution(mesh):
    seq, tp = mesh.shape["seq"], mesh.shape["tp"]
    if (seq, tp) == (8, 4):
        shape, names = (2, 2, 2, 2, 2), ("zh", "zl", "x", "y", "c")
        mesh = Mesh(mesh.devices.reshape(shape), names)
        body, rows, cols = paired_on_device, SEQ, TP
    else:
        body, rows, cols = on_device, "seq", "tp"
    return jax.shard_map(
        body,
        mesh=mesh,
        in_specs=(
            P(rows, cols),
            P(cols),
            P(rows, None, cols),
            P(None, cols),
            P(rows, cols),
            P(cols),
            P(rows, cols),
            P(rows, cols),
            P(rows, cols),
            P(),
            P(rows, cols),
        ),
        out_specs=(
            P(rows, cols),
            P(rows, cols),
            P(cols),
            P(rows, None, cols),
            P(None, cols),
            P(rows, cols),
            P(cols),
            P(rows, cols),
            P(rows, cols),
            P(rows, cols),
            P(None, rows),
        ),
        check_vma=False,
    )
```

```python
import jax
import jax.numpy as jnp
from jax import lax
from jax.experimental import pallas as pl
from jax.experimental.pallas import tpu as pltpu
from jax.sharding import Mesh, PartitionSpec as P

epsilon = 1e-05


def from_behind(shard, axis, by):
    count = lax.axis_size(axis)
    pairs = [(i, i + by) for i in range(count) if 0 <= i + by < count]
    return lax.ppermute(shard, axis, pairs)


def doc_count(doc_starts, positions):
    return jnp.sum((doc_starts[None, :] <= positions[:, None]).astype(jnp.int32), axis=1)


def lag_masks(doc_starts, positions):
    current = doc_count(doc_starts, positions)
    one = (positions >= 1) & (doc_count(doc_starts, positions - 1) == current)
    two = (positions >= 2) & (doc_count(doc_starts, positions - 2) == current)
    return (one.astype(jnp.float32)[:, None], two.astype(jnp.float32)[:, None])


def contract_rows(left, right):
    return lax.dot_general(
        left, right, (((0,), (0,)), ((), ())), preferred_element_type=jnp.float32
    )


def contract_cols(left, right):
    return lax.dot_general(
        left, right, (((1,), (1,)), ((), ())), preferred_element_type=jnp.float32
    )


def reduce_tp(partial_rows):
    return lax.psum_scatter(
        partial_rows.astype(jnp.bfloat16), "tp", scatter_dimension=1, tiled=True
    ).astype(jnp.float32)


def reduce_seq(partial_grad):
    return lax.psum_scatter(
        partial_grad.astype(jnp.bfloat16), "seq", scatter_dimension=0, tiled=True
    ).astype(jnp.float32)


def gather_grads(grad_rows):
    return lax.all_gather(grad_rows, "tp", axis=1, tiled=True)


def normalize(values, gain):
    width = gain.shape[0] * lax.axis_size("tp")
    squares = lax.psum(jnp.sum(values * values, axis=1, keepdims=True), "tp")
    inverse = lax.rsqrt(squares / width + epsilon)
    normed = lax.all_gather(
        (values * inverse * gain).astype(jnp.bfloat16), "tp", axis=1, tiled=True
    )
    return (normed, inverse, jnp.sqrt(squares[:, 0] / width + epsilon))


def norm_backward(values, gain, inverse, grad_rows):
    width = gain.shape[0] * lax.axis_size("tp")
    gained = gain * grad_rows
    total = lax.psum(jnp.sum(values * gained, axis=1, keepdims=True), "tp")
    grad_values = inverse * gained - values * inverse**3 * (total / width)
    grad_gain = jnp.sum(grad_rows * values * inverse, axis=0)
    return (grad_values, grad_gain)


def on_device(
    stream,
    norm1_gain,
    in_weight,
    conv_weight,
    out_weight,
    norm2_gain,
    gate_weight,
    up_weight,
    down_weight,
    doc_starts,
    out_grad,
):
    tokens = stream.shape[0]
    local = stream.shape[1]
    rows_here = in_weight.shape[0]
    whole_in, whole_out, whole_gate, whole_up, whole_down = (
        lax.all_gather(in_weight, "seq", axis=0, tiled=True),
        lax.all_gather(out_weight, "seq", axis=0, tiled=True),
        lax.all_gather(gate_weight, "seq", axis=0, tiled=True),
        lax.all_gather(up_weight, "seq", axis=0, tiled=True),
        lax.all_gather(down_weight, "seq", axis=0, tiled=True),
    )
    width = whole_out.shape[0]
    in_matrix = whole_in.reshape(width, 3 * local)
    positions = lax.axis_index("seq") * tokens + jnp.arange(tokens, dtype=jnp.int32)
    mask_one, mask_two = lag_masks(doc_starts, positions)
    normed_in, inverse_in, rms_in = normalize(stream, norm1_gain)
    projected = jnp.dot(normed_in, in_matrix, preferred_element_type=jnp.float32)
    in_gate = projected[:, :local]
    out_gate = projected[:, local : 2 * local]
    carried = projected[:, 2 * local :]
    mixed = in_gate * carried
    previous = from_behind(mixed[-2:], "seq", 1)
    extended = jnp.concatenate([previous, mixed], axis=0)
    convolved = (
        conv_weight[0] * mixed
        + mask_one * conv_weight[1] * extended[1:-1]
        + mask_two * conv_weight[2] * extended[:-2]
    )
    gated = (out_gate * convolved).astype(jnp.bfloat16)
    middle = stream + reduce_tp(contract_cols(gated, whole_out))
    normed_mid, inverse_mid, rms_mid = normalize(middle, norm2_gain)
    gate = jnp.dot(normed_mid, whole_gate, preferred_element_type=jnp.float32)
    upward = jnp.dot(normed_mid, whole_up, preferred_element_type=jnp.float32)
    hidden = (jax.nn.silu(gate) * upward).astype(jnp.bfloat16)
    result = middle + reduce_tp(contract_cols(hidden, whole_down))
    out_full = gather_grads(out_grad.astype(jnp.bfloat16))
    hidden_grad = jnp.dot(out_full, whole_down, preferred_element_type=jnp.float32)
    sigmoid_gate = jax.nn.sigmoid(gate)
    gate_rows = (hidden_grad * upward * sigmoid_gate * (1.0 + gate * (1.0 - sigmoid_gate))).astype(
        jnp.bfloat16
    )
    up_rows = (hidden_grad * gate * sigmoid_gate).astype(jnp.bfloat16)
    normed_mid_grad = reduce_tp(
        contract_cols(gate_rows, whole_gate) + contract_cols(up_rows, whole_up)
    )
    middle_norm_grad, gain_mid_grad = norm_backward(
        middle, norm2_gain, inverse_mid, normed_mid_grad
    )
    middle_grad = out_grad + middle_norm_grad
    branch_full = gather_grads(middle_grad.astype(jnp.bfloat16))
    gated_grad = jnp.dot(branch_full, whole_out, preferred_element_type=jnp.float32)
    out_gate_grad = gated_grad * convolved
    conv_grad = gated_grad * out_gate
    lag_one = mask_one * conv_grad
    lag_two = mask_two * conv_grad
    next_one, next_two = from_behind((lag_one[:2], lag_two[:2]), "seq", -1)
    after_one = jnp.concatenate([lag_one, next_one], axis=0)
    after_two = jnp.concatenate([lag_two, next_two], axis=0)
    mixed_grad = (
        conv_weight[0] * conv_grad
        + conv_weight[1] * after_one[1 : tokens + 1]
        + conv_weight[2] * after_two[2:]
    )
    tap_grads = jnp.stack(
        [
            jnp.sum(conv_grad * mixed, axis=0),
            jnp.sum(lag_one * extended[1:-1], axis=0),
            jnp.sum(lag_two * extended[:-2], axis=0),
        ]
    )
    projected_grad = jnp.concatenate(
        [mixed_grad * carried, out_gate_grad, mixed_grad * in_gate], axis=1
    ).astype(jnp.bfloat16)
    normed_in_grad = reduce_tp(contract_cols(projected_grad, in_matrix))
    stream_norm_grad, gain_in_grad = norm_backward(stream, norm1_gain, inverse_in, normed_in_grad)
    stream_grad = middle_grad + stream_norm_grad
    conv_total, gain_in_total, gain_mid_total = lax.psum(
        (tap_grads, gain_in_grad, gain_mid_grad), "seq"
    )
    down_weight_grad = reduce_seq(contract_rows(out_full, hidden))
    gate_weight_grad = reduce_seq(contract_rows(normed_mid, gate_rows))
    up_weight_grad = reduce_seq(contract_rows(normed_mid, up_rows))
    out_weight_grad = reduce_seq(contract_rows(branch_full, gated))
    in_weight_grad = reduce_seq(contract_rows(normed_in, projected_grad)).reshape(
        rows_here, 3, local
    )
    rms_values = jnp.stack([rms_in, rms_mid])
    return (
        result,
        stream_grad,
        gain_in_total,
        in_weight_grad,
        conv_total,
        out_weight_grad,
        gain_mid_total,
        gate_weight_grad,
        up_weight_grad,
        down_weight_grad,
        rms_values,
    )


MESH = pl.DeviceIdType.MESH
BF = jnp.bfloat16
F32 = jnp.float32
ANY = pl.BlockSpec(memory_space=pl.ANY)
VMEM = pl.BlockSpec(memory_space=pltpu.VMEM)
OWN, MATE, NEAR, FAR = 0, 1, 2, 3


def dot(left, right):
    return jnp.dot(left, right, preferred_element_type=F32)


def remote(src, dst, send_sem, recv_sem, device):
    return pltpu.make_async_remote_copy(
        src_ref=src,
        dst_ref=dst,
        send_sem=send_sem,
        recv_sem=recv_sem,
        device_id=device,
        device_id_type=MESH,
    )


class Place:
    def __init__(self):
        self.zh, self.zl = lax.axis_index("zh"), lax.axis_index("zl")
        self.x, self.y, self.c = lax.axis_index("x"), lax.axis_index("y"), lax.axis_index("c")
        self.z = 2 * self.zh + self.zl
        self.inner = (self.z == 1) | (self.z == 2)
        self.outer = (self.z == 0) | (self.z == 3)
        self.rows = [self.z, 2 * self.zh + 1 - self.zl, 2 - self.zh, 3 - 3 * self.zh]
        self.mate = (self.zh, 1 - self.zl, self.x, self.y, self.c)
        self.mid = (1 - self.zh, 1 - self.zl, self.x, self.y, self.c)
        self.across = (self.zh, self.zl, 1 - self.x, self.y, self.c)

    def block(self, which, x):
        return self.rows[which] * 2 + x

    def enter(self, *others):
        barrier = pltpu.get_barrier_semaphore()

        def greet(device):
            pl.semaphore_signal(barrier, inc=1, device_id=device, device_id_type=MESH)

        greet(self.mate)
        greet(self.across)
        for device in others:
            greet(device)

        @pl.when(self.inner)
        def _():
            greet(self.mid)

        @pl.when(self.inner)
        def _():
            pl.semaphore_wait(barrier, 3 + len(others))

        @pl.when(self.outer)
        def _():
            pl.semaphore_wait(barrier, 2 + len(others))


def in_stages(chunks):
    stages = len(chunks[0])
    for step in range(len(chunks) + stages - 1):
        for stage in range(stages):
            if 0 <= step - stage < len(chunks):
                chunks[step - stage][stage]()


def pair_gather_chunk(p, weight, out, relay, ss, rs, first, count, rows):
    half = out.shape[1]
    here = pl.ds(first, count)
    own = weight.at[here, pl.ds(pl.multiple_of(p.zl * half, half), half)]
    other = weight.at[here, pl.ds(pl.multiple_of((1 - p.zl) * half, half), half)]

    def block(which, x):
        return out.at[pl.ds(pl.multiple_of(p.block(which, x) * rows + first, count), count), :]

    held = [relay.at[i, here, :] for i in range(3)]

    def send(slot, src, dst, recv, device):
        return remote(src, dst, ss.at[slot], rs.at[recv], device)

    def arrived(recv, dst):
        remote(dst, dst, ss.at[0], rs.at[recv], p.mate).wait_recv()

    local = pltpu.make_async_copy(own, block(OWN, p.x), ss.at[11])
    across = [
        send(7 + k, own if k == OWN else block(k, p.x), block(k, p.x), 6 + k, p.across)
        for k in range(4)
    ]
    to_mate = send(0, other, block(OWN, p.x), 0, p.mate)
    outer_own = send(1, own, held[0], 3, p.mate)
    mid_other = send(3, other, block(OWN, p.x), 1, p.mid)
    mid_own = send(4, own, held[1], 4, p.mid)
    mid_far = send(5, held[0], block(MATE, p.x), 2, p.mid)
    mid_far_own = send(6, block(MATE, p.x), held[2], 5, p.mid)
    back_near = send(1, held[1], block(NEAR, p.x), 1, p.mate)
    back_far = send(2, held[2], block(FAR, p.x), 2, p.mate)

    def begin():
        @pl.when(p.inner)
        def _():
            mid_other.start()
            mid_own.start()

        to_mate.start()

        @pl.when(p.outer)
        def _():
            outer_own.start()

        across[OWN].start()
        local.start()

    def mate_here():
        arrived(0, block(MATE, p.x))

        @pl.when(p.inner)
        def _():
            arrived(3, held[0])
            mid_far.start()
            mid_far_own.start()
            arrived(4, held[1])
            back_near.start()

        across[MATE].start()

    def near_here():
        arrived(1, block(NEAR, p.x))
        across[NEAR].start()

        @pl.when(p.inner)
        def _():
            arrived(5, held[2])
            back_far.start()

    def far_here():
        arrived(2, block(FAR, p.x))
        across[FAR].start()

    def finish():
        for k in range(4):
            arrived(6 + k, block(k, 1 - p.x))
            across[k].wait_send()
        local.wait()
        to_mate.wait_send()

        @pl.when(p.inner)
        def _():
            for copy in (mid_other, mid_own, mid_far, mid_far_own, back_near, back_far):
                copy.wait_send()

        @pl.when(p.outer)
        def _():
            outer_own.wait_send()

    return [begin, mate_here, near_here, far_here, finish]


def gather_pair(weights, collective, split=4):
    n = len(weights)
    rows, width = weights[0].shape
    half = width // 2
    count = rows // split

    def kernel(*refs):
        ins, outs = refs[:n], refs[n : 2 * n]
        relay, ss, rs = refs[2 * n :]
        p = Place()
        p.enter()
        in_stages(
            [
                pair_gather_chunk(
                    p, ins[i], outs[i], relay.at[i], ss.at[i * split + c], rs.at[i * split + c],
                    c * count, count, rows,
                )
                for i in range(n)
                for c in range(split)
            ]
        )

    return pl.pallas_call(
        kernel,
        out_shape=[jax.ShapeDtypeStruct((8 * rows, half), BF)] * n,
        in_specs=[ANY] * n,
        out_specs=[ANY] * n,
        scratch_shapes=[
            pltpu.VMEM((n, 3, rows, half), BF),
            pltpu.SemaphoreType.DMA((n * split, 12)),
            pltpu.SemaphoreType.DMA((n * split, 10)),
        ],
        compiler_params=pltpu.CompilerParams(
            collective_id=collective, has_side_effects=True, vmem_limit_bytes=32 << 20
        ),
        cost_estimate=pl.CostEstimate(flops=0, bytes_accessed=n * (100 << 20), transcendentals=0),
        name="gather_pair",
    )(*weights)


def gather_down_and_hidden(weight, normed, gate, up, collective, split=4):
    rows, width = weight.shape
    half = width // 2
    pair, owners, tokens, local = normed.shape
    count = rows // split
    tile = pair * tokens // 8

    def kernel(*refs):
        weight_ref, normed_ref, gate_ref, up_ref = refs[:4]
        down_ref, hidden_ref, silu_ref, slope_ref = refs[4:8]
        relay, x, results, ss, rs, x_sem, result_sem = refs[8:]

        def loads(m, act):
            start = m % (8 // pair) * tile
            for j in range(owners):
                copy = pltpu.make_async_copy(
                    normed_ref.at[m // (8 // pair), j, pl.ds(start, tile), :],
                    x.at[m % 2, :, pl.ds(j * local, local)],
                    x_sem.at[m % 2, j],
                )
                getattr(copy, act)()

        def stores(m, act):
            for i, ref in enumerate((hidden_ref, silu_ref, slope_ref)):
                copy = pltpu.make_async_copy(
                    results.at[m % 2, i], ref.at[pl.ds(m * tile, tile), :], result_sem.at[m % 2, i]
                )
                getattr(copy, act)()

        loads(0, "start")
        loads(1, "start")
        p = Place()
        p.enter()
        chunks = [
            pair_gather_chunk(
                p, weight_ref, down_ref, relay.at[0], ss.at[c], rs.at[c], c * count, count, rows
            )
            for c in range(split)
        ]

        def compute(m):
            loads(m, "wait")
            if m >= 2:
                stores(m - 2, "wait")
            for part in range(2):
                here = pl.ds(part * half // 2, half // 2)
                value = dot(x[m % 2], gate_ref[:, here])
                upward = dot(x[m % 2], up_ref[:, here])
                sigmoid = jax.nn.sigmoid(value)
                silu = value * sigmoid
                results[m % 2, 0, :, here] = (silu * upward).astype(BF)
                results[m % 2, 1, :, here] = silu.astype(BF)
                results[m % 2, 2, :, here] = (
                    upward * (sigmoid + silu * (1.0 - sigmoid))
                ).astype(BF)
            stores(m, "start")
            if m + 2 < 8:
                loads(m + 2, "start")

        for step in range(split + 4):
            for stage in range(5):
                if 0 <= step - stage < split:
                    chunks[step - stage][stage]()
            for m in range(step * 8 // (split + 4), (step + 1) * 8 // (split + 4)):
                compute(m)
        stores(6, "wait")
        stores(7, "wait")

    units = jax.ShapeDtypeStruct((pair * tokens, half), BF)
    return pl.pallas_call(
        kernel,
        out_shape=[jax.ShapeDtypeStruct((8 * rows, half), BF), units, units, units],
        in_specs=[ANY, ANY, VMEM, VMEM],
        out_specs=[ANY] * 4,
        scratch_shapes=[
            pltpu.VMEM((1, 3, rows, half), BF),
            pltpu.VMEM((2, tile, owners * local), BF),
            pltpu.VMEM((2, 3, tile, half), BF),
            pltpu.SemaphoreType.DMA((split, 12)),
            pltpu.SemaphoreType.DMA((split, 10)),
            pltpu.SemaphoreType.DMA((2, owners)),
            pltpu.SemaphoreType.DMA((2, 3)),
        ],
        compiler_params=pltpu.CompilerParams(
            collective_id=collective, has_side_effects=True, vmem_limit_bytes=48 << 20
        ),
        cost_estimate=pl.CostEstimate(flops=0, bytes_accessed=100 << 20, transcendentals=0),
        name="gather_down_and_hidden",
    )(weight, normed, gate, up)


def line_gather_chunk(p, weight, out, ss, rs, first, count, rows):
    own = weight.at[pl.ds(first, count), :]

    def block(which, x):
        return out.at[pl.ds(pl.multiple_of(p.block(which, x) * rows + first, count), count), :]

    def send(slot, src, dst, recv, device):
        return remote(src, dst, ss.at[slot], rs.at[recv], device)

    def arrived(recv, dst):
        remote(dst, dst, ss.at[0], rs.at[recv], p.mate).wait_recv()

    local = pltpu.make_async_copy(own, block(OWN, p.x), ss.at[9])
    across = [
        send(k, own if k == OWN else block(k, p.x), block(k, p.x), 3 + k, p.across)
        for k in range(4)
    ]
    to_mate = send(4, own, block(OWN, p.x), MATE - 1, p.mate)
    to_mid = send(5, own, block(OWN, p.x), NEAR - 1, p.mid)
    mid_far = send(6, block(MATE, p.x), block(MATE, p.x), FAR - 1, p.mid)
    back_near = send(7, block(NEAR, p.x), block(NEAR, p.x), NEAR - 1, p.mate)
    back_far = send(8, block(FAR, p.x), block(FAR, p.x), FAR - 1, p.mate)

    def begin():
        @pl.when(p.inner)
        def _():
            to_mid.start()

        to_mate.start()
        across[OWN].start()
        local.start()

    def mate_here():
        arrived(MATE - 1, block(MATE, p.x))

        @pl.when(p.inner)
        def _():
            mid_far.start()

        across[MATE].start()

    def near_here():
        arrived(NEAR - 1, block(NEAR, p.x))

        @pl.when(p.inner)
        def _():
            back_near.start()

        across[NEAR].start()

    def far_here():
        arrived(FAR - 1, block(FAR, p.x))

        @pl.when(p.inner)
        def _():
            back_far.start()

        across[FAR].start()

    def finish():
        for k in range(4):
            arrived(3 + k, block(k, 1 - p.x))
            across[k].wait_send()
        local.wait()
        to_mate.wait_send()

        @pl.when(p.inner)
        def _():
            for copy in (to_mid, mid_far, back_near, back_far):
                copy.wait_send()

    return [begin, mate_here, near_here, far_here, finish]


def gather_line(weights, collective, split=2):
    n = len(weights)
    rows = weights[0].shape[0]
    count = rows // split

    def kernel(*refs):
        ins, outs = refs[:n], refs[n : 2 * n]
        ss, rs = refs[2 * n :]
        p = Place()
        p.enter()
        in_stages(
            [
                line_gather_chunk(
                    p, ins[i], outs[i], ss.at[i * split + c], rs.at[i * split + c],
                    c * count, count, rows,
                )
                for i in range(n)
                for c in range(split)
            ]
        )

    return pl.pallas_call(
        kernel,
        out_shape=[jax.ShapeDtypeStruct((8 * rows, w.shape[1]), BF) for w in weights],
        in_specs=[ANY] * n,
        out_specs=[ANY] * n,
        scratch_shapes=[
            pltpu.SemaphoreType.DMA((n * split, 10)),
            pltpu.SemaphoreType.DMA((n * split, 7)),
        ],
        compiler_params=pltpu.CompilerParams(
            collective_id=collective, has_side_effects=True, vmem_limit_bytes=32 << 20
        ),
        cost_estimate=pl.CostEstimate(flops=0, bytes_accessed=n * (100 << 20), transcendentals=0),
        name="gather_line",
    )(*weights)


def contract_tokens(left, right):
    return lax.dot_general(left, right, (((0,), (0,)), ((), ())), preferred_element_type=F32)


class PairScatter:
    def __init__(self, p, product, sx, rx, sz, rz, rm, held, out, ss, rs):
        self.p, self.product = p, product
        self.sx, self.rx, self.sz, self.rz, self.rm = sx, rx, sz, rz, rm
        self.held, self.out, self.ss, self.rs = held, out, ss, rs
        self.half = held.shape[1]

    def across(self, k):
        return remote(self.sx.at[k], self.rx.at[k], self.ss.at[k], self.rs.at[k], self.p.across)

    def outward(self, j):
        return remote(self.sz.at[j], self.rz.at[j], self.ss.at[4 + j], self.rs.at[4 + j], self.p.mate)

    def middle(self, j):
        return remote(self.sz.at[j], self.rm.at[j], self.ss.at[7 + j], self.rs.at[7 + j], self.p.mid)

    def relay(self, j):
        return remote(
            self.rz.at[j], self.rm.at[2 + j], self.ss.at[9 + j], self.rs.at[9 + j], self.p.mid
        )

    def forward(self):
        return remote(self.rm.at[0], self.rz.at[0], self.ss.at[4], self.rs.at[4], self.p.mate)

    def back(self):
        return remote(self.sz.at[2], self.rz.at[1], self.ss.at[5], self.rs.at[5], self.p.mate)

    def cols_of(self, place):
        return pl.ds(pl.multiple_of(place * self.half, self.half), self.half)

    def send_across(self, k, *sent):
        self.sx[k] = self.product(k, 1 - self.p.x).astype(BF)
        self.sent(*sent)
        self.across(k).start()

    def summed(self, k):
        total = self.product(k, self.p.x)
        self.across(k).wait_recv()
        return total + self.rx[k].astype(F32)

    def send_on(self, k, j):
        self.sz[j] = self.summed(k).astype(BF)

        @pl.when(self.p.outer)
        def _():
            self.outward(j).start()

        @pl.when(self.p.inner)
        def _():
            self.middle(j).start()

    def send_relay(self, j):
        @pl.when(self.p.inner)
        def _():
            self.outward(j).wait_recv()
            self.relay(j).start()

    def mate_rows(self):
        total = self.summed(MATE)

        @pl.when(self.p.outer)
        def _():
            self.sz[2] = total.astype(BF)
            self.outward(2).start()

        @pl.when(self.p.inner)
        def _():
            self.held[...] = total

    def send_forward(self):
        @pl.when(self.p.inner)
        def _():
            self.middle(0).wait_recv()
            self.forward().start()

    def own_rows(self):
        self.out[:, self.cols_of(self.p.zl)] = self.summed(OWN)

    def send_back(self):
        @pl.when(self.p.inner)
        def _():
            self.relay(0).wait_recv()
            self.sz[2] = (self.held[...] + self.rm[2].astype(F32)).astype(BF)
            self.back().start()

    def finish(self):
        p, out = self.p, self.out
        here, there = self.cols_of(p.zl), self.cols_of(1 - p.zl)

        @pl.when(p.inner)
        def _():
            self.relay(1).wait_recv()
            out[:, here] = out[:, here] + self.rm[3].astype(F32)
            self.outward(2).wait_recv()
            self.middle(1).wait_recv()
            out[:, there] = self.rz[2].astype(F32) + self.rm[1].astype(F32)

        @pl.when(p.outer)
        def _():
            self.forward().wait_recv()
            out[:, here] = out[:, here] + self.rz[0].astype(F32)
            self.back().wait_recv()
            out[:, there] = self.rz[1].astype(F32)

        @pl.when(p.inner)
        def _():
            for j in range(2):
                self.relay(j).wait_send()
            self.forward().wait_send()

    def sent_on(self):
        @pl.when(self.p.outer)
        def _():
            for j in range(3):
                self.outward(j).wait_send()

        @pl.when(self.p.inner)
        def _():
            for j in range(2):
                self.middle(j).wait_send()
            self.back().wait_send()

    def sent(self, *which):
        for k in which:
            self.across(k).wait_send()


def pair_scatter_scratch(n, rows, half):
    return [
        pltpu.VMEM((4, rows, half), BF),
        pltpu.VMEM((n, 4, rows, half), BF),
        pltpu.VMEM((3, rows, half), BF),
        pltpu.VMEM((n, 3, rows, half), BF),
        pltpu.VMEM((n, 4, rows, half), BF),
        pltpu.VMEM((rows, half), F32),
        pltpu.SemaphoreType.DMA((n, 11)),
        pltpu.SemaphoreType.DMA((n, 11)),
    ]


class Columns:
    def __init__(self, p, jobs, buffer, sems):
        self.p, self.jobs, self.buffer, self.sems, self.at = p, jobs, buffer, sems, 0
        for n in range(min(2, len(jobs))):
            self.copies(n, "start")

    def copies(self, n, act):
        array, k, flip = self.jobs[n]
        pair, _, tokens, local = array.shape
        rows = self.buffer.shape[2]
        start = self.p.block(k, 1 - self.p.x if flip else self.p.x) * rows
        cols = pl.ds(pl.multiple_of(start % local, rows), rows)
        for q in range(pair):
            copy = pltpu.make_async_copy(
                array.at[q, start // local, :, cols],
                self.buffer.at[n % 2, pl.ds(q * tokens, tokens), :],
                self.sems.at[n % 2, q],
            )
            getattr(copy, act)()

    def times(self, right):
        n = self.at
        self.at += 1
        self.copies(n, "wait")
        product = contract_tokens(self.buffer[n % 2], right)
        if n + 2 < len(self.jobs):
            self.copies(n + 2, "start")
        return product


ORDER = (FAR, NEAR, MATE, OWN)


def scatter_pair(left, right, collective):
    tokens, half = right.shape
    rows = left.shape[1] * left.shape[3] // 8

    def kernel(left_ref, right_ref, out, *scratch):
        sx, rx, sz, rz, rm, held, ss, rs, cols, cols_sem = scratch
        p = Place()
        p.enter()
        feed = Columns(
            p, [(left_ref, k, flip) for flip in (True, False) for k in ORDER], cols, cols_sem
        )
        m = PairScatter(
            p, lambda k, x: feed.times(right_ref[...]), sx, rx.at[0], sz, rz.at[0], rm.at[0],
            held, out, ss.at[0], rs.at[0],
        )
        m.send_across(FAR)
        m.send_across(NEAR)
        m.send_across(MATE, FAR)
        m.send_across(OWN, NEAR)
        m.send_on(FAR, 0)
        m.send_on(NEAR, 1)
        m.send_relay(0)
        m.mate_rows()
        m.send_relay(1)
        m.send_forward()
        m.own_rows()
        m.send_back()
        m.finish()
        m.sent_on()
        m.sent(MATE, OWN)

    return pl.pallas_call(
        kernel,
        out_shape=jax.ShapeDtypeStruct((rows, 2 * half), F32),
        in_specs=[ANY, VMEM],
        out_specs=VMEM,
        scratch_shapes=pair_scatter_scratch(1, rows, half)
        + [pltpu.VMEM((2, tokens, rows), BF), pltpu.SemaphoreType.DMA((2, 2))],
        compiler_params=pltpu.CompilerParams(
            collective_id=collective, has_side_effects=True, vmem_limit_bytes=40 << 20
        ),
        cost_estimate=pl.CostEstimate(flops=0, bytes_accessed=150 << 20, transcendentals=0),
        name="scatter_pair",
    )(left, right)


def scatter_line(lefts, rights, which, collective):
    n, nx, ny = len(which), len(lefts), len(rights)
    rows = lefts[-1].shape[1] // 8
    width = min(r.shape[1] for r in rights)

    def kernel(*refs):
        left, right, out = refs[:nx], refs[nx : nx + ny], refs[nx + ny : nx + 2 * ny]
        sx, rx, sz, rz, rm, own, ss, rs = refs[nx + 2 * ny :]
        p = Place()
        p.enter()

        def product(i, k, x):
            a, b, group = which[i]
            start = p.block(k, x) * rows
            if len(left[a].shape) == 2:
                block = left[a][:, pl.ds(pl.multiple_of(start, rows), rows)]
            else:
                local = left[a].shape[2]
                block = left[a][start // local, :, pl.ds(pl.multiple_of(start % local, rows), rows)]
            return contract_tokens(block, right[b][:, group * width : (group + 1) * width])

        def across(i, k):
            return remote(sx.at[i, k], rx.at[i, k], ss.at[i, k], rs.at[i, k], p.across)

        def outward(i, j):
            return remote(sz.at[i, j], rz.at[i, j], ss.at[i, 4 + j], rs.at[i, 4 + j], p.mate)

        def middle(i, j):
            return remote(sz.at[i, j], rm.at[i, j], ss.at[i, 7 + j], rs.at[i, 7 + j], p.mid)

        def back(i):
            return remote(sz.at[i, 2], rz.at[i, 0], ss.at[i, 4], rs.at[i, 4], p.mate)

        def send_across(i):
            for k in (FAR, NEAR, MATE, OWN):
                sx[i, k] = product(i, k, 1 - p.x).astype(BF)
                across(i, k).start()

        def summed(i, k):
            total = product(i, k, p.x)
            across(i, k).wait_recv()
            return total + rx[i, k].astype(F32)

        def send_on(i, k, j):
            total = summed(i, k)

            @pl.when(p.outer)
            def _():
                sz[i, j] = total.astype(BF)
                outward(i, j).start()

            @pl.when(p.inner)
            def _():
                outward(i, j).wait_recv()
                sz[i, j] = (total + rz[i, j].astype(F32)).astype(BF)
                middle(i, j).start()

        def mate_rows(i):
            total = summed(i, MATE)

            @pl.when(p.outer)
            def _():
                sz[i, 2] = total.astype(BF)
                outward(i, 2).start()

            @pl.when(p.inner)
            def _():
                own[i, 0] = total

        def own_rows(i):
            own[i, 1] = summed(i, OWN)

        def finish(i):
            b, group = which[i][1:]
            here = pl.ds(group * width, width)

            @pl.when(p.inner)
            def _():
                middle(i, 0).wait_recv()
                sz[i, 2] = (own[i, 0] + rm[i, 0].astype(F32)).astype(BF)
                back(i).start()
                outward(i, 2).wait_recv()
                middle(i, 1).wait_recv()
                out[b][:, here] = own[i, 1] + rz[i, 2].astype(F32) + rm[i, 1].astype(F32)

            @pl.when(p.outer)
            def _():
                back(i).wait_recv()
                out[b][:, here] = own[i, 1] + rz[i, 0].astype(F32)
                for j in range(3):
                    outward(i, j).wait_send()

            for k in range(4):
                across(i, k).wait_send()

            @pl.when(p.inner)
            def _():
                for j in range(2):
                    middle(i, j).wait_send()
                back(i).wait_send()

        send_across(0)
        for i in range(n):
            if i + 1 < n:
                send_across(i + 1)
            send_on(i, FAR, 0)
            send_on(i, NEAR, 1)
            mate_rows(i)
            own_rows(i)
            if i > 0:
                finish(i - 1)
        finish(n - 1)

    return pl.pallas_call(
        kernel,
        out_shape=[jax.ShapeDtypeStruct((rows, r.shape[1]), F32) for r in rights],
        in_specs=[VMEM] * (nx + ny),
        out_specs=[VMEM] * ny,
        scratch_shapes=[
            pltpu.VMEM((n, 4, rows, width), BF),
            pltpu.VMEM((n, 4, rows, width), BF),
            pltpu.VMEM((n, 3, rows, width), BF),
            pltpu.VMEM((n, 3, rows, width), BF),
            pltpu.VMEM((n, 2, rows, width), BF),
            pltpu.VMEM((n, 2, rows, width), F32),
            pltpu.SemaphoreType.DMA((n, 9)),
            pltpu.SemaphoreType.DMA((n, 9)),
        ],
        compiler_params=pltpu.CompilerParams(
            collective_id=collective, has_side_effects=True, vmem_limit_bytes=60 << 20
        ),
        cost_estimate=pl.CostEstimate(flops=0, bytes_accessed=n * (80 << 20), transcendentals=0),
        name="scatter_line",
    )(*lefts, *rights)


class Spread:
    def __init__(self, p, view, ss, rs):
        self.p = p
        self.view, self.ss, self.rs = view, ss, rs

    def to_core(self):
        block = self.view(self.p.me)
        return remote(block, block, self.ss.at[0], self.rs.at[0], self.p.core)

    def to_side(self):
        block = self.view(self.p.me)
        return remote(block, block, self.ss.at[1], self.rs.at[1], self.p.side)

    def on_to_core(self):
        block = self.view(self.p.side_owner)
        return remote(block, block, self.ss.at[2], self.rs.at[2], self.p.core)

    def start(self):
        self.to_side().start()
        self.to_core().start()

    def forward(self):
        self.to_side().wait_recv()
        self.on_to_core().start()

    def finish(self):
        self.to_core().wait_recv()
        self.on_to_core().wait_recv()
        self.to_core().wait_send()
        self.to_side().wait_send()
        self.on_to_core().wait_send()


def lanes_of(column):
    return jnp.broadcast_to(column, (column.shape[0], 128)).T[:8]


def column_of(lanes):
    return jnp.broadcast_to(lanes[:1], (128, lanes.shape[1])).T[:, :1]


def block_forward(
    normed_here, stream, masks, conv_weight, gain, in_weight, out_weight, gate_weight, up_weight,
    down_weight, collective,
):
    tokens, local = normed_here.shape
    rows, width = gate_weight.shape
    half = width // 2
    three = in_weight.shape[1]
    owners, pair = 4, 2
    features = owners * local
    tile = tokens // 4
    plan = [("in", rows // 4)] * 4 + [("out", rows)]
    plan += [(name, rows // 4) for name in ("gate", "up", "down") for _ in range(4)]
    n_chunks = len(plan)

    def kernel(*refs):
        here_ref, stream_ref, masks_ref, conv_ref, gain_ref = refs[:5]
        in_ref, out_ref, gate_ref, up_ref, down_ref = refs[5:10]
        in_all, out_all, gate_all, up_all, down_all = refs[10:15]
        normed_all, projected_all, convolved_all, gated_all, mid_all = refs[15:20]
        hidden_all, silu_all, slope_all, middle, squares, halo = refs[20:26]
        x, in_vm, out_vm, gate_vm, up_vm, projected, mixed, convolved, gated = refs[26:35]
        to_core, sums, from_y, near_squares, mid, results, relay = refs[35:42]
        chunk_ss, chunk_rs, x_ss, x_rs, mid_ss, mid_rs, move_ss, move_rs = refs[42:50]
        square_ss, square_rs, halo_sem, store_sem, result_sem = refs[50:55]

        p = Place()
        p.core = (p.zh, p.zl, p.x, p.y, 1 - p.c)
        p.side = (p.zh, p.zl, p.x, 1 - p.y, p.c)
        diagonal = (p.zh, p.zl, p.x, 1 - p.y, 1 - p.c)
        p.me, p.side_owner = 2 * p.y + p.c, 2 * (1 - p.y) + p.c
        place = 2 * p.z + p.x
        last = 2 * 4 - 1

        def device_at(s):
            return (s // 4, s // 2 % 2, s % 2, p.y, p.c)

        following, previous = device_at(lax.rem(place + 1, 8)), device_at(lax.rem(place + 7, 8))
        local_x = pltpu.make_async_copy(here_ref, x.at[p.me], store_sem.at[0])
        local_x.start()
        p.enter(p.core, p.side, diagonal, following, previous)

        chunks = []
        firsts = {}
        targets = {
            "in": (in_ref, in_vm), "out": (out_ref, out_vm), "gate": (gate_ref, gate_vm),
            "up": (up_ref, up_vm), "down": (down_ref, down_all),
        }
        for c, (name, count) in enumerate(plan):
            first = firsts.get(name, 0)
            firsts[name] = first + count
            source, target = targets[name]
            if name in ("in", "out"):
                chunk = line_gather_chunk(
                    p, source, target, chunk_ss.at[c], chunk_rs.at[c], first, count, rows
                )
            else:
                held = relay.at[("gate", "up", "down").index(name)]
                chunk = pair_gather_chunk(
                    p, source, target, held, chunk_ss.at[c], chunk_rs.at[c], first, count, rows
                )
            chunks.append(chunk)

        def pump(step):
            for stage in range(5):
                if 0 <= step - stage < n_chunks:
                    chunks[step - stage][stage]()

        stores = []

        def store(source, target):
            copy = pltpu.make_async_copy(source, target, store_sem.at[1 + len(stores)])
            copy.start()
            stores.append(copy)

        spread_x = Spread(p, lambda owner: x.at[owner], x_ss, x_rs)

        def project(t):
            here = pl.ds(t * tile, tile)
            value = sum(
                dot(x[j, here, :], in_vm[j * local : (j + 1) * local, :]) for j in range(owners)
            )
            projected[here, :] = value
            mixed[pl.ds(8 + t * tile, tile), :] = value[:, :local] * value[:, 2 * local :]

        def halo_copy():
            return remote(
                mixed.at[pl.ds(tokens, 8), :], halo, halo_sem.at[0], halo_sem.at[1], following
            )

        def send_halo():
            @pl.when(place < last)
            def _():
                halo_copy().start()

        def take_halo():
            @pl.when(place > 0)
            def _():
                halo_copy().wait_recv()

            @pl.when(place == 0)
            def _():
                halo[...] = jnp.zeros_like(halo)

            mixed[:8, :] = halo[...]

        def convolve(t):
            here = pl.ds(t * tile, tile)
            value = (
                conv_ref[0:1, :] * mixed[pl.ds(8 + t * tile, tile), :]
                + masks_ref[0, here, :] * conv_ref[1:2, :] * mixed[pl.ds(7 + t * tile, tile), :]
                + masks_ref[1, here, :] * conv_ref[2:3, :] * mixed[pl.ds(6 + t * tile, tile), :]
            )
            convolved[here, :] = value
            gated[here, :] = (projected[here, local : 2 * local] * value).astype(BF)

        owner = [
            2 * (1 - p.y) + 1 - p.c, 2 * (1 - p.y) + p.c, 2 * p.y + 1 - p.c, 2 * p.y + p.c
        ]

        def core_copy(b, t):
            return remote(
                to_core.at[b, t], sums.at[b, t], move_ss.at[b, t], move_rs.at[b, t], p.core
            )

        def side_copy(t):
            return remote(sums.at[0, t], from_y.at[t], move_ss.at[2, t], move_rs.at[2, t], p.side)

        def mixer_out(n):
            out_rows = pl.ds(pl.multiple_of(owner[n] * local, local), local)
            for t in range(4):
                here = pl.ds(t * tile, tile)
                value = contract_cols(gated[here, :], out_vm[out_rows, :])
                b = n // 2
                if n % 2 == 0:
                    to_core[b, t] = value.astype(BF)
                    core_copy(b, t).start()
                else:
                    core_copy(b, t).wait_recv()
                    value = value + sums[b, t].astype(F32)
                    if b == 0:
                        sums[b, t] = value.astype(BF)
                        side_copy(t).start()
                    else:
                        middle[here, :] = stream_ref[here, :] + value

        def residual(t):
            here = pl.ds(t * tile, tile)
            side_copy(t).wait_recv()
            value = middle[here, :] + from_y[t].astype(F32)
            middle[here, :] = value
            squares[:, here] = lanes_of(jnp.sum(value * value, axis=1, keepdims=True))

        def square_copies():
            return [
                remote(
                    squares, near_squares.at[i], square_ss.at[i], square_rs.at[i], device
                )
                for i, device in enumerate((p.core, p.side, diagonal))
            ]

        def sum_squares():
            for copy in square_copies():
                copy.wait_recv()
                copy.wait_send()
            squares[...] = (
                squares[...] + near_squares[0] + near_squares[1] + near_squares[2]
            )

        def own_tile(t):
            return lambda who: mid.at[p.zl, who, pl.ds(t * tile, tile), :]

        def mate_tile(t):
            return lambda who: mid.at[1 - p.zl, who, pl.ds(t * tile, tile), :]

        spread_own = [Spread(p, own_tile(t), mid_ss.at[0, t], mid_rs.at[0, t]) for t in range(4)]
        spread_mate = [Spread(p, mate_tile(t), mid_ss.at[1, t], mid_rs.at[1, t]) for t in range(4)]

        def mate_send(t):
            block = own_tile(t)(p.me)
            return remote(block, block, mid_ss.at[0, t, 3], mid_rs.at[0, t, 3], p.mate)

        def normalize_mid(t):
            here = pl.ds(t * tile, tile)
            inverse = lax.rsqrt(squares[:, here] / features + epsilon)
            value = middle[here, :] * column_of(inverse) * gain_ref[...]
            mid[p.zl, p.me, here, :] = value.astype(BF)
            mate_send(t).start()
            spread_own[t].start()

        def pass_on(t):
            spread_own[t].forward()
            mate_send(t).wait_recv()
            spread_mate[t].start()

        def result_stores(m, act):
            start = pl.multiple_of(tile_place(m) * tile, tile)
            for i, ref in enumerate((hidden_all, silu_all, slope_all)):
                copy = pltpu.make_async_copy(
                    results.at[m % 2, i], ref.at[pl.ds(start, tile), :], result_sem.at[m % 2, i]
                )
                getattr(copy, act)()

        def tile_place(m):
            return (p.zl if m < 4 else 1 - p.zl) * 4 + m % 4

        def hidden_units(m):
            q = p.zl if m < 4 else 1 - p.zl
            here = pl.ds(m % 4 * tile, tile)
            (spread_own if m < 4 else spread_mate)[m % 4].finish()
            if m >= 2:
                result_stores(m - 2, "wait")
            for part in range(2):
                cols = pl.ds(part * half // 2, half // 2)
                value = sum(
                    dot(mid[q, j, here, :], gate_vm[j * local : (j + 1) * local, cols])
                    for j in range(owners)
                )
                upward = sum(
                    dot(mid[q, j, here, :], up_vm[j * local : (j + 1) * local, cols])
                    for j in range(owners)
                )
                sigmoid = jax.nn.sigmoid(value)
                silu = value * sigmoid
                results[m % 2, 0, :, cols] = (silu * upward).astype(BF)
                results[m % 2, 1, :, cols] = silu.astype(BF)
                results[m % 2, 2, :, cols] = (upward * (sigmoid + silu * (1.0 - sigmoid))).astype(BF)
            result_stores(m, "start")

        pump(0)
        local_x.wait()
        spread_x.start()
        pump(1)
        pump(2)
        spread_x.forward()
        pump(3)
        pump(4)
        pump(5)
        spread_x.finish()
        pump(6)
        pump(7)
        store(x, normed_all)
        store(in_vm, in_all)
        project(3)
        send_halo()
        project(2)
        pump(8)
        project(1)
        project(0)
        store(projected, projected_all)
        store(out_vm, out_all)
        pump(9)
        take_halo()
        for t in range(4):
            convolve(t)
        store(convolved, convolved_all)
        store(gated, gated_all)
        mixer_out(0)
        mixer_out(1)
        pump(10)
        mixer_out(2)
        mixer_out(3)
        pump(11)
        residual(0)
        residual(1)
        pump(12)
        store(gate_vm, gate_all)
        residual(2)
        residual(3)
        for copy in square_copies():
            copy.start()
        pump(13)
        sum_squares()
        for t in range(4):
            normalize_mid(t)
        pump(14)
        pass_on(0)
        pass_on(1)
        pump(15)
        pass_on(2)
        pass_on(3)
        pump(16)
        store(up_vm, up_all)
        for t in range(4):
            spread_mate[t].forward()
        hidden_units(0)
        hidden_units(1)
        pump(17)
        hidden_units(2)
        hidden_units(3)
        pump(18)
        hidden_units(4)
        hidden_units(5)
        pump(19)
        hidden_units(6)
        hidden_units(7)
        store(mid, mid_all)
        pump(20)
        result_stores(6, "wait")
        result_stores(7, "wait")
        for copy in stores:
            copy.wait()
        for t in range(4):
            core_copy(0, t).wait_send()
            core_copy(1, t).wait_send()
            side_copy(t).wait_send()
            mate_send(t).wait_send()

        @pl.when(place < last)
        def _():
            halo_copy().wait_send()

    def array(*shape, dtype=BF):
        return jax.ShapeDtypeStruct(shape, dtype)

    units = array(pair * tokens, half)
    outs = [
        (array(8 * rows, three), ANY), (array(8 * rows, local), ANY),
        (array(8 * rows, half), ANY), (array(8 * rows, half), ANY), (array(8 * rows, half), ANY),
        (array(owners, tokens, local), ANY), (array(tokens, three, dtype=F32), ANY),
        (array(tokens, local, dtype=F32), ANY), (array(tokens, local), ANY),
        (array(pair, owners, tokens, local), ANY),
        (units, ANY), (units, ANY), (units, ANY),
        (array(tokens, local, dtype=F32), VMEM), (array(8, tokens, dtype=F32), VMEM),
        (array(8, local, dtype=F32), VMEM),
    ]
    return pl.pallas_call(
        kernel,
        out_shape=[o[0] for o in outs],
        in_specs=[ANY, VMEM, VMEM, VMEM, VMEM] + [ANY] * 5,
        out_specs=[o[1] for o in outs],
        scratch_shapes=[
            pltpu.VMEM((owners, tokens, local), BF),
            pltpu.VMEM((8 * rows, three), BF),
            pltpu.VMEM((8 * rows, local), BF),
            pltpu.VMEM((8 * rows, half), BF),
            pltpu.VMEM((8 * rows, half), BF),
            pltpu.VMEM((tokens, three), F32),
            pltpu.VMEM((8 + tokens, local), F32),
            pltpu.VMEM((tokens, local), F32),
            pltpu.VMEM((tokens, local), BF),
            pltpu.VMEM((2, 4, tile, local), BF),
            pltpu.VMEM((2, 4, tile, local), BF),
            pltpu.VMEM((4, tile, local), BF),
            pltpu.VMEM((3, 8, tokens), F32),
            pltpu.VMEM((pair, owners, tokens, local), BF),
            pltpu.VMEM((2, 3, tile, half), BF),
            pltpu.VMEM((3, 3, rows, half), BF),
            pltpu.SemaphoreType.DMA((n_chunks, 12)),
            pltpu.SemaphoreType.DMA((n_chunks, 10)),
            pltpu.SemaphoreType.DMA((3,)),
            pltpu.SemaphoreType.DMA((3,)),
            pltpu.SemaphoreType.DMA((2, 4, 4)),
            pltpu.SemaphoreType.DMA((2, 4, 4)),
            pltpu.SemaphoreType.DMA((3, 4)),
            pltpu.SemaphoreType.DMA((3, 4)),
            pltpu.SemaphoreType.DMA((3,)),
            pltpu.SemaphoreType.DMA((3,)),
            pltpu.SemaphoreType.DMA((2,)),
            pltpu.SemaphoreType.DMA((12,)),
            pltpu.SemaphoreType.DMA((2, 3)),
        ],
        compiler_params=pltpu.CompilerParams(
            collective_id=collective, has_side_effects=True, vmem_limit_bytes=62 << 20
        ),
        cost_estimate=pl.CostEstimate(flops=0, bytes_accessed=600 << 20, transcendentals=0),
        name="block_forward",
    )(
        normed_here, stream, masks, conv_weight, gain, in_weight, out_weight, gate_weight, up_weight,
        down_weight,
    )


def feed_forward_backward(out_rows, normed, hidden, silu, slope, gate, up, down, collective):
    pair, owners, tokens, local = normed.shape
    total, half = hidden.shape
    rows = owners * local // 8
    tile = total // 8
    piece = total // 4

    def kernel(*refs):
        out_ref, normed_ref, hidden_ref, silu_ref, slope_ref, gate_ref, up_ref, down_ref = refs[:8]
        normed_grad, down_grad, gate_grad, up_rows = refs[8:12]
        gate_rows, weights, cols, outs, factors, to_core, sums, from_y, from_mate = refs[12:21]
        cols_sem, outs_sem, factors_sem, weights_sem, move_ss, move_rs = refs[21:27]
        sx, rx, sz, rz, rm, held, ss, rs = refs[27:]
        p = Place()
        core = (p.zh, p.zl, p.x, p.y, 1 - p.c)
        side = (p.zh, p.zl, p.x, 1 - p.y, p.c)

        down_load = pltpu.make_async_copy(down_ref, weights, weights_sem.at[0])
        down_load.start()

        def tile_loads(m, act):
            start = m % (8 // pair) * tile
            for j in range(owners):
                copy = pltpu.make_async_copy(
                    out_ref.at[m // (8 // pair), j, pl.ds(start, tile), :],
                    outs.at[m % 2, :, pl.ds(j * local, local)],
                    outs_sem.at[m % 2, j],
                )
                getattr(copy, act)()
            for i, ref in enumerate((silu_ref, slope_ref)):
                copy = pltpu.make_async_copy(
                    ref.at[pl.ds(m * tile, tile), :], factors.at[m % 2, i], factors_sem.at[m % 2, i]
                )
                getattr(copy, act)()

        D = (out_ref, normed_ref)
        jobs = [(D[0], k, True) for k in ORDER] + [(D[0], FAR, False), (D[0], NEAR, False)]
        jobs += [(D[1], FAR, True), (D[1], NEAR, True), (D[0], MATE, False), (D[0], OWN, False)]
        jobs += [(D[1], MATE, True), (D[1], OWN, True)]
        jobs += [(D[1], k, False) for k in ORDER]
        feed = Columns(p, jobs, cols, cols_sem)
        tile_loads(0, "start")
        tile_loads(1, "start")
        p.enter(core, side)

        dm = PairScatter(
            p, lambda k, x: feed.times(hidden_ref[...]), sx, rx.at[0], sz, rz.at[0],
            rm.at[0], held, down_grad, ss.at[0], rs.at[0],
        )
        gm = PairScatter(
            p, lambda k, x: feed.times(gate_rows[...]), sx, rx.at[1], sz, rz.at[1],
            rm.at[1], held, gate_grad, ss.at[1], rs.at[1],
        )

        def rows_backward(m):
            tile_loads(m, "wait")
            here = pl.ds(m * tile, tile)
            hidden_grad = dot(outs[m % 2], weights[...])
            up_rows[here, :] = (hidden_grad * factors[m % 2, 0].astype(F32)).astype(BF)
            gate_rows[here, :] = (hidden_grad * factors[m % 2, 1].astype(F32)).astype(BF)
            if m + 2 < 8:
                tile_loads(m + 2, "start")

        owner = [
            2 * (1 - p.y) + 1 - p.c, 2 * (1 - p.y) + p.c, 2 * p.y + 1 - p.c, 2 * p.y + p.c
        ]

        def weight_loads(n, act):
            start = pl.multiple_of(owner[n] * local, local)
            for i, ref in enumerate((gate_ref, up_ref)):
                copy = pltpu.make_async_copy(
                    ref.at[pl.ds(start, local), :],
                    weights.at[pl.ds((n % 2 * 2 + i) * local, local), :],
                    weights_sem.at[1 + n % 2 * 2 + i],
                )
                getattr(copy, act)()

        def piece_rows(t):
            place = p.zl if t >= 2 else 1 - p.zl
            return pl.ds(pl.multiple_of(place * tokens + t % 2 * piece, piece), piece)

        def core_copy(b, t):
            return remote(
                to_core.at[b, t], sums.at[b, t], move_ss.at[b, t], move_rs.at[b, t], core
            )

        def side_copy(t):
            return remote(sums.at[0, t], from_y.at[t], move_ss.at[2, t], move_rs.at[2, t], side)

        def mate_copy(t):
            return remote(sums.at[1, t], from_mate.at[t], move_ss.at[3, t], move_rs.at[3, t], p.mate)

        def partial_sum(n, t):
            here = piece_rows(t)
            first = n % 2 * 2 * local
            return contract_cols(gate_rows[here, :], weights[first : first + local, :]) + contract_cols(
                up_rows[here, :], weights[first + local : first + 2 * local, :]
            )

        def partial_block(n):
            weight_loads(n, "wait")
            for t in range(4):
                value = partial_sum(n, t)
                b = n // 2
                if n % 2 == 0:
                    to_core[b, t] = value.astype(BF)
                    core_copy(b, t).start()
                else:
                    core_copy(b, t).wait_recv()
                    sums[b, t] = (value + sums[b, t].astype(F32)).astype(BF)
                    if b == 0 and t < 2:
                        side_copy(t).start()
            if n + 2 < 4:
                weight_loads(n + 2, "start")

        def side_next():
            for t in range(2):
                side_copy(t).wait_send()
                side_copy(t + 2).start()

        def to_mate(t):
            side_copy(t).wait_recv()
            sums[1, t] = (sums[1, t].astype(F32) + from_y[t].astype(F32)).astype(BF)
            mate_copy(t).start()

        def final(t):
            side_copy(t).wait_recv()
            mate_copy(t - 2).wait_recv()
            normed_grad[pl.ds((t - 2) * piece, piece), :] = (
                sums[1, t].astype(F32) + from_y[t].astype(F32) + from_mate[t - 2].astype(F32)
            )

        dm.send_across(FAR)
        dm.send_across(NEAR)
        down_load.wait()
        for m in range(8):
            rows_backward(m)
        weight_loads(0, "start")
        weight_loads(1, "start")
        dm.send_across(MATE, FAR)
        dm.send_across(OWN, NEAR)
        dm.send_on(FAR, 0)
        dm.send_on(NEAR, 1)
        partial_block(0)
        partial_block(1)
        dm.send_relay(0)
        partial_block(2)
        dm.sent(MATE)
        gm.send_across(FAR)
        dm.sent(OWN)
        gm.send_across(NEAR)
        dm.mate_rows()
        dm.send_relay(1)
        dm.send_forward()
        dm.own_rows()
        partial_block(3)
        side_next()
        dm.send_back()
        to_mate(0)
        gm.send_across(MATE, FAR)
        gm.send_across(OWN, NEAR)
        to_mate(1)
        dm.sent_on()
        gm.send_on(FAR, 0)
        gm.send_on(NEAR, 1)
        gm.send_relay(0)
        final(2)
        final(3)
        gm.mate_rows()
        gm.send_relay(1)
        gm.send_forward()
        gm.own_rows()
        gm.send_back()
        dm.finish()
        gm.finish()
        gm.sent_on()
        gm.sent(MATE, OWN)
        for t in range(4):
            core_copy(0, t).wait_send()
            core_copy(1, t).wait_send()
        for t in range(2):
            side_copy(t + 2).wait_send()
            mate_copy(t).wait_send()

    grad = jax.ShapeDtypeStruct((rows, 2 * half), F32)
    return pl.pallas_call(
        kernel,
        out_shape=[
            jax.ShapeDtypeStruct((tokens, local), F32),
            grad,
            grad,
            jax.ShapeDtypeStruct((total, half), BF),
        ],
        in_specs=[ANY, ANY, VMEM, ANY, ANY, ANY, ANY, ANY],
        out_specs=[VMEM] * 4,
        scratch_shapes=[
            pltpu.VMEM((total, half), BF),
            pltpu.VMEM((owners * local, half), BF),
            pltpu.VMEM((2, total, rows), BF),
            pltpu.VMEM((2, tile, owners * local), BF),
            pltpu.VMEM((2, 2, tile, half), BF),
            pltpu.VMEM((2, 4, piece, local), BF),
            pltpu.VMEM((2, 4, piece, local), BF),
            pltpu.VMEM((4, piece, local), BF),
            pltpu.VMEM((2, piece, local), BF),
            pltpu.SemaphoreType.DMA((2, pair)),
            pltpu.SemaphoreType.DMA((2, owners)),
            pltpu.SemaphoreType.DMA((2, 2)),
            pltpu.SemaphoreType.DMA((5,)),
            pltpu.SemaphoreType.DMA((4, 4)),
            pltpu.SemaphoreType.DMA((4, 4)),
        ]
        + pair_scatter_scratch(2, rows, half),
        compiler_params=pltpu.CompilerParams(
            collective_id=collective, has_side_effects=True, vmem_limit_bytes=62 << 20
        ),
        cost_estimate=pl.CostEstimate(flops=0, bytes_accessed=300 << 20, transcendentals=0),
        name="feed_forward_backward",
    )(out_rows, normed, hidden, silu, slope, gate, up, down)


SEQ = ("zh", "zl", "x")
TP = ("y", "c")
PAIR = ("zl", "y", "c")


def after(value, *others):
    return lax.optimization_barrier((value, *others))[0]


def gather_pair_rows(rows):
    blocks = lax.all_gather(rows, PAIR, axis=0)
    return blocks.reshape(lax.axis_size("zl"), lax.axis_size(TP), *rows.shape)


def reduce_pair_product(left, right):
    pair, parts = lax.axis_size("zl"), lax.axis_size(TP)
    tokens, local = left.shape[0] // pair, right.shape[0] // parts
    blocks = jnp.concatenate(
        [
            contract_cols(
                left[q * tokens : (q + 1) * tokens], right[j * local : (j + 1) * local]
            ).astype(BF)
            for q in range(pair)
            for j in range(parts)
        ]
    )
    return lax.psum_scatter(blocks, PAIR, scatter_dimension=0, tiled=True).astype(F32)


def reduce_features(partial_rows):
    return lax.psum_scatter(
        partial_rows.astype(BF), TP, scatter_dimension=1, tiled=True
    ).astype(F32)


def rms_scale(values, gain):
    width = gain.shape[0] * lax.axis_size(TP)
    squares = lax.psum(jnp.sum(values * values, axis=1, keepdims=True), TP)
    inverse = lax.rsqrt(squares / width + epsilon)
    return (values * inverse * gain).astype(BF), inverse, jnp.sqrt(squares[:, 0] / width + epsilon)


def scale_backward(values, gain, inverse, grad_rows):
    width = gain.shape[0] * lax.axis_size(TP)
    gained = gain * grad_rows
    total = lax.psum(jnp.sum(values * gained, axis=1, keepdims=True), TP)
    grad_values = inverse * gained - values * inverse**3 * (total / width)
    return grad_values, jnp.sum(grad_rows * values * inverse, axis=0)


def paired_on_device(
    stream,
    norm1_gain,
    in_weight,
    conv_weight,
    out_weight,
    norm2_gain,
    gate_weight,
    up_weight,
    down_weight,
    doc_starts,
    out_grad,
):
    tokens, local = stream.shape
    rows_here = in_weight.shape[0]
    positions = lax.axis_index(SEQ) * tokens + jnp.arange(tokens, dtype=jnp.int32)
    mask_one, mask_two = lag_masks(doc_starts, positions)
    normed_here, inverse_in, rms_in = rms_scale(stream, norm1_gain)
    (
        in_matrix, whole_out, whole_gate, whole_up, whole_down, normed_in, projected, convolved, gated,
        normed_mid, hidden, silu, slope, middle, squares, halo,
    ) = block_forward(
        normed_here,
        stream,
        jnp.stack([mask_one, mask_two]),
        conv_weight,
        norm2_gain[None],
        in_weight.reshape(rows_here, 3 * local),
        out_weight,
        gate_weight,
        up_weight,
        down_weight,
        0,
    )
    out_full = gather_pair_rows(after(out_grad.astype(BF), normed_here))
    mean_square = squares[0] / (local * lax.axis_size(TP)) + epsilon
    rms_mid, inverse_mid = jnp.sqrt(mean_square), lax.rsqrt(mean_square)[:, None]
    in_gate = projected[:, :local]
    out_gate = projected[:, local : 2 * local]
    carried = projected[:, 2 * local :]
    mixed = in_gate * carried
    extended = jnp.concatenate([halo[-2:], mixed], axis=0)
    result = middle + reduce_pair_product(hidden, whole_down)
    normed_mid_grad, down_weight_grad, gate_weight_grad, up_rows = feed_forward_backward(
        out_full, normed_mid, hidden, silu, slope, whole_gate, whole_up, whole_down, 4
    )
    middle_norm_grad, gain_mid_grad = scale_backward(
        middle, norm2_gain, inverse_mid, normed_mid_grad
    )
    middle_grad = out_grad + middle_norm_grad
    branch_here = middle_grad.astype(BF)
    branch_full = lax.all_gather(branch_here, TP, axis=1, tiled=True)
    up_weight_grad = scatter_pair(normed_mid, after(up_rows, branch_here), 5)
    branch_full = after(branch_full, up_weight_grad)
    gated_grad = dot(branch_full, whole_out)
    out_gate_grad = gated_grad * convolved
    conv_grad = gated_grad * out_gate
    lag_one = mask_one * conv_grad
    lag_two = mask_two * conv_grad
    next_one, next_two = from_behind((lag_one[:2], lag_two[:2]), SEQ, -1)
    after_one = jnp.concatenate([lag_one, next_one], axis=0)
    after_two = jnp.concatenate([lag_two, next_two], axis=0)
    mixed_grad = (
        conv_weight[0] * conv_grad
        + conv_weight[1] * after_one[1 : tokens + 1]
        + conv_weight[2] * after_two[2:]
    )
    tap_grads = jnp.stack(
        [
            jnp.sum(conv_grad * mixed, axis=0),
            jnp.sum(lag_one * extended[1:-1], axis=0),
            jnp.sum(lag_two * extended[:-2], axis=0),
        ]
    )
    projected_grad = jnp.concatenate(
        [mixed_grad * carried, out_gate_grad, mixed_grad * in_gate], axis=1
    ).astype(BF)
    in_partial = contract_cols(projected_grad, in_matrix).astype(BF)
    normed_in_grad = reduce_features(in_partial)
    out_weight_grad, in_weight_grad = scatter_line(
        [normed_in, branch_full],
        [after(gated, in_partial), projected_grad],
        [(1, 0, 0), (0, 1, 0), (0, 1, 1), (0, 1, 2)],
        6,
    )
    normed_in_grad = after(normed_in_grad, in_weight_grad)
    stream_norm_grad, gain_in_grad = scale_backward(stream, norm1_gain, inverse_in, normed_in_grad)
    stream_grad = middle_grad + stream_norm_grad
    conv_total, gain_in_total, gain_mid_total = lax.psum(
        (tap_grads, gain_in_grad, gain_mid_grad), SEQ
    )
    return (
        result,
        stream_grad,
        gain_in_total,
        in_weight_grad.reshape(rows_here, 3, local),
        conv_total,
        out_weight_grad,
        gain_mid_total,
        gate_weight_grad,
        up_weight_grad,
        down_weight_grad,
        jnp.stack([rms_in, rms_mid]),
    )


def solution(mesh):
    seq, tp = mesh.shape["seq"], mesh.shape["tp"]
    if (seq, tp) == (8, 4):
        shape, names = (2, 2, 2, 2, 2), ("zh", "zl", "x", "y", "c")
        mesh = Mesh(mesh.devices.reshape(shape), names)
        body, rows, cols = paired_on_device, SEQ, TP
    else:
        body, rows, cols = on_device, "seq", "tp"
    return jax.shard_map(
        body,
        mesh=mesh,
        in_specs=(
            P(rows, cols),
            P(cols),
            P(rows, None, cols),
            P(None, cols),
            P(rows, cols),
            P(cols),
            P(rows, cols),
            P(rows, cols),
            P(rows, cols),
            P(),
            P(rows, cols),
        ),
        out_specs=(
            P(rows, cols),
            P(rows, cols),
            P(cols),
            P(rows, None, cols),
            P(None, cols),
            P(rows, cols),
            P(cols),
            P(rows, cols),
            P(rows, cols),
            P(rows, cols),
            P(None, rows),
        ),
        check_vma=False,
    )
```

```python
import jax
import jax.numpy as jnp
from jax import lax
from jax.experimental import pallas as pl
from jax.experimental.pallas import tpu as pltpu
from jax.sharding import Mesh, PartitionSpec as P

epsilon = 1e-05


def from_behind(shard, axis, by):
    count = lax.axis_size(axis)
    pairs = [(i, i + by) for i in range(count) if 0 <= i + by < count]
    return lax.ppermute(shard, axis, pairs)


def doc_count(doc_starts, positions):
    return jnp.sum((doc_starts[None, :] <= positions[:, None]).astype(jnp.int32), axis=1)


def lag_masks(doc_starts, positions):
    current = doc_count(doc_starts, positions)
    one = (positions >= 1) & (doc_count(doc_starts, positions - 1) == current)
    two = (positions >= 2) & (doc_count(doc_starts, positions - 2) == current)
    return (one.astype(jnp.float32)[:, None], two.astype(jnp.float32)[:, None])


def contract_rows(left, right):
    return lax.dot_general(
        left, right, (((0,), (0,)), ((), ())), preferred_element_type=jnp.float32
    )


def contract_cols(left, right):
    return lax.dot_general(
        left, right, (((1,), (1,)), ((), ())), preferred_element_type=jnp.float32
    )


def reduce_tp(partial_rows):
    return lax.psum_scatter(
        partial_rows.astype(jnp.bfloat16), "tp", scatter_dimension=1, tiled=True
    ).astype(jnp.float32)


def reduce_seq(partial_grad):
    return lax.psum_scatter(
        partial_grad.astype(jnp.bfloat16), "seq", scatter_dimension=0, tiled=True
    ).astype(jnp.float32)


def gather_grads(grad_rows):
    return lax.all_gather(grad_rows, "tp", axis=1, tiled=True)


def normalize(values, gain):
    width = gain.shape[0] * lax.axis_size("tp")
    squares = lax.psum(jnp.sum(values * values, axis=1, keepdims=True), "tp")
    inverse = lax.rsqrt(squares / width + epsilon)
    normed = lax.all_gather(
        (values * inverse * gain).astype(jnp.bfloat16), "tp", axis=1, tiled=True
    )
    return (normed, inverse, jnp.sqrt(squares[:, 0] / width + epsilon))


def norm_backward(values, gain, inverse, grad_rows):
    width = gain.shape[0] * lax.axis_size("tp")
    gained = gain * grad_rows
    total = lax.psum(jnp.sum(values * gained, axis=1, keepdims=True), "tp")
    grad_values = inverse * gained - values * inverse**3 * (total / width)
    grad_gain = jnp.sum(grad_rows * values * inverse, axis=0)
    return (grad_values, grad_gain)


def on_device(
    stream,
    norm1_gain,
    in_weight,
    conv_weight,
    out_weight,
    norm2_gain,
    gate_weight,
    up_weight,
    down_weight,
    doc_starts,
    out_grad,
):
    tokens = stream.shape[0]
    local = stream.shape[1]
    rows_here = in_weight.shape[0]
    whole_in, whole_out, whole_gate, whole_up, whole_down = (
        lax.all_gather(in_weight, "seq", axis=0, tiled=True),
        lax.all_gather(out_weight, "seq", axis=0, tiled=True),
        lax.all_gather(gate_weight, "seq", axis=0, tiled=True),
        lax.all_gather(up_weight, "seq", axis=0, tiled=True),
        lax.all_gather(down_weight, "seq", axis=0, tiled=True),
    )
    width = whole_out.shape[0]
    in_matrix = whole_in.reshape(width, 3 * local)
    positions = lax.axis_index("seq") * tokens + jnp.arange(tokens, dtype=jnp.int32)
    mask_one, mask_two = lag_masks(doc_starts, positions)
    normed_in, inverse_in, rms_in = normalize(stream, norm1_gain)
    projected = jnp.dot(normed_in, in_matrix, preferred_element_type=jnp.float32)
    in_gate = projected[:, :local]
    out_gate = projected[:, local : 2 * local]
    carried = projected[:, 2 * local :]
    mixed = in_gate * carried
    previous = from_behind(mixed[-2:], "seq", 1)
    extended = jnp.concatenate([previous, mixed], axis=0)
    convolved = (
        conv_weight[0] * mixed
        + mask_one * conv_weight[1] * extended[1:-1]
        + mask_two * conv_weight[2] * extended[:-2]
    )
    gated = (out_gate * convolved).astype(jnp.bfloat16)
    middle = stream + reduce_tp(contract_cols(gated, whole_out))
    normed_mid, inverse_mid, rms_mid = normalize(middle, norm2_gain)
    gate = jnp.dot(normed_mid, whole_gate, preferred_element_type=jnp.float32)
    upward = jnp.dot(normed_mid, whole_up, preferred_element_type=jnp.float32)
    hidden = (jax.nn.silu(gate) * upward).astype(jnp.bfloat16)
    result = middle + reduce_tp(contract_cols(hidden, whole_down))
    out_full = gather_grads(out_grad.astype(jnp.bfloat16))
    hidden_grad = jnp.dot(out_full, whole_down, preferred_element_type=jnp.float32)
    sigmoid_gate = jax.nn.sigmoid(gate)
    gate_rows = (hidden_grad * upward * sigmoid_gate * (1.0 + gate * (1.0 - sigmoid_gate))).astype(
        jnp.bfloat16
    )
    up_rows = (hidden_grad * gate * sigmoid_gate).astype(jnp.bfloat16)
    normed_mid_grad = reduce_tp(
        contract_cols(gate_rows, whole_gate) + contract_cols(up_rows, whole_up)
    )
    middle_norm_grad, gain_mid_grad = norm_backward(
        middle, norm2_gain, inverse_mid, normed_mid_grad
    )
    middle_grad = out_grad + middle_norm_grad
    branch_full = gather_grads(middle_grad.astype(jnp.bfloat16))
    gated_grad = jnp.dot(branch_full, whole_out, preferred_element_type=jnp.float32)
    out_gate_grad = gated_grad * convolved
    conv_grad = gated_grad * out_gate
    lag_one = mask_one * conv_grad
    lag_two = mask_two * conv_grad
    next_one, next_two = from_behind((lag_one[:2], lag_two[:2]), "seq", -1)
    after_one = jnp.concatenate([lag_one, next_one], axis=0)
    after_two = jnp.concatenate([lag_two, next_two], axis=0)
    mixed_grad = (
        conv_weight[0] * conv_grad
        + conv_weight[1] * after_one[1 : tokens + 1]
        + conv_weight[2] * after_two[2:]
    )
    tap_grads = jnp.stack(
        [
            jnp.sum(conv_grad * mixed, axis=0),
            jnp.sum(lag_one * extended[1:-1], axis=0),
            jnp.sum(lag_two * extended[:-2], axis=0),
        ]
    )
    projected_grad = jnp.concatenate(
        [mixed_grad * carried, out_gate_grad, mixed_grad * in_gate], axis=1
    ).astype(jnp.bfloat16)
    normed_in_grad = reduce_tp(contract_cols(projected_grad, in_matrix))
    stream_norm_grad, gain_in_grad = norm_backward(stream, norm1_gain, inverse_in, normed_in_grad)
    stream_grad = middle_grad + stream_norm_grad
    conv_total, gain_in_total, gain_mid_total = lax.psum(
        (tap_grads, gain_in_grad, gain_mid_grad), "seq"
    )
    down_weight_grad = reduce_seq(contract_rows(out_full, hidden))
    gate_weight_grad = reduce_seq(contract_rows(normed_mid, gate_rows))
    up_weight_grad = reduce_seq(contract_rows(normed_mid, up_rows))
    out_weight_grad = reduce_seq(contract_rows(branch_full, gated))
    in_weight_grad = reduce_seq(contract_rows(normed_in, projected_grad)).reshape(
        rows_here, 3, local
    )
    rms_values = jnp.stack([rms_in, rms_mid])
    return (
        result,
        stream_grad,
        gain_in_total,
        in_weight_grad,
        conv_total,
        out_weight_grad,
        gain_mid_total,
        gate_weight_grad,
        up_weight_grad,
        down_weight_grad,
        rms_values,
    )


MESH = pl.DeviceIdType.MESH
BF = jnp.bfloat16
F32 = jnp.float32
ANY = pl.BlockSpec(memory_space=pl.ANY)
VMEM = pl.BlockSpec(memory_space=pltpu.VMEM)
OWN, MATE, NEAR, FAR = 0, 1, 2, 3


def dot(left, right):
    return jnp.dot(left, right, preferred_element_type=F32)


def remote(src, dst, send_sem, recv_sem, device):
    return pltpu.make_async_remote_copy(
        src_ref=src,
        dst_ref=dst,
        send_sem=send_sem,
        recv_sem=recv_sem,
        device_id=device,
        device_id_type=MESH,
    )


class Place:
    def __init__(self):
        self.zh, self.zl = lax.axis_index("zh"), lax.axis_index("zl")
        self.x, self.y, self.c = lax.axis_index("x"), lax.axis_index("y"), lax.axis_index("c")
        self.z = 2 * self.zh + self.zl
        self.inner = (self.z == 1) | (self.z == 2)
        self.outer = (self.z == 0) | (self.z == 3)
        self.rows = [self.z, 2 * self.zh + 1 - self.zl, 2 - self.zh, 3 - 3 * self.zh]
        self.mate = (self.zh, 1 - self.zl, self.x, self.y, self.c)
        self.mid = (1 - self.zh, 1 - self.zl, self.x, self.y, self.c)
        self.across = (self.zh, self.zl, 1 - self.x, self.y, self.c)

    def block(self, which, x):
        return self.rows[which] * 2 + x

    def enter_all(self, devices):
        barrier = pltpu.get_barrier_semaphore()
        for device in devices:
            pl.semaphore_signal(barrier, inc=1, device_id=device, device_id_type=MESH)
        pl.semaphore_wait(barrier, len(devices))

    def enter(self, *others):
        barrier = pltpu.get_barrier_semaphore()

        def greet(device):
            pl.semaphore_signal(barrier, inc=1, device_id=device, device_id_type=MESH)

        greet(self.mate)
        greet(self.across)
        for device in others:
            greet(device)

        @pl.when(self.inner)
        def _():
            greet(self.mid)

        @pl.when(self.inner)
        def _():
            pl.semaphore_wait(barrier, 3 + len(others))

        @pl.when(self.outer)
        def _():
            pl.semaphore_wait(barrier, 2 + len(others))


def pair_gather_chunk(p, weight, out, relay, ss, rs, first, count, rows):
    half = out.shape[1]
    here = pl.ds(first, count)
    own = weight.at[here, pl.ds(pl.multiple_of(p.zl * half, half), half)]
    other = weight.at[here, pl.ds(pl.multiple_of((1 - p.zl) * half, half), half)]

    def block(which, x):
        return out.at[pl.ds(pl.multiple_of(p.block(which, x) * rows + first, count), count), :]

    held = [relay.at[i, here, :] for i in range(3)]

    def send(slot, src, dst, recv, device):
        return remote(src, dst, ss.at[slot], rs.at[recv], device)

    def arrived(recv, dst):
        remote(dst, dst, ss.at[0], rs.at[recv], p.mate).wait_recv()

    local = pltpu.make_async_copy(own, block(OWN, p.x), ss.at[11])
    across = [
        send(7 + k, own if k == OWN else block(k, p.x), block(k, p.x), 6 + k, p.across)
        for k in range(4)
    ]
    to_mate = send(0, other, block(OWN, p.x), 0, p.mate)
    outer_own = send(1, own, held[0], 3, p.mate)
    mid_other = send(3, other, block(OWN, p.x), 1, p.mid)
    mid_own = send(4, own, held[1], 4, p.mid)
    mid_far = send(5, held[0], block(MATE, p.x), 2, p.mid)
    mid_far_own = send(6, block(MATE, p.x), held[2], 5, p.mid)
    back_near = send(1, held[1], block(NEAR, p.x), 1, p.mate)
    back_far = send(2, held[2], block(FAR, p.x), 2, p.mate)

    def begin():
        @pl.when(p.inner)
        def _():
            mid_other.start()
            mid_own.start()

        to_mate.start()

        @pl.when(p.outer)
        def _():
            outer_own.start()

        across[OWN].start()
        local.start()

    def mate_here():
        arrived(0, block(MATE, p.x))

        @pl.when(p.inner)
        def _():
            arrived(3, held[0])
            mid_far.start()
            mid_far_own.start()
            arrived(4, held[1])
            back_near.start()

        across[MATE].start()

    def near_here():
        arrived(1, block(NEAR, p.x))
        across[NEAR].start()

        @pl.when(p.inner)
        def _():
            arrived(5, held[2])
            back_far.start()

    def far_here():
        arrived(2, block(FAR, p.x))
        across[FAR].start()

    def finish():
        for k in range(4):
            arrived(6 + k, block(k, 1 - p.x))
            across[k].wait_send()
        local.wait()
        to_mate.wait_send()

        @pl.when(p.inner)
        def _():
            for copy in (mid_other, mid_own, mid_far, mid_far_own, back_near, back_far):
                copy.wait_send()

        @pl.when(p.outer)
        def _():
            outer_own.wait_send()

    return [begin, mate_here, near_here, far_here, finish]


def line_gather_chunk(p, weight, out, ss, rs, first, count, rows):
    own = weight.at[pl.ds(first, count), :]

    def block(which, x):
        return out.at[pl.ds(pl.multiple_of(p.block(which, x) * rows + first, count), count), :]

    def send(slot, src, dst, recv, device):
        return remote(src, dst, ss.at[slot], rs.at[recv], device)

    def arrived(recv, dst):
        remote(dst, dst, ss.at[0], rs.at[recv], p.mate).wait_recv()

    local = pltpu.make_async_copy(own, block(OWN, p.x), ss.at[9])
    across = [
        send(k, own if k == OWN else block(k, p.x), block(k, p.x), 3 + k, p.across)
        for k in range(4)
    ]
    to_mate = send(4, own, block(OWN, p.x), MATE - 1, p.mate)
    to_mid = send(5, own, block(OWN, p.x), NEAR - 1, p.mid)
    mid_far = send(6, block(MATE, p.x), block(MATE, p.x), FAR - 1, p.mid)
    back_near = send(7, block(NEAR, p.x), block(NEAR, p.x), NEAR - 1, p.mate)
    back_far = send(8, block(FAR, p.x), block(FAR, p.x), FAR - 1, p.mate)

    def begin():
        @pl.when(p.inner)
        def _():
            to_mid.start()

        to_mate.start()
        across[OWN].start()
        local.start()

    def mate_here():
        arrived(MATE - 1, block(MATE, p.x))

        @pl.when(p.inner)
        def _():
            mid_far.start()

        across[MATE].start()

    def near_here():
        arrived(NEAR - 1, block(NEAR, p.x))

        @pl.when(p.inner)
        def _():
            back_near.start()

        across[NEAR].start()

    def far_here():
        arrived(FAR - 1, block(FAR, p.x))

        @pl.when(p.inner)
        def _():
            back_far.start()

        across[FAR].start()

    def finish():
        for k in range(4):
            arrived(3 + k, block(k, 1 - p.x))
            across[k].wait_send()
        local.wait()
        to_mate.wait_send()

        @pl.when(p.inner)
        def _():
            for copy in (to_mid, mid_far, back_near, back_far):
                copy.wait_send()

    return [begin, mate_here, near_here, far_here, finish]


def contract_tokens(left, right):
    return lax.dot_general(left, right, (((0,), (0,)), ((), ())), preferred_element_type=F32)


class PairScatter:
    def __init__(self, p, product, sx, rx, sz, rz, rm, held, out, ss, rs):
        self.p, self.product = p, product
        self.sx, self.rx, self.sz, self.rz, self.rm = sx, rx, sz, rz, rm
        self.held, self.out, self.ss, self.rs = held, out, ss, rs
        self.half = held.shape[1]

    def across(self, k):
        return remote(self.sx.at[k], self.rx.at[k], self.ss.at[k], self.rs.at[k], self.p.across)

    def outward(self, j):
        return remote(self.sz.at[j], self.rz.at[j], self.ss.at[4 + j], self.rs.at[4 + j], self.p.mate)

    def middle(self, j):
        return remote(self.sz.at[j], self.rm.at[j], self.ss.at[7 + j], self.rs.at[7 + j], self.p.mid)

    def relay(self, j):
        return remote(
            self.rz.at[j], self.rm.at[2 + j], self.ss.at[9 + j], self.rs.at[9 + j], self.p.mid
        )

    def forward(self):
        return remote(self.rm.at[0], self.rz.at[0], self.ss.at[4], self.rs.at[4], self.p.mate)

    def back(self):
        return remote(self.sz.at[2], self.rz.at[1], self.ss.at[5], self.rs.at[5], self.p.mate)

    def cols_of(self, place):
        return pl.ds(pl.multiple_of(place * self.half, self.half), self.half)

    def send_across(self, k, *sent):
        self.sx[k] = self.product(k, 1 - self.p.x).astype(BF)
        self.sent(*sent)
        self.across(k).start()

    def summed(self, k):
        total = self.product(k, self.p.x)
        self.across(k).wait_recv()
        return total + self.rx[k].astype(F32)

    def send_on(self, k, j):
        self.sz[j] = self.summed(k).astype(BF)

        @pl.when(self.p.outer)
        def _():
            self.outward(j).start()

        @pl.when(self.p.inner)
        def _():
            self.middle(j).start()

    def send_relay(self, j):
        @pl.when(self.p.inner)
        def _():
            self.outward(j).wait_recv()
            self.relay(j).start()

    def mate_rows(self):
        total = self.summed(MATE)

        @pl.when(self.p.outer)
        def _():
            self.sz[2] = total.astype(BF)
            self.outward(2).start()

        @pl.when(self.p.inner)
        def _():
            self.held[...] = total

    def send_forward(self):
        @pl.when(self.p.inner)
        def _():
            self.middle(0).wait_recv()
            self.forward().start()

    def own_rows(self):
        self.out[:, self.cols_of(self.p.zl)] = self.summed(OWN)

    def send_back(self):
        @pl.when(self.p.inner)
        def _():
            self.relay(0).wait_recv()
            self.sz[2] = (self.held[...] + self.rm[2].astype(F32)).astype(BF)
            self.back().start()

    def finish(self):
        p, out = self.p, self.out
        here, there = self.cols_of(p.zl), self.cols_of(1 - p.zl)

        @pl.when(p.inner)
        def _():
            self.relay(1).wait_recv()
            out[:, here] = out[:, here] + self.rm[3].astype(F32)
            self.outward(2).wait_recv()
            self.middle(1).wait_recv()
            out[:, there] = self.rz[2].astype(F32) + self.rm[1].astype(F32)

        @pl.when(p.outer)
        def _():
            self.forward().wait_recv()
            out[:, here] = out[:, here] + self.rz[0].astype(F32)
            self.back().wait_recv()
            out[:, there] = self.rz[1].astype(F32)

        @pl.when(p.inner)
        def _():
            for j in range(2):
                self.relay(j).wait_send()
            self.forward().wait_send()

    def sent_on(self):
        @pl.when(self.p.outer)
        def _():
            for j in range(3):
                self.outward(j).wait_send()

        @pl.when(self.p.inner)
        def _():
            for j in range(2):
                self.middle(j).wait_send()
            self.back().wait_send()

    def sent(self, *which):
        for k in which:
            self.across(k).wait_send()


def pair_scatter_scratch(n, rows, half):
    return [
        pltpu.VMEM((4, rows, half), BF),
        pltpu.VMEM((n, 4, rows, half), BF),
        pltpu.VMEM((3, rows, half), BF),
        pltpu.VMEM((n, 3, rows, half), BF),
        pltpu.VMEM((n, 4, rows, half), BF),
        pltpu.VMEM((rows, half), F32),
        pltpu.SemaphoreType.DMA((n, 11)),
        pltpu.SemaphoreType.DMA((n, 11)),
    ]


class Columns:
    def __init__(self, p, jobs, buffer, sems):
        self.p, self.jobs, self.buffer, self.sems, self.at = p, jobs, buffer, sems, 0
        for n in range(min(2, len(jobs))):
            self.copies(n, "start")

    def copies(self, n, act):
        array, k, flip = self.jobs[n]
        pair, _, tokens, local = array.shape
        rows = self.buffer.shape[2]
        start = self.p.block(k, 1 - self.p.x if flip else self.p.x) * rows
        cols = pl.ds(pl.multiple_of(start % local, rows), rows)
        for q in range(pair):
            copy = pltpu.make_async_copy(
                array.at[q, start // local, :, cols],
                self.buffer.at[n % 2, pl.ds(q * tokens, tokens), :],
                self.sems.at[n % 2, q],
            )
            getattr(copy, act)()

    def times(self, right):
        return self.times_next(right, True, True)

    def times_next(self, right, first, last):
        if first:
            self.at += 1
            self.copies(self.at - 1, "wait")
        n = self.at - 1
        tokens = self.jobs[n][0].shape[0] * self.jobs[n][0].shape[2]
        product = contract_tokens(self.buffer[n % 2, :tokens, :], right)
        if last and n + 2 < len(self.jobs):
            self.copies(n + 2, "start")
        return product


ORDER = (FAR, NEAR, MATE, OWN)


class Spread:
    def __init__(self, p, view, ss, rs):
        self.p = p
        self.view, self.ss, self.rs = view, ss, rs

    def to_core(self):
        block = self.view(self.p.me)
        return remote(block, block, self.ss.at[0], self.rs.at[0], self.p.core)

    def to_side(self):
        block = self.view(self.p.me)
        return remote(block, block, self.ss.at[1], self.rs.at[1], self.p.side)

    def on_to_core(self):
        block = self.view(self.p.side_owner)
        return remote(block, block, self.ss.at[2], self.rs.at[2], self.p.core)

    def start(self):
        self.to_side().start()
        self.to_core().start()

    def forward(self):
        self.to_side().wait_recv()
        self.on_to_core().start()

    def finish(self):
        self.to_core().wait_recv()
        self.on_to_core().wait_recv()
        self.to_core().wait_send()
        self.to_side().wait_send()
        self.on_to_core().wait_send()


def lanes_of(column):
    return jnp.broadcast_to(column, (column.shape[0], 128)).T[:8]


def column_of(lanes):
    return jnp.broadcast_to(lanes[:1], (128, lanes.shape[1])).T[:, :1]


def block_forward(
    normed_here, stream, masks, conv_weight, gain, in_weight, out_weight, gate_weight, up_weight,
    down_weight, collective,
):
    tokens, local = normed_here.shape
    rows, width = gate_weight.shape
    half = width // 2
    three = in_weight.shape[1]
    owners, pair = 4, 2
    features = owners * local
    tile = tokens // 4
    plan = [("in", rows // 4)] * 4 + [("out", rows)]
    plan += [(name, rows // 4) for name in ("gate", "up", "down") for _ in range(4)]
    n_chunks = len(plan)

    def kernel(*refs):
        here_ref, stream_ref, masks_ref, conv_ref, gain_ref = refs[:5]
        in_ref, out_ref, gate_ref, up_ref, down_ref = refs[5:10]
        in_all, out_all, gate_all, up_all, down_all = refs[10:15]
        normed_all, projected_all, convolved_all, gated_all, mid_all = refs[15:20]
        hidden_all, silu_all, slope_all, mixed_all, middle, squares = refs[20:26]
        x, in_vm, out_vm, gate_vm, up_vm, projected, mixed, convolved, gated = refs[26:35]
        to_core, sums, from_y, near_squares, mid, results, relay = refs[35:42]
        halo = refs[55]
        chunk_ss, chunk_rs, x_ss, x_rs, mid_ss, mid_rs, move_ss, move_rs = refs[42:50]
        square_ss, square_rs, halo_sem, store_sem, result_sem = refs[50:55]

        p = Place()
        p.core = (p.zh, p.zl, p.x, p.y, 1 - p.c)
        p.side = (p.zh, p.zl, p.x, 1 - p.y, p.c)
        diagonal = (p.zh, p.zl, p.x, 1 - p.y, 1 - p.c)
        p.me, p.side_owner = 2 * p.y + p.c, 2 * (1 - p.y) + p.c
        place = 2 * p.z + p.x
        last = 2 * 4 - 1

        def device_at(s):
            return (s // 4, s // 2 % 2, s % 2, p.y, p.c)

        following, previous = device_at(lax.rem(place + 1, 8)), device_at(lax.rem(place + 7, 8))
        local_x = pltpu.make_async_copy(here_ref, x.at[p.me], store_sem.at[0])
        local_x.start()
        p.enter(p.core, p.side, diagonal, following, previous)

        chunks = []
        firsts = {}
        targets = {
            "in": (in_ref, in_vm), "out": (out_ref, out_vm), "gate": (gate_ref, gate_vm),
            "up": (up_ref, up_vm), "down": (down_ref, down_all),
        }
        for c, (name, count) in enumerate(plan):
            first = firsts.get(name, 0)
            firsts[name] = first + count
            source, target = targets[name]
            if name in ("in", "out"):
                chunk = line_gather_chunk(
                    p, source, target, chunk_ss.at[c], chunk_rs.at[c], first, count, rows
                )
            else:
                held = relay.at[("gate", "up", "down").index(name)]
                chunk = pair_gather_chunk(
                    p, source, target, held, chunk_ss.at[c], chunk_rs.at[c], first, count, rows
                )
            chunks.append(chunk)

        def pump(step):
            for stage in range(5):
                if 0 <= step - stage < n_chunks:
                    chunks[step - stage][stage]()

        stores = []

        def store(source, target):
            copy = pltpu.make_async_copy(source, target, store_sem.at[1 + len(stores)])
            copy.start()
            stores.append(copy)

        spread_x = Spread(p, lambda owner: x.at[owner], x_ss, x_rs)

        def project(t):
            here = pl.ds(t * tile, tile)
            value = sum(
                dot(x[j, here, :], in_vm[j * local : (j + 1) * local, :]) for j in range(owners)
            )
            projected[here, :] = value
            mixed[pl.ds(8 + t * tile, tile), :] = value[:, :local] * value[:, 2 * local :]

        def halo_copy():
            return remote(
                mixed.at[pl.ds(tokens, 8), :], halo, halo_sem.at[0], halo_sem.at[1], following
            )

        def send_halo():
            @pl.when(place < last)
            def _():
                halo_copy().start()

        def take_halo():
            @pl.when(place > 0)
            def _():
                halo_copy().wait_recv()

            @pl.when(place == 0)
            def _():
                halo[...] = jnp.zeros_like(halo)

            mixed[:8, :] = halo[...]

        def convolve(t):
            here = pl.ds(t * tile, tile)
            value = (
                conv_ref[0:1, :] * mixed[pl.ds(8 + t * tile, tile), :]
                + masks_ref[0, here, :] * conv_ref[1:2, :] * mixed[pl.ds(7 + t * tile, tile), :]
                + masks_ref[1, here, :] * conv_ref[2:3, :] * mixed[pl.ds(6 + t * tile, tile), :]
            )
            convolved[here, :] = value
            gated[here, :] = (projected[here, local : 2 * local] * value).astype(BF)

        owner = [
            2 * (1 - p.y) + 1 - p.c, 2 * (1 - p.y) + p.c, 2 * p.y + 1 - p.c, 2 * p.y + p.c
        ]

        def core_copy(b, t):
            return remote(
                to_core.at[b, t], sums.at[b, t], move_ss.at[b, t], move_rs.at[b, t], p.core
            )

        def side_copy(t):
            return remote(sums.at[0, t], from_y.at[t], move_ss.at[2, t], move_rs.at[2, t], p.side)

        def mixer_out(n):
            out_rows = pl.ds(pl.multiple_of(owner[n] * local, local), local)
            for t in range(4):
                here = pl.ds(t * tile, tile)
                value = contract_cols(gated[here, :], out_vm[out_rows, :])
                b = n // 2
                if n % 2 == 0:
                    to_core[b, t] = value.astype(BF)
                    core_copy(b, t).start()
                else:
                    core_copy(b, t).wait_recv()
                    value = value + sums[b, t].astype(F32)
                    if b == 0:
                        sums[b, t] = value.astype(BF)
                        side_copy(t).start()
                    else:
                        middle[here, :] = stream_ref[here, :] + value

        def residual(t):
            here = pl.ds(t * tile, tile)
            side_copy(t).wait_recv()
            value = middle[here, :] + from_y[t].astype(F32)
            middle[here, :] = value
            squares[:, here] = lanes_of(jnp.sum(value * value, axis=1, keepdims=True))

        def square_copies():
            return [
                remote(
                    squares, near_squares.at[i], square_ss.at[i], square_rs.at[i], device
                )
                for i, device in enumerate((p.core, p.side, diagonal))
            ]

        def sum_squares():
            for copy in square_copies():
                copy.wait_recv()
                copy.wait_send()
            squares[...] = (
                squares[...] + near_squares[0] + near_squares[1] + near_squares[2]
            )

        def own_tile(t):
            return lambda who: mid.at[p.zl, who, pl.ds(t * tile, tile), :]

        def mate_tile(t):
            return lambda who: mid.at[1 - p.zl, who, pl.ds(t * tile, tile), :]

        spread_own = [Spread(p, own_tile(t), mid_ss.at[0, t], mid_rs.at[0, t]) for t in range(4)]
        spread_mate = [Spread(p, mate_tile(t), mid_ss.at[1, t], mid_rs.at[1, t]) for t in range(4)]

        def mate_send(t):
            block = own_tile(t)(p.me)
            return remote(block, block, mid_ss.at[0, t, 3], mid_rs.at[0, t, 3], p.mate)

        def normalize_mid(t):
            here = pl.ds(t * tile, tile)
            inverse = lax.rsqrt(squares[:, here] / features + epsilon)
            value = middle[here, :] * column_of(inverse) * gain_ref[...]
            mid[p.zl, p.me, here, :] = value.astype(BF)
            mate_send(t).start()
            spread_own[t].start()

        def pass_on(t):
            spread_own[t].forward()
            mate_send(t).wait_recv()
            spread_mate[t].start()

        def result_stores(m, act):
            start = pl.multiple_of(tile_place(m) * tile, tile)
            for i, ref in enumerate((hidden_all, silu_all, slope_all)):
                copy = pltpu.make_async_copy(
                    results.at[m % 2, i], ref.at[pl.ds(start, tile), :], result_sem.at[m % 2, i]
                )
                getattr(copy, act)()

        def tile_place(m):
            return (p.zl if m < 4 else 1 - p.zl) * 4 + m % 4

        def hidden_units(m):
            q = p.zl if m < 4 else 1 - p.zl
            here = pl.ds(m % 4 * tile, tile)
            (spread_own if m < 4 else spread_mate)[m % 4].finish()
            if m >= 2:
                result_stores(m - 2, "wait")
            for part in range(2):
                cols = pl.ds(part * half // 2, half // 2)
                value = sum(
                    dot(mid[q, j, here, :], gate_vm[j * local : (j + 1) * local, cols])
                    for j in range(owners)
                )
                upward = sum(
                    dot(mid[q, j, here, :], up_vm[j * local : (j + 1) * local, cols])
                    for j in range(owners)
                )
                sigmoid = jax.nn.sigmoid(value)
                silu = value * sigmoid
                results[m % 2, 0, :, cols] = (silu * upward).astype(BF)
                results[m % 2, 1, :, cols] = silu.astype(BF)
                results[m % 2, 2, :, cols] = (upward * (sigmoid + silu * (1.0 - sigmoid))).astype(BF)
            result_stores(m, "start")

        pump(0)
        local_x.wait()
        spread_x.start()
        pump(1)
        pump(2)
        spread_x.forward()
        pump(3)
        pump(4)
        pump(5)
        spread_x.finish()
        pump(6)
        pump(7)
        store(x, normed_all)
        store(in_vm, in_all)
        project(3)
        send_halo()
        project(2)
        pump(8)
        project(1)
        project(0)
        store(projected, projected_all)
        store(out_vm, out_all)
        pump(9)
        take_halo()
        for t in range(4):
            convolve(t)
        store(convolved, convolved_all)
        store(mixed, mixed_all)
        store(gated, gated_all)
        mixer_out(0)
        mixer_out(1)
        pump(10)
        mixer_out(2)
        mixer_out(3)
        pump(11)
        residual(0)
        residual(1)
        pump(12)
        store(gate_vm, gate_all)
        residual(2)
        residual(3)
        for copy in square_copies():
            copy.start()
        pump(13)
        sum_squares()
        for t in range(4):
            normalize_mid(t)
        pump(14)
        pass_on(0)
        pass_on(1)
        pump(15)
        pass_on(2)
        pass_on(3)
        pump(16)
        store(up_vm, up_all)
        for t in range(4):
            spread_mate[t].forward()
        hidden_units(0)
        hidden_units(1)
        pump(17)
        hidden_units(2)
        hidden_units(3)
        pump(18)
        hidden_units(4)
        hidden_units(5)
        pump(19)
        hidden_units(6)
        hidden_units(7)
        store(mid, mid_all)
        pump(20)
        result_stores(6, "wait")
        result_stores(7, "wait")
        for copy in stores:
            copy.wait()
        for t in range(4):
            core_copy(0, t).wait_send()
            core_copy(1, t).wait_send()
            side_copy(t).wait_send()
            mate_send(t).wait_send()

        @pl.when(place < last)
        def _():
            halo_copy().wait_send()

    def array(*shape, dtype=BF):
        return jax.ShapeDtypeStruct(shape, dtype)

    units = array(pair * tokens, half)
    outs = [
        (array(8 * rows, three), ANY), (array(8 * rows, local), ANY),
        (array(8 * rows, half), ANY), (array(8 * rows, half), ANY), (array(8 * rows, half), ANY),
        (array(owners, tokens, local), ANY), (array(tokens, three, dtype=F32), ANY),
        (array(tokens, local, dtype=F32), ANY), (array(tokens, local), ANY),
        (array(pair, owners, tokens, local), ANY),
        (units, ANY), (units, ANY), (units, ANY),
        (array(8 + tokens, local, dtype=F32), ANY),
        (array(tokens, local, dtype=F32), VMEM), (array(8, tokens, dtype=F32), VMEM),
    ]
    return pl.pallas_call(
        kernel,
        out_shape=[o[0] for o in outs],
        in_specs=[ANY, VMEM, VMEM, VMEM, VMEM] + [ANY] * 5,
        out_specs=[o[1] for o in outs],
        scratch_shapes=[
            pltpu.VMEM((owners, tokens, local), BF),
            pltpu.VMEM((8 * rows, three), BF),
            pltpu.VMEM((8 * rows, local), BF),
            pltpu.VMEM((8 * rows, half), BF),
            pltpu.VMEM((8 * rows, half), BF),
            pltpu.VMEM((tokens, three), F32),
            pltpu.VMEM((8 + tokens, local), F32),
            pltpu.VMEM((tokens, local), F32),
            pltpu.VMEM((tokens, local), BF),
            pltpu.VMEM((2, 4, tile, local), BF),
            pltpu.VMEM((2, 4, tile, local), BF),
            pltpu.VMEM((4, tile, local), BF),
            pltpu.VMEM((3, 8, tokens), F32),
            pltpu.VMEM((pair, owners, tokens, local), BF),
            pltpu.VMEM((2, 3, tile, half), BF),
            pltpu.VMEM((3, 3, rows, half), BF),
            pltpu.SemaphoreType.DMA((n_chunks, 12)),
            pltpu.SemaphoreType.DMA((n_chunks, 10)),
            pltpu.SemaphoreType.DMA((3,)),
            pltpu.SemaphoreType.DMA((3,)),
            pltpu.SemaphoreType.DMA((2, 4, 4)),
            pltpu.SemaphoreType.DMA((2, 4, 4)),
            pltpu.SemaphoreType.DMA((3, 4)),
            pltpu.SemaphoreType.DMA((3, 4)),
            pltpu.SemaphoreType.DMA((3,)),
            pltpu.SemaphoreType.DMA((3,)),
            pltpu.SemaphoreType.DMA((2,)),
            pltpu.SemaphoreType.DMA((12,)),
            pltpu.SemaphoreType.DMA((2, 3)),
            pltpu.VMEM((8, local), F32),
        ],
        compiler_params=pltpu.CompilerParams(
            collective_id=collective, has_side_effects=True, vmem_limit_bytes=62 << 20
        ),
        cost_estimate=pl.CostEstimate(flops=0, bytes_accessed=600 << 20, transcendentals=0),
        name="block_forward",
    )(
        normed_here, stream, masks, conv_weight, gain, in_weight, out_weight, gate_weight, up_weight,
        down_weight,
    )


def feed_forward_backward(
    out_rows, normed, hidden, silu, slope, gate, up, down, middle, out_grad, squares, gain, collective
):
    pair, owners, tokens, local = normed.shape
    total, half = hidden.shape
    rows = owners * local // 8
    tile = total // 8
    piece = total // 4

    def kernel(*refs):
        out_ref, normed_ref, hidden_ref, silu_ref, slope_ref, gate_ref, up_ref, down_ref = refs[:8]
        middle_ref, out_grad_ref, squares_ref, gain_ref = refs[8:12]
        middle_grad, branch_all, gain_grad, partials, down_grad_all, gate_grad_all, up_rows = refs[12:19]
        gate_rows, weights, cols, early, to_core, sums, from_y, from_mate, lanes = refs[19:28]
        near_lanes, residual, weight_grad, cols_sem, early_sem, weights_sem, move_ss, move_rs = refs[28:36]
        lanes_ss, lanes_rs, branch_ss, branch_rs, tile_sem = refs[36:41]
        sx, rx, sz, rz, rm, held, ss, rs = refs[41:]
        p = Place()
        p.core = (p.zh, p.zl, p.x, p.y, 1 - p.c)
        p.side = (p.zh, p.zl, p.x, 1 - p.y, p.c)
        diagonal = (p.zh, p.zl, p.x, 1 - p.y, 1 - p.c)
        p.me, p.side_owner = 2 * p.y + p.c, 2 * (1 - p.y) + p.c

        down_load = pltpu.make_async_copy(down_ref, weights, weights_sem.at[0])
        down_load.start()

        def tile_loads(m, act):
            start = m % (8 // pair) * tile
            copies = [
                (
                    out_ref.at[m // (8 // pair), j, pl.ds(start, tile), :],
                    early.at[m % 2, pl.ds(j * tile, tile), :],
                )
                for j in range(owners)
            ]
            copies += [
                (
                    ref.at[pl.ds(m * tile, tile), pl.ds(part * local, local)],
                    early.at[2 + m % 2, pl.ds((2 * i + part) * tile, tile), :],
                )
                for i, ref in enumerate((silu_ref, slope_ref))
                for part in range(2)
            ]
            for i, (source, target) in enumerate(copies):
                getattr(pltpu.make_async_copy(source, target, early_sem.at[m % 2, i]), act)()

        quarter = tokens // 4
        D = (out_ref, normed_ref)
        jobs = [(D[0], k, True) for k in ORDER]
        jobs += [(D[0], FAR, False), (D[0], NEAR, False), (D[0], MATE, False)]
        jobs += [(D[1], FAR, True), (D[1], NEAR, True), (D[0], OWN, False)]
        jobs += [(D[1], MATE, True), (D[1], OWN, True)]
        jobs += [(D[1], k, False) for k in ORDER]
        feed = Columns(p, jobs, cols, cols_sem)
        tile_loads(0, "start")
        tile_loads(1, "start")
        p.enter(p.core, p.side, diagonal)

        dm = PairScatter(
            p, lambda k, x: feed.times(hidden_ref[...]), sx, rx.at[0], sz, rz.at[0],
            rm.at[0], held, weight_grad, ss.at[0], rs.at[0],
        )
        gm = PairScatter(
            p, lambda k, x: feed.times(gate_rows[...]), sx, rx.at[1], sz, rz.at[1],
            rm.at[1], held, weight_grad, ss.at[1], rs.at[1],
        )

        def rows_backward(m):
            tile_loads(m, "wait")
            here = pl.ds(m * tile, tile)
            hidden_grad = sum(
                dot(
                    early[m % 2, j * tile : (j + 1) * tile, :],
                    weights[j * local : (j + 1) * local, :],
                )
                for j in range(owners)
            )
            for part in range(2):
                units = pl.ds(part * local, local)
                value = hidden_grad[:, part * local : (part + 1) * local]
                for i, ref in enumerate((up_rows, gate_rows)):
                    first = (2 * i + part) * tile
                    factor = early[2 + m % 2, first : first + tile, :]
                    ref[here, units] = (value * factor.astype(F32)).astype(BF)
            if m + 2 < 8:
                tile_loads(m + 2, "start")

        owner = [
            2 * (1 - p.y) + 1 - p.c, 2 * (1 - p.y) + p.c, 2 * p.y + 1 - p.c, 2 * p.y + p.c
        ]

        def weight_loads(n, act):
            start = pl.multiple_of(owner[n] * local, local)
            for i, ref in enumerate((gate_ref, up_ref)):
                copy = pltpu.make_async_copy(
                    ref.at[pl.ds(start, local), :],
                    weights.at[pl.ds((n % 2 * 2 + i) * local, local), :],
                    weights_sem.at[1 + n % 2 * 2 + i],
                )
                getattr(copy, act)()

        def piece_rows(t):
            place = p.zl if t >= 2 else 1 - p.zl
            return pl.ds(pl.multiple_of(place * tokens + t % 2 * piece, piece), piece)

        def core_copy(b, t):
            return remote(
                to_core.at[t], sums.at[b, t], move_ss.at[b, t], move_rs.at[b, t], p.core
            )

        def side_copy(t):
            return remote(sums.at[0, t], from_y.at[t], move_ss.at[2, t], move_rs.at[2, t], p.side)

        def mate_copy(t):
            return remote(sums.at[1, t], from_mate.at[t], move_ss.at[3, t], move_rs.at[3, t], p.mate)

        def partial_sum(n, t):
            here = piece_rows(t)
            first = n % 2 * 2 * local
            return contract_cols(gate_rows[here, :], weights[first : first + local, :]) + contract_cols(
                up_rows[here, :], weights[first + local : first + 2 * local, :]
            )

        def partial_block(n):
            weight_loads(n, "wait")
            for t in range(4):
                value = partial_sum(n, t)
                b = n // 2
                if n % 2 == 0:
                    if b == 1:
                        core_copy(0, t).wait_send()
                    to_core[t] = value.astype(BF)
                    core_copy(b, t).start()
                else:
                    core_copy(b, t).wait_recv()
                    sums[b, t] = (value + sums[b, t].astype(F32)).astype(BF)
                    if b == 0:
                        side_copy(t).start()
            if n + 2 < 4:
                weight_loads(n + 2, "start")

        def to_mate(t):
            side_copy(t).wait_recv()
            sums[1, t] = (sums[1, t].astype(F32) + from_y[t].astype(F32)).astype(BF)
            mate_copy(t).start()

        def final(t):
            side_copy(t).wait_recv()
            mate_copy(t - 2).wait_recv()
            middle_grad[pl.ds((t - 2) * piece, piece), :] = (
                sums[1, t].astype(F32) + from_y[t].astype(F32) + from_mate[t - 2].astype(F32)
            )

        def lane_copies():
            return [
                remote(lanes, near_lanes.at[i], lanes_ss.at[i], lanes_rs.at[i], device)
                for i, device in enumerate((p.core, p.side, diagonal))
            ]

        inverse_lanes = lax.rsqrt(squares_ref[...] / (owners * local) + epsilon)

        def residual_loads(n, act):
            here = pl.ds(n % 4 * quarter, quarter)
            for i, ref in enumerate((middle_ref, out_grad_ref)):
                copy = pltpu.make_async_copy(ref.at[here, :], residual.at[n % 2, i], tile_sem.at[n % 2, i])
                getattr(copy, act)()

        def row_sums():
            total = jnp.zeros((1, local), F32)
            for t in range(4):
                here = pl.ds(t * quarter, quarter)
                residual_loads(t, "wait")
                product = middle_grad[here, :] * residual[t % 2, 0]
                residual_loads(t + 2, "start")
                lanes[:, here] = lanes_of(
                    jnp.sum(product * gain_ref[...], axis=1, keepdims=True)
                )
                inverse = column_of(inverse_lanes[:, t * quarter : (t + 1) * quarter])
                total = total + jnp.sum(product * inverse, axis=0, keepdims=True)
            gain_grad[...] = total
            for copy in lane_copies():
                copy.start()

        spreads = [
            Spread(
                p,
                lambda who, t=t: early.at[who, pl.ds(t * quarter, quarter), :],
                branch_ss.at[t],
                branch_rs.at[t],
            )
            for t in range(4)
        ]

        def residual_grad():
            for copy in lane_copies():
                copy.wait_recv()
            sums_all = (lanes[...] + near_lanes[0] + near_lanes[1] + near_lanes[2]) / (owners * local)
            scale_all = inverse_lanes * inverse_lanes * inverse_lanes * sums_all
            for t in range(4):
                here = pl.ds(t * quarter, quarter)
                part = slice(t * quarter, (t + 1) * quarter)
                residual_loads(4 + t, "wait")
                value = (
                    residual[t % 2, 1]
                    + column_of(inverse_lanes[:, part]) * gain_ref[...] * middle_grad[here, :]
                    - residual[t % 2, 0] * column_of(scale_all[:, part])
                )
                middle_grad[here, :] = value
                early[p.me, here, :] = value.astype(BF)
                spreads[t].start()
                if t + 2 < 4:
                    residual_loads(6 + t, "start")

        def out_store(m, j):
            start = m % (8 // pair) * tile
            return pltpu.make_async_copy(
                to_core.at[j % 2, pl.ds(0, tile), :],
                partials.at[m // (8 // pair), j, pl.ds(start, tile), :],
                tile_sem.at[2, j % 2],
            )

        def out_partial(m):
            for j in range(owners):
                value = contract_cols(
                    hidden_ref[pl.ds(m * tile, tile), :], weights[j * local : (j + 1) * local, :]
                )
                if m > 0 or j >= 2:
                    out_store(m if j >= 2 else m - 1, (j - 2) % owners).wait()
                to_core[j % 2, :tile, :] = value.astype(BF)
                out_store(m, j).start()

        for k in ORDER:
            dm.send_across(k)
        down_load.wait()
        for m in range(3):
            rows_backward(m)
        dm.send_on(FAR, 0)
        for m in range(3, 7):
            rows_backward(m)
        dm.send_on(NEAR, 1)
        rows_backward(7)
        weight_loads(0, "start")
        weight_loads(1, "start")
        dm.send_relay(0)
        partial_block(0)
        partial_block(1)
        dm.mate_rows()
        dm.send_relay(1)
        dm.send_forward()
        dm.sent(FAR)
        gm.send_across(FAR)
        dm.sent(NEAR)
        gm.send_across(NEAR)
        partial_block(2)
        dm.own_rows()
        dm.sent(MATE)
        gm.send_across(MATE)
        dm.sent(OWN)
        gm.send_across(OWN)
        dm.send_back()
        partial_block(3)
        down_again = pltpu.make_async_copy(down_ref, weights, weights_sem.at[0])
        down_again.start()
        to_mate(0)
        dm.sent_on()
        gm.send_on(FAR, 0)
        down_again.wait()
        for t in range(4):
            core_copy(1, t).wait_send()
        for m in range(4):
            out_partial(m)
        to_mate(1)
        gm.send_on(NEAR, 1)
        gm.send_relay(0)
        for m in range(4, 8):
            out_partial(m)
        residual_loads(0, "start")
        residual_loads(1, "start")
        final(2)
        gm.mate_rows()
        gm.send_relay(1)
        gm.send_forward()
        final(3)
        row_sums()
        dm.finish()
        down_store = pltpu.make_async_copy(weight_grad, down_grad_all, weights_sem.at[1])
        down_store.start()
        residual_grad()
        down_store.wait()
        gm.own_rows()
        gm.send_back()
        for t in range(4):
            spreads[t].forward()
        gm.finish()
        gate_store = pltpu.make_async_copy(weight_grad, gate_grad_all, weights_sem.at[1])
        gate_store.start()
        for t in range(4):
            spreads[t].finish()
        gather_done = pltpu.make_async_copy(early, branch_all, early_sem.at[0, 0])
        gather_done.start()
        gm.sent_on()
        gm.sent(*ORDER)
        for t in range(4):
            side_copy(t).wait_send()
        for t in range(2):
            mate_copy(t).wait_send()
        for copy in lane_copies():
            copy.wait_send()
        out_store(7, 2).wait()
        out_store(7, 3).wait()
        gather_done.wait()
        gate_store.wait()

    def array(*shape, dtype=F32):
        return jax.ShapeDtypeStruct(shape, dtype)

    return pl.pallas_call(
        kernel,
        out_shape=[
            array(tokens, local),
            array(owners, tokens, local, dtype=BF),
            array(1, local),
            array(pair, owners, tokens, local, dtype=BF),
            array(rows, 2 * half),
            array(rows, 2 * half),
            array(total, half, dtype=BF),
        ],
        in_specs=[ANY, ANY, VMEM, ANY, ANY, ANY, ANY, ANY, ANY, ANY, VMEM, VMEM],
        out_specs=[VMEM, ANY, VMEM, ANY, ANY, ANY, VMEM],
        scratch_shapes=[
            pltpu.VMEM((total, half), BF),
            pltpu.VMEM((owners * local, half), BF),
            pltpu.VMEM((2, total, rows), BF),
            pltpu.VMEM((owners, tokens, local), BF),
            pltpu.VMEM((4, piece, local), BF),
            pltpu.VMEM((2, 4, piece, local), BF),
            pltpu.VMEM((4, piece, local), BF),
            pltpu.VMEM((2, piece, local), BF),
            pltpu.VMEM((8, tokens), F32),
            pltpu.VMEM((3, 8, tokens), F32),
            pltpu.VMEM((2, 2, tokens // 4, local), F32),
            pltpu.VMEM((rows, 2 * half), F32),
            pltpu.SemaphoreType.DMA((2, pair)),
            pltpu.SemaphoreType.DMA((2, 8)),
            pltpu.SemaphoreType.DMA((5,)),
            pltpu.SemaphoreType.DMA((4, 4)),
            pltpu.SemaphoreType.DMA((4, 4)),
            pltpu.SemaphoreType.DMA((3,)),
            pltpu.SemaphoreType.DMA((3,)),
            pltpu.SemaphoreType.DMA((4, 3)),
            pltpu.SemaphoreType.DMA((4, 3)),
            pltpu.SemaphoreType.DMA((3, 2)),
        ]
        + pair_scatter_scratch(2, rows, half),
        compiler_params=pltpu.CompilerParams(
            collective_id=collective, has_side_effects=True, vmem_limit_bytes=62 << 20
        ),
        cost_estimate=pl.CostEstimate(flops=0, bytes_accessed=300 << 20, transcendentals=0),
        name="feed_forward_backward",
    )(
        out_rows, normed, hidden, silu, slope, gate, up, down, middle, out_grad, squares, gain
    )


class LineScatter:
    def __init__(self, p, product, sx, rx, sz, rz, rm, held, out, ss, rs):
        self.p, self.product = p, product
        self.sx, self.rx, self.sz, self.rz, self.rm = sx, rx, sz, rz, rm
        self.held, self.out, self.ss, self.rs = held, out, ss, rs

    def across(self, k):
        return remote(self.sx.at[k], self.rx.at[k], self.ss.at[k], self.rs.at[k], self.p.across)

    def outward(self, j):
        return remote(self.sz.at[j], self.rz.at[j], self.ss.at[4 + j], self.rs.at[4 + j], self.p.mate)

    def middle(self, j):
        return remote(self.sz.at[j], self.rm.at[j], self.ss.at[7 + j], self.rs.at[7 + j], self.p.mid)

    def back(self):
        return remote(self.sz.at[2], self.rz.at[0], self.ss.at[4], self.rs.at[4], self.p.mate)

    def send_across(self, k):
        self.sx[k] = self.product(k, 1 - self.p.x).astype(BF)
        self.across(k).start()

    def summed(self, k):
        total = self.product(k, self.p.x)
        self.across(k).wait_recv()
        return total + self.rx[k].astype(F32)

    def send_on(self, k, j):
        total = self.summed(k)

        @pl.when(self.p.outer)
        def _():
            self.sz[j] = total.astype(BF)
            self.outward(j).start()

        @pl.when(self.p.inner)
        def _():
            self.outward(j).wait_recv()
            self.sz[j] = (total + self.rz[j].astype(F32)).astype(BF)
            self.middle(j).start()

    def mate_rows(self):
        total = self.summed(MATE)

        @pl.when(self.p.outer)
        def _():
            self.sz[2] = total.astype(BF)
            self.outward(2).start()

        @pl.when(self.p.inner)
        def _():
            self.held[...] = total

    def own_rows(self):
        self.out[...] = self.summed(OWN)

    def send_back(self):
        @pl.when(self.p.inner)
        def _():
            self.middle(0).wait_recv()
            self.sz[2] = (self.held[...] + self.rm[0].astype(F32)).astype(BF)
            self.back().start()

    def finish(self):
        @pl.when(self.p.inner)
        def _():
            self.outward(2).wait_recv()
            self.middle(1).wait_recv()
            self.out[...] = self.out[...] + self.rz[2].astype(F32) + self.rm[1].astype(F32)
            for j in range(2):
                self.middle(j).wait_send()
            self.back().wait_send()

        @pl.when(self.p.outer)
        def _():
            self.back().wait_recv()
            self.out[...] = self.out[...] + self.rz[0].astype(F32)
            for j in range(3):
                self.outward(j).wait_send()

        for k in range(4):
            self.across(k).wait_send()


def mixer_backward(
    normed_mid, up_rows, branch, whole_out, in_matrix, projected, convolved, mixed, gated, normed_in,
    masks, conv_weight, stream, middle_grad, gain, inverse, gain_mid_grad, collective,
):
    pair, owners, tokens, local = normed_mid.shape
    total, half = up_rows.shape
    rows = owners * local // 8
    three = in_matrix.shape[1]
    tile = tokens // 4
    groups = three // local

    def kernel(*refs):
        normed_mid_ref, up_rows_ref, branch_ref, out_ref, in_ref, projected_ref, convolved_ref = refs[:7]
        mixed_ref, gated_ref, normed_in_ref, masks_ref, conv_ref, stream_ref = refs[7:13]
        middle_ref, gain_ref, inverse_ref, gain_mid_ref = refs[13:17]
        stream_grad, small_sums, up_grad, out_grad, in_grad = refs[17:22]
        conv_grad, rows_grad, stage, stage_mixed, weights, to_core, sums, from_y, lanes, near_lanes = refs[22:32]
        smalls, cols, stage_sem, in_sem, move_ss, move_rs, lanes_ss, lanes_rs = refs[32:40]
        small_ss, small_rs, halo_sem, cols_sem = refs[40:44]
        branch_sem = refs[59]
        sx, rx, sz, rz, rm, held, ss, rs = refs[44:52]
        lx, lrx, lz, lrz, lrm, lss, lrs = refs[52:59]
        lheld = held.at[:, pl.ds(0, local)]

        p = Place()
        p.core = (p.zh, p.zl, p.x, p.y, 1 - p.c)
        p.side = (p.zh, p.zl, p.x, 1 - p.y, p.c)
        diagonal = (p.zh, p.zl, p.x, 1 - p.y, 1 - p.c)
        place = 2 * p.z + p.x
        last = 7

        def device_at(s):
            return (s // 4, s // 2 % 2, s % 2, p.y, p.c)

        others = [lax.rem(place + d, 8) for d in range(1, 8)]

        jobs = []
        for t in range(4):
            jobs.append(((projected_ref, 1), (convolved_ref, 0), t))
        for t in range(4):
            jobs.append(((projected_ref, 0), (projected_ref, 2), t))
        for _ in range(2):
            for t in range(4):
                jobs.append(((stream_ref, 0), (middle_ref, 0), t))
        taken = []

        def stage_copies(n, act):
            for i, (ref, group) in enumerate(jobs[n][:2]):
                copy = pltpu.make_async_copy(
                    ref.at[pl.ds(jobs[n][2] * tile, tile), pl.ds(group * local, local)],
                    stage.at[n % 2, i],
                    stage_sem.at[n % 2, i],
                )
                getattr(copy, act)()

        def mixed_load(t):
            return pltpu.make_async_copy(
                mixed_ref.at[pl.ds(t * tile, tile + 8), :], stage_mixed.at[t % 2], stage_sem.at[t % 2, 2]
            )

        def branch_slot(t, j):
            return to_core.at[j] if t % 2 == 0 else lz.at[j // 3, j % 3]

        def branch_loads(t, act):
            for j in range(owners):
                copy = pltpu.make_async_copy(
                    branch_ref.at[0, j, pl.ds(t * tile, tile), :], branch_slot(t, j), branch_sem.at[t % 2, j]
                )
                getattr(copy, act)()

        def staged():
            n = len(taken)
            taken.append(n)
            stage_copies(n, "wait")
            values = stage[n % 2, 0], stage[n % 2, 1]
            return values

        def staged_done():
            n = len(taken) - 1
            if n + 2 < len(jobs):
                stage_copies(n + 2, "start")

        def out_loads(act):
            for j in range(owners):
                copy = pltpu.make_async_copy(
                    out_ref.at[pl.ds(j * local, local), :], weights.at[j], in_sem.at[j]
                )
                getattr(copy, act)()

        out_loads("start")
        stage_copies(0, "start")
        stage_copies(1, "start")
        branch_loads(0, "start")
        branch_loads(1, "start")
        mixed_load(0).start()
        mixed_load(1).start()
        feed_jobs = [(normed_mid_ref, k, True) for k in ORDER]
        feed_jobs += [(normed_mid_ref, FAR, False)]
        feed_jobs += [(branch_ref, k, True) for k in ORDER]
        feed_jobs += [(normed_mid_ref, NEAR, False)]
        feed_jobs += [(normed_in_ref, FAR, True), (normed_in_ref, NEAR, True)]
        feed_jobs += [(normed_mid_ref, MATE, False)]
        feed_jobs += [(normed_in_ref, MATE, True), (normed_in_ref, OWN, True)]
        feed_jobs += [(normed_mid_ref, OWN, False)]
        feed_jobs += [(branch_ref, k, False) for k in ORDER]
        feed_jobs += [(normed_in_ref, k, False) for k in ORDER]
        feed = Columns(p, feed_jobs, cols, cols_sem)
        owner = [
            2 * (1 - p.y) + 1 - p.c, 2 * (1 - p.y) + p.c, 2 * p.y + 1 - p.c, 2 * p.y + p.c
        ]
        p.enter_all([device_at(s) for s in others] + [p.core, p.side, diagonal])

        um = PairScatter(
            p, lambda k, x: feed.times(up_rows_ref[...]), sx, rx.at[0], sz, rz.at[0], rm.at[0], held,
            up_grad, ss.at[0], rs.at[0],
        )

        om = LineScatter(
            p, lambda k, x: feed.times(gated_ref[...]), lx.at[0], lrx.at[0], lz.at[0], lrz.at[0], lrm.at[0], lheld,
            out_grad, lss.at[0], lrs.at[0],
        )
        ims = [
            LineScatter(
                p, lambda k, x, g=g: feed.times_next(rows_grad[g], g == 0, g == groups - 1),
                lx.at[1 + g], lrx.at[1 + g], lz.at[1 + g], lrz.at[1 + g], lrm.at[1 + g],
                lheld, in_grad.at[:, pl.ds(g * local, local)], lss.at[1 + g], lrs.at[1 + g],
            )
            for g in range(groups)
        ]

        def halo_copy():
            return remote(
                conv_grad.at[pl.ds(0, 8), :],
                conv_grad.at[pl.ds(tokens, 8), :],
                halo_sem.at[0],
                halo_sem.at[1],
                device_at(others[6]),
            )

        taps = [jnp.zeros((1, local), F32) for _ in range(3)]

        def gated_backward(t):
            here = pl.ds(t * tile, tile)
            branch_loads(t, "wait")
            gated_grad = sum(
                dot(branch_slot(t, j)[...], weights[j])
                for j in range(owners)
            )
            if t + 2 < 4:
                branch_loads(t + 2, "start")
            out_gate, conv = staged()
            mixed_load(t).wait()
            near = stage_mixed.at[t % 2]
            rows_grad[1, here, :] = (gated_grad * conv).astype(BF)
            value = gated_grad * out_gate
            conv_grad[here, :] = value
            staged_done()
            taps[0] += jnp.sum(value * near[pl.ds(8, tile), :], axis=0, keepdims=True)
            taps[1] += jnp.sum(
                masks_ref[here, 0:1] * value * near[pl.ds(7, tile), :],
                axis=0, keepdims=True,
            )
            taps[2] += jnp.sum(
                masks_ref[here, 1:2] * value * near[pl.ds(6, tile), :],
                axis=0, keepdims=True,
            )
            if t + 2 < 4:
                mixed_load(t + 2).start()

        def send_halo():
            @pl.when(place > 0)
            def _():
                halo_copy().start()

        def take_halo():
            @pl.when(place < last)
            def _():
                halo_copy().wait_recv()

            @pl.when(place == last)
            def _():
                conv_grad[tokens:, :] = jnp.zeros((8, local), F32)

        def conv_backward(t):
            here = pl.ds(t * tile, tile)
            in_gate, carried = staged()
            value = (
                conv_ref[0:1, :] * conv_grad[here, :]
                + masks_ref[here, 2:3] * conv_ref[1:2, :] * conv_grad[pl.ds(1 + t * tile, tile), :]
                + masks_ref[here, 3:4] * conv_ref[2:3, :] * conv_grad[pl.ds(2 + t * tile, tile), :]
            )
            rows_grad[0, here, :] = (value * carried).astype(BF)
            rows_grad[2, here, :] = (value * in_gate).astype(BF)
            staged_done()

        def in_loads(n, act):
            start = pl.multiple_of(owner[n] * local, local)
            for g in range(groups):
                copy = pltpu.make_async_copy(
                    in_ref.at[pl.ds(start, local), pl.ds(g * local, local)], weights.at[g], in_sem.at[g]
                )
                getattr(copy, act)()

        def core_copy(b, t):
            return remote(to_core.at[t], sums.at[b, t], move_ss.at[b, t], move_rs.at[b, t], p.core)

        def side_copy(t):
            return remote(sums.at[0, t], from_y.at[t], move_ss.at[2, t], move_rs.at[2, t], p.side)

        def partial_block(n):
            in_loads(n, "wait")
            b = n // 2
            for t in range(4):
                here = pl.ds(t * tile, tile)
                value = sum(
                    contract_cols(rows_grad[g, here, :], weights[g])
                    for g in range(groups)
                )
                if n % 2 == 0:
                    if b == 1:
                        core_copy(0, t).wait_send()
                    to_core[t] = value.astype(BF)
                    core_copy(b, t).start()
                else:
                    core_copy(b, t).wait_recv()
                    value = value + sums[b, t].astype(F32)
                    if b == 0:
                        sums[b, t] = value.astype(BF)
                        side_copy(t).start()
                    else:
                        stream_grad[here, :] = value
            if n + 1 < 4:
                in_loads(n + 1, "start")

        def lane_copies():
            return [
                remote(lanes, near_lanes.at[i], lanes_ss.at[i], lanes_rs.at[i], device)
                for i, device in enumerate((p.core, p.side, diagonal))
            ]

        def small_copies():
            return [
                remote(
                    smalls.at[place], smalls.at[place], small_ss.at[d], small_rs.at[place], device_at(s)
                )
                for d, s in enumerate(others)
            ]

        def row_sums():
            total_gain = jnp.zeros((1, local), F32)
            for t in range(4):
                here = pl.ds(t * tile, tile)
                side_copy(t).wait_recv()
                value = stream_grad[here, :] + from_y[t].astype(F32)
                stream_grad[here, :] = value
                values = staged()[0]
                staged_done()
                product = value * values
                lanes[:, here] = lanes_of(jnp.sum(product * gain_ref[...], axis=1, keepdims=True))
                inverse_here = column_of(inverse_ref[:, here])
                total_gain = total_gain + jnp.sum(product * inverse_here, axis=0, keepdims=True)
            for copy in lane_copies():
                copy.start()
            smalls[place] = jnp.concatenate(
                taps + [total_gain, gain_mid_ref[...], jnp.zeros((3, local), F32)], axis=0
            )
            for copy in small_copies():
                copy.start()

        def input_grad():
            for copy in lane_copies():
                copy.wait_recv()
            sums_all = (lanes[...] + near_lanes[0] + near_lanes[1] + near_lanes[2]) / (owners * local)
            scale_all = inverse_ref[...] * inverse_ref[...] * inverse_ref[...] * sums_all
            for t in range(4):
                here = pl.ds(t * tile, tile)
                values, residual = staged()
                stream_grad[here, :] = (
                    residual
                    + column_of(inverse_ref[:, here]) * gain_ref[...] * stream_grad[here, :]
                    - values * column_of(scale_all[:, t * tile : (t + 1) * tile])
                )
                staged_done()

        def sum_smalls():
            for s in others:
                block = smalls.at[s]
                remote(block, block, small_ss.at[0], small_rs.at[s], p.mate).wait_recv()
            value = smalls[0]
            for s in range(1, 8):
                value = value + smalls[s]
            small_sums[...] = value

        for k in ORDER:
            um.send_across(k)
        out_loads("wait")
        for t in range(4):
            gated_backward(t)
            if t == 0:
                send_halo()
        in_loads(0, "start")
        um.send_on(FAR, 0)
        take_halo()
        for t in range(4):
            conv_backward(t)
        for k in ORDER:
            om.send_across(k)
        um.send_on(NEAR, 1)
        um.send_relay(0)
        partial_block(0)
        partial_block(1)
        for k in (FAR, NEAR):
            for m in ims:
                m.send_across(k)
        um.mate_rows()
        um.send_relay(1)
        um.send_forward()
        partial_block(2)
        partial_block(3)
        for k in (MATE, OWN):
            for m in ims:
                m.send_across(k)
        um.own_rows()
        um.send_back()
        row_sums()
        om.send_on(FAR, 0)
        om.send_on(NEAR, 1)
        input_grad()
        um.finish()
        om.mate_rows()
        om.own_rows()
        om.send_back()
        for m in ims:
            m.send_on(FAR, 0)
        sum_smalls()
        for m in ims:
            m.send_on(NEAR, 1)
        om.finish()
        for m in ims:
            m.mate_rows()
            m.send_back()
        for m in ims:
            m.own_rows()
        for m in ims:
            m.finish()
        um.sent_on()
        um.sent(*ORDER)
        for t in range(4):
            core_copy(1, t).wait_send()
            side_copy(t).wait_send()
        for copy in lane_copies() + small_copies():
            copy.wait_send()

        @pl.when(place > 0)
        def _():
            halo_copy().wait_send()

    def array(*shape):
        return jax.ShapeDtypeStruct(shape, F32)

    n = 1 + groups
    return pl.pallas_call(
        kernel,
        out_shape=[
            array(tokens, local),
            array(8, local),
            array(rows, 2 * half),
            array(rows, local),
            array(rows, three),
        ],
        in_specs=[ANY, VMEM, ANY, ANY, ANY, ANY, ANY, ANY, VMEM, ANY, VMEM, VMEM, ANY, ANY]
        + [VMEM] * 3,
        out_specs=[VMEM] * 5,
        scratch_shapes=[
            pltpu.VMEM((tokens + 8, local), F32),
            pltpu.VMEM((groups, tokens, local), BF),
            pltpu.VMEM((2, 2, tile, local), F32),
            pltpu.VMEM((2, tile + 8, local), F32),
            pltpu.VMEM((owners, local, local), BF),
            pltpu.VMEM((4, tile, local), BF),
            pltpu.VMEM((2, 4, tile, local), BF),
            pltpu.VMEM((4, tile, local), BF),
            pltpu.VMEM((8, tokens), F32),
            pltpu.VMEM((3, 8, tokens), F32),
            pltpu.VMEM((8, 8, local), F32),
            pltpu.VMEM((2, total, rows), BF),
            pltpu.SemaphoreType.DMA((2, 3)),
            pltpu.SemaphoreType.DMA((owners,)),
            pltpu.SemaphoreType.DMA((3, 4)),
            pltpu.SemaphoreType.DMA((3, 4)),
            pltpu.SemaphoreType.DMA((3,)),
            pltpu.SemaphoreType.DMA((3,)),
            pltpu.SemaphoreType.DMA((7,)),
            pltpu.SemaphoreType.DMA((8,)),
            pltpu.SemaphoreType.DMA((2,)),
            pltpu.SemaphoreType.DMA((2, pair)),
        ]
        + pair_scatter_scratch(1, rows, half)
        + [
            pltpu.VMEM((n, 4, rows, local), BF),
            pltpu.VMEM((n, 4, rows, local), BF),
            pltpu.VMEM((n, 3, rows, local), BF),
            pltpu.VMEM((n, 3, rows, local), BF),
            pltpu.VMEM((n, 2, rows, local), BF),
            pltpu.SemaphoreType.DMA((n, 9)),
            pltpu.SemaphoreType.DMA((n, 9)),
            pltpu.SemaphoreType.DMA((2, owners)),
        ],
        compiler_params=pltpu.CompilerParams(
            collective_id=collective, has_side_effects=True, vmem_limit_bytes=62 << 20
        ),
        cost_estimate=pl.CostEstimate(flops=0, bytes_accessed=300 << 20, transcendentals=0),
        name="mixer_backward",
    )(
        normed_mid, up_rows, branch[None], whole_out, in_matrix, projected, convolved, mixed, gated,
        normed_in[None], masks, conv_weight, stream, middle_grad, gain, inverse, gain_mid_grad,
    )


SEQ = ("zh", "zl", "x")
TP = ("y", "c")
PAIR = ("zl", "y", "c")


def after(value, *others):
    return lax.optimization_barrier((value, *others))[0]


def gather_pair_rows(rows):
    blocks = lax.all_gather(rows, PAIR, axis=0)
    return blocks.reshape(lax.axis_size("zl"), lax.axis_size(TP), *rows.shape)


def rms_scale(values, gain):
    width = gain.shape[0] * lax.axis_size(TP)
    squares = lax.psum(jnp.sum(values * values, axis=1, keepdims=True), TP)
    inverse = lax.rsqrt(squares / width + epsilon)
    return (values * inverse * gain).astype(BF), inverse, jnp.sqrt(squares[:, 0] / width + epsilon)


def paired_on_device(
    stream,
    norm1_gain,
    in_weight,
    conv_weight,
    out_weight,
    norm2_gain,
    gate_weight,
    up_weight,
    down_weight,
    doc_starts,
    out_grad,
):
    tokens, local = stream.shape
    rows_here = in_weight.shape[0]
    positions = lax.axis_index(SEQ) * tokens + jnp.arange(tokens, dtype=jnp.int32)
    mask_one, mask_two = lag_masks(doc_starts, positions)
    normed_here, inverse_in, rms_in = rms_scale(stream, norm1_gain)
    (
        in_matrix, whole_out, whole_gate, whole_up, whole_down, normed_in, projected, convolved, gated,
        normed_mid, hidden, silu, slope, mixed, middle, squares,
    ) = block_forward(
        normed_here,
        stream,
        jnp.stack([mask_one, mask_two]),
        conv_weight,
        norm2_gain[None],
        in_weight.reshape(rows_here, 3 * local),
        out_weight,
        gate_weight,
        up_weight,
        down_weight,
        0,
    )
    out_full = gather_pair_rows(after(out_grad.astype(BF), normed_here))
    mean_square = squares[0] / (local * lax.axis_size(TP)) + epsilon
    rms_mid, inverse_mid = jnp.sqrt(mean_square), lax.rsqrt(mean_square)[:, None]
    middle_grad, branch_blocks, gain_mid_grad, ffn_partial, down_weight_grad, gate_weight_grad, up_rows = (
        feed_forward_backward(
            out_full, normed_mid, hidden, silu, slope, whole_gate, whole_up, whole_down, middle, out_grad,
            squares, norm2_gain[None], 4,
        )
    )
    result = middle + lax.psum_scatter(
        ffn_partial.reshape(-1, local), PAIR, scatter_dimension=0, tiled=True
    ).astype(F32)
    next_one, next_two = lag_masks(doc_starts, positions + 1)[0], lag_masks(doc_starts, positions + 2)[1]
    count = tokens * lax.axis_size(SEQ)
    masks = jnp.concatenate(
        [
            mask_one,
            mask_two,
            jnp.where(positions[:, None] + 1 < count, next_one, 0.0),
            jnp.where(positions[:, None] + 2 < count, next_two, 0.0),
        ],
        axis=1,
    )
    stream_grad, small_sums, up_weight_grad, out_weight_grad, in_weight_grad = mixer_backward(
        normed_mid, up_rows, branch_blocks, whole_out, in_matrix, projected, convolved, mixed, gated,
        normed_in, masks, conv_weight, stream, middle_grad, norm1_gain[None],
        jnp.broadcast_to(inverse_in.reshape(1, tokens), (8, tokens)), gain_mid_grad, 5,
    )
    conv_total, gain_in_total, gain_mid_total = small_sums[:3], small_sums[3], small_sums[4]
    return (
        result,
        stream_grad,
        gain_in_total,
        in_weight_grad.reshape(rows_here, 3, local),
        conv_total,
        out_weight_grad,
        gain_mid_total,
        gate_weight_grad,
        up_weight_grad,
        down_weight_grad,
        jnp.stack([rms_in, rms_mid]),
    )


def solution(mesh):
    seq, tp = mesh.shape["seq"], mesh.shape["tp"]
    if (seq, tp) == (8, 4):
        shape, names = (2, 2, 2, 2, 2), ("zh", "zl", "x", "y", "c")
        mesh = Mesh(mesh.devices.reshape(shape), names)
        body, rows, cols = paired_on_device, SEQ, TP
    else:
        body, rows, cols = on_device, "seq", "tp"
    return jax.shard_map(
        body,
        mesh=mesh,
        in_specs=(
            P(rows, cols),
            P(cols),
            P(rows, None, cols),
            P(None, cols),
            P(rows, cols),
            P(cols),
            P(rows, cols),
            P(rows, cols),
            P(rows, cols),
            P(),
            P(rows, cols),
        ),
        out_specs=(
            P(rows, cols),
            P(rows, cols),
            P(cols),
            P(rows, None, cols),
            P(None, cols),
            P(rows, cols),
            P(cols),
            P(rows, cols),
            P(rows, cols),
            P(rows, cols),
            P(None, rows),
        ),
        check_vma=False,
    )
```

```python
import jax
import jax.numpy as jnp
from jax import lax
from jax.experimental import pallas as pl
from jax.experimental.pallas import tpu as pltpu
from jax.sharding import Mesh, PartitionSpec as P

epsilon = 1e-05


def from_behind(shard, axis, by):
    count = lax.axis_size(axis)
    pairs = [(i, i + by) for i in range(count) if 0 <= i + by < count]
    return lax.ppermute(shard, axis, pairs)


def doc_count(doc_starts, positions):
    return jnp.sum((doc_starts[None, :] <= positions[:, None]).astype(jnp.int32), axis=1)


def lag_masks(doc_starts, positions):
    current = doc_count(doc_starts, positions)
    one = (positions >= 1) & (doc_count(doc_starts, positions - 1) == current)
    two = (positions >= 2) & (doc_count(doc_starts, positions - 2) == current)
    return (one.astype(jnp.float32)[:, None], two.astype(jnp.float32)[:, None])


def contract_rows(left, right):
    return lax.dot_general(
        left, right, (((0,), (0,)), ((), ())), preferred_element_type=jnp.float32
    )


def contract_cols(left, right):
    return lax.dot_general(
        left, right, (((1,), (1,)), ((), ())), preferred_element_type=jnp.float32
    )


def reduce_tp(partial_rows):
    return lax.psum_scatter(
        partial_rows.astype(jnp.bfloat16), "tp", scatter_dimension=1, tiled=True
    ).astype(jnp.float32)


def reduce_seq(partial_grad):
    return lax.psum_scatter(
        partial_grad.astype(jnp.bfloat16), "seq", scatter_dimension=0, tiled=True
    ).astype(jnp.float32)


def gather_grads(grad_rows):
    return lax.all_gather(grad_rows, "tp", axis=1, tiled=True)


def normalize(values, gain):
    width = gain.shape[0] * lax.axis_size("tp")
    squares = lax.psum(jnp.sum(values * values, axis=1, keepdims=True), "tp")
    inverse = lax.rsqrt(squares / width + epsilon)
    normed = lax.all_gather(
        (values * inverse * gain).astype(jnp.bfloat16), "tp", axis=1, tiled=True
    )
    return (normed, inverse, jnp.sqrt(squares[:, 0] / width + epsilon))


def norm_backward(values, gain, inverse, grad_rows):
    width = gain.shape[0] * lax.axis_size("tp")
    gained = gain * grad_rows
    total = lax.psum(jnp.sum(values * gained, axis=1, keepdims=True), "tp")
    grad_values = inverse * gained - values * inverse**3 * (total / width)
    grad_gain = jnp.sum(grad_rows * values * inverse, axis=0)
    return (grad_values, grad_gain)


def on_device(
    stream,
    norm1_gain,
    in_weight,
    conv_weight,
    out_weight,
    norm2_gain,
    gate_weight,
    up_weight,
    down_weight,
    doc_starts,
    out_grad,
):
    tokens = stream.shape[0]
    local = stream.shape[1]
    rows_here = in_weight.shape[0]
    whole_in, whole_out, whole_gate, whole_up, whole_down = (
        lax.all_gather(in_weight, "seq", axis=0, tiled=True),
        lax.all_gather(out_weight, "seq", axis=0, tiled=True),
        lax.all_gather(gate_weight, "seq", axis=0, tiled=True),
        lax.all_gather(up_weight, "seq", axis=0, tiled=True),
        lax.all_gather(down_weight, "seq", axis=0, tiled=True),
    )
    width = whole_out.shape[0]
    in_matrix = whole_in.reshape(width, 3 * local)
    positions = lax.axis_index("seq") * tokens + jnp.arange(tokens, dtype=jnp.int32)
    mask_one, mask_two = lag_masks(doc_starts, positions)
    normed_in, inverse_in, rms_in = normalize(stream, norm1_gain)
    projected = jnp.dot(normed_in, in_matrix, preferred_element_type=jnp.float32)
    in_gate = projected[:, :local]
    out_gate = projected[:, local : 2 * local]
    carried = projected[:, 2 * local :]
    mixed = in_gate * carried
    previous = from_behind(mixed[-2:], "seq", 1)
    extended = jnp.concatenate([previous, mixed], axis=0)
    convolved = (
        conv_weight[0] * mixed
        + mask_one * conv_weight[1] * extended[1:-1]
        + mask_two * conv_weight[2] * extended[:-2]
    )
    gated = (out_gate * convolved).astype(jnp.bfloat16)
    middle = stream + reduce_tp(contract_cols(gated, whole_out))
    normed_mid, inverse_mid, rms_mid = normalize(middle, norm2_gain)
    gate = jnp.dot(normed_mid, whole_gate, preferred_element_type=jnp.float32)
    upward = jnp.dot(normed_mid, whole_up, preferred_element_type=jnp.float32)
    hidden = (jax.nn.silu(gate) * upward).astype(jnp.bfloat16)
    result = middle + reduce_tp(contract_cols(hidden, whole_down))
    out_full = gather_grads(out_grad.astype(jnp.bfloat16))
    hidden_grad = jnp.dot(out_full, whole_down, preferred_element_type=jnp.float32)
    sigmoid_gate = jax.nn.sigmoid(gate)
    gate_rows = (hidden_grad * upward * sigmoid_gate * (1.0 + gate * (1.0 - sigmoid_gate))).astype(
        jnp.bfloat16
    )
    up_rows = (hidden_grad * gate * sigmoid_gate).astype(jnp.bfloat16)
    normed_mid_grad = reduce_tp(
        contract_cols(gate_rows, whole_gate) + contract_cols(up_rows, whole_up)
    )
    middle_norm_grad, gain_mid_grad = norm_backward(
        middle, norm2_gain, inverse_mid, normed_mid_grad
    )
    middle_grad = out_grad + middle_norm_grad
    branch_full = gather_grads(middle_grad.astype(jnp.bfloat16))
    gated_grad = jnp.dot(branch_full, whole_out, preferred_element_type=jnp.float32)
    out_gate_grad = gated_grad * convolved
    conv_grad = gated_grad * out_gate
    lag_one = mask_one * conv_grad
    lag_two = mask_two * conv_grad
    next_one, next_two = from_behind((lag_one[:2], lag_two[:2]), "seq", -1)
    after_one = jnp.concatenate([lag_one, next_one], axis=0)
    after_two = jnp.concatenate([lag_two, next_two], axis=0)
    mixed_grad = (
        conv_weight[0] * conv_grad
        + conv_weight[1] * after_one[1 : tokens + 1]
        + conv_weight[2] * after_two[2:]
    )
    tap_grads = jnp.stack(
        [
            jnp.sum(conv_grad * mixed, axis=0),
            jnp.sum(lag_one * extended[1:-1], axis=0),
            jnp.sum(lag_two * extended[:-2], axis=0),
        ]
    )
    projected_grad = jnp.concatenate(
        [mixed_grad * carried, out_gate_grad, mixed_grad * in_gate], axis=1
    ).astype(jnp.bfloat16)
    normed_in_grad = reduce_tp(contract_cols(projected_grad, in_matrix))
    stream_norm_grad, gain_in_grad = norm_backward(stream, norm1_gain, inverse_in, normed_in_grad)
    stream_grad = middle_grad + stream_norm_grad
    conv_total, gain_in_total, gain_mid_total = lax.psum(
        (tap_grads, gain_in_grad, gain_mid_grad), "seq"
    )
    down_weight_grad = reduce_seq(contract_rows(out_full, hidden))
    gate_weight_grad = reduce_seq(contract_rows(normed_mid, gate_rows))
    up_weight_grad = reduce_seq(contract_rows(normed_mid, up_rows))
    out_weight_grad = reduce_seq(contract_rows(branch_full, gated))
    in_weight_grad = reduce_seq(contract_rows(normed_in, projected_grad)).reshape(
        rows_here, 3, local
    )
    rms_values = jnp.stack([rms_in, rms_mid])
    return (
        result,
        stream_grad,
        gain_in_total,
        in_weight_grad,
        conv_total,
        out_weight_grad,
        gain_mid_total,
        gate_weight_grad,
        up_weight_grad,
        down_weight_grad,
        rms_values,
    )


MESH = pl.DeviceIdType.MESH
BF = jnp.bfloat16
F32 = jnp.float32
ANY = pl.BlockSpec(memory_space=pl.ANY)
VMEM = pl.BlockSpec(memory_space=pltpu.VMEM)
OWN, MATE, NEAR, FAR = 0, 1, 2, 3


def dot(left, right):
    return jnp.dot(left, right, preferred_element_type=F32)


def remote(src, dst, send_sem, recv_sem, device):
    return pltpu.make_async_remote_copy(
        src_ref=src,
        dst_ref=dst,
        send_sem=send_sem,
        recv_sem=recv_sem,
        device_id=device,
        device_id_type=MESH,
    )


class Place:
    def __init__(self):
        self.zh, self.zl = lax.axis_index("zh"), lax.axis_index("zl")
        self.x, self.y, self.c = lax.axis_index("x"), lax.axis_index("y"), lax.axis_index("c")
        self.z = 2 * self.zh + self.zl
        self.inner = (self.z == 1) | (self.z == 2)
        self.outer = (self.z == 0) | (self.z == 3)
        self.rows = [self.z, 2 * self.zh + 1 - self.zl, 2 - self.zh, 3 - 3 * self.zh]
        self.mate = (self.zh, 1 - self.zl, self.x, self.y, self.c)
        self.mid = (1 - self.zh, 1 - self.zl, self.x, self.y, self.c)
        self.across = (self.zh, self.zl, 1 - self.x, self.y, self.c)

    def block(self, which, x):
        return self.rows[which] * 2 + x

    def enter_all(self, devices):
        barrier = pltpu.get_barrier_semaphore()
        for device in devices:
            pl.semaphore_signal(barrier, inc=1, device_id=device, device_id_type=MESH)
        pl.semaphore_wait(barrier, len(devices))

    def enter(self, *others):
        barrier = pltpu.get_barrier_semaphore()

        def greet(device):
            pl.semaphore_signal(barrier, inc=1, device_id=device, device_id_type=MESH)

        greet(self.mate)
        greet(self.across)
        for device in others:
            greet(device)

        @pl.when(self.inner)
        def _():
            greet(self.mid)

        @pl.when(self.inner)
        def _():
            pl.semaphore_wait(barrier, 3 + len(others))

        @pl.when(self.outer)
        def _():
            pl.semaphore_wait(barrier, 2 + len(others))


def pair_gather_chunk(p, weight, out, relay, ss, rs, first, count, rows):
    half = out.shape[1]
    here = pl.ds(first, count)
    own = weight.at[here, pl.ds(pl.multiple_of(p.zl * half, half), half)]
    other = weight.at[here, pl.ds(pl.multiple_of((1 - p.zl) * half, half), half)]

    def block(which, x):
        return out.at[pl.ds(pl.multiple_of(p.block(which, x) * rows + first, count), count), :]

    held = [relay.at[i, here, :] for i in range(3)]

    def send(slot, src, dst, recv, device):
        return remote(src, dst, ss.at[slot], rs.at[recv], device)

    def arrived(recv, dst):
        remote(dst, dst, ss.at[0], rs.at[recv], p.mate).wait_recv()

    local = pltpu.make_async_copy(own, block(OWN, p.x), ss.at[11])
    across = [
        send(7 + k, own if k == OWN else block(k, p.x), block(k, p.x), 6 + k, p.across)
        for k in range(4)
    ]
    to_mate = send(0, other, block(OWN, p.x), 0, p.mate)
    outer_own = send(1, own, held[0], 3, p.mate)
    mid_other = send(3, other, block(OWN, p.x), 1, p.mid)
    mid_own = send(4, own, held[1], 4, p.mid)
    mid_far = send(5, held[0], block(MATE, p.x), 2, p.mid)
    mid_far_own = send(6, block(MATE, p.x), held[2], 5, p.mid)
    back_near = send(1, held[1], block(NEAR, p.x), 1, p.mate)
    back_far = send(2, held[2], block(FAR, p.x), 2, p.mate)

    def begin():
        @pl.when(p.inner)
        def _():
            mid_other.start()
            mid_own.start()

        to_mate.start()

        @pl.when(p.outer)
        def _():
            outer_own.start()

        across[OWN].start()
        local.start()

    def mate_here():
        arrived(0, block(MATE, p.x))

        @pl.when(p.inner)
        def _():
            arrived(3, held[0])
            mid_far.start()
            mid_far_own.start()
            arrived(4, held[1])
            back_near.start()

        across[MATE].start()

    def near_here():
        arrived(1, block(NEAR, p.x))
        across[NEAR].start()

        @pl.when(p.inner)
        def _():
            arrived(5, held[2])
            back_far.start()

    def far_here():
        arrived(2, block(FAR, p.x))
        across[FAR].start()

    def finish():
        for k in range(4):
            arrived(6 + k, block(k, 1 - p.x))
            across[k].wait_send()
        local.wait()
        to_mate.wait_send()

        @pl.when(p.inner)
        def _():
            for copy in (mid_other, mid_own, mid_far, mid_far_own, back_near, back_far):
                copy.wait_send()

        @pl.when(p.outer)
        def _():
            outer_own.wait_send()

    return [begin, mate_here, near_here, far_here, finish]


def line_gather_chunk(p, weight, out, ss, rs, first, count, rows):
    own = weight.at[pl.ds(first, count), :]

    def block(which, x):
        return out.at[pl.ds(pl.multiple_of(p.block(which, x) * rows + first, count), count), :]

    def send(slot, src, dst, recv, device):
        return remote(src, dst, ss.at[slot], rs.at[recv], device)

    def arrived(recv, dst):
        remote(dst, dst, ss.at[0], rs.at[recv], p.mate).wait_recv()

    local = pltpu.make_async_copy(own, block(OWN, p.x), ss.at[9])
    across = [
        send(k, own if k == OWN else block(k, p.x), block(k, p.x), 3 + k, p.across)
        for k in range(4)
    ]
    to_mate = send(4, own, block(OWN, p.x), MATE - 1, p.mate)
    to_mid = send(5, own, block(OWN, p.x), NEAR - 1, p.mid)
    mid_far = send(6, block(MATE, p.x), block(MATE, p.x), FAR - 1, p.mid)
    back_near = send(7, block(NEAR, p.x), block(NEAR, p.x), NEAR - 1, p.mate)
    back_far = send(8, block(FAR, p.x), block(FAR, p.x), FAR - 1, p.mate)

    def begin():
        @pl.when(p.inner)
        def _():
            to_mid.start()

        to_mate.start()
        across[OWN].start()
        local.start()

    def mate_here():
        arrived(MATE - 1, block(MATE, p.x))

        @pl.when(p.inner)
        def _():
            mid_far.start()

        across[MATE].start()

    def near_here():
        arrived(NEAR - 1, block(NEAR, p.x))

        @pl.when(p.inner)
        def _():
            back_near.start()

        across[NEAR].start()

    def far_here():
        arrived(FAR - 1, block(FAR, p.x))

        @pl.when(p.inner)
        def _():
            back_far.start()

        across[FAR].start()

    def finish():
        for k in range(4):
            arrived(3 + k, block(k, 1 - p.x))
            across[k].wait_send()
        local.wait()
        to_mate.wait_send()

        @pl.when(p.inner)
        def _():
            for copy in (to_mid, mid_far, back_near, back_far):
                copy.wait_send()

    return [begin, mate_here, near_here, far_here, finish]


def contract_tokens(left, right):
    return lax.dot_general(left, right, (((0,), (0,)), ((), ())), preferred_element_type=F32)


class PairScatter:
    def __init__(self, p, product, sx, rx, sz, rz, rm, held, out, ss, rs):
        self.p, self.product = p, product
        self.sx, self.rx, self.sz, self.rz, self.rm = sx, rx, sz, rz, rm
        self.held, self.out, self.ss, self.rs = held, out, ss, rs
        self.half = held.shape[1]

    def across(self, k):
        return remote(self.sx.at[k], self.rx.at[k], self.ss.at[k], self.rs.at[k], self.p.across)

    def outward(self, j):
        return remote(self.sz.at[j], self.rz.at[j], self.ss.at[4 + j], self.rs.at[4 + j], self.p.mate)

    def middle(self, j):
        return remote(self.sz.at[j], self.rm.at[j], self.ss.at[7 + j], self.rs.at[7 + j], self.p.mid)

    def relay(self, j):
        return remote(
            self.rz.at[j], self.rm.at[2 + j], self.ss.at[9 + j], self.rs.at[9 + j], self.p.mid
        )

    def forward(self):
        return remote(self.rm.at[0], self.rz.at[0], self.ss.at[4], self.rs.at[4], self.p.mate)

    def back(self):
        return remote(self.sz.at[2], self.rz.at[1], self.ss.at[5], self.rs.at[5], self.p.mate)

    def cols_of(self, place):
        return pl.ds(pl.multiple_of(place * self.half, self.half), self.half)

    def send_across(self, k, *sent):
        self.sx[k] = self.product(k, 1 - self.p.x).astype(BF)
        self.sent(*sent)
        self.across(k).start()

    def summed(self, k):
        total = self.product(k, self.p.x)
        self.across(k).wait_recv()
        return total + self.rx[k].astype(F32)

    def send_on(self, k, j):
        self.sz[j] = self.summed(k).astype(BF)

        @pl.when(self.p.outer)
        def _():
            self.outward(j).start()

        @pl.when(self.p.inner)
        def _():
            self.middle(j).start()

    def send_relay(self, j):
        @pl.when(self.p.inner)
        def _():
            self.outward(j).wait_recv()
            self.relay(j).start()

    def mate_rows(self):
        total = self.summed(MATE)

        @pl.when(self.p.outer)
        def _():
            self.sz[2] = total.astype(BF)
            self.outward(2).start()

        @pl.when(self.p.inner)
        def _():
            self.held[...] = total

    def send_forward(self):
        @pl.when(self.p.inner)
        def _():
            self.middle(0).wait_recv()
            self.forward().start()

    def own_rows(self):
        self.out[:, self.cols_of(self.p.zl)] = self.summed(OWN)

    def send_back(self):
        @pl.when(self.p.inner)
        def _():
            self.relay(0).wait_recv()
            self.sz[2] = (self.held[...] + self.rm[2].astype(F32)).astype(BF)
            self.back().start()

    def finish(self):
        p, out = self.p, self.out
        here, there = self.cols_of(p.zl), self.cols_of(1 - p.zl)

        @pl.when(p.inner)
        def _():
            self.relay(1).wait_recv()
            out[:, here] = out[:, here] + self.rm[3].astype(F32)
            self.outward(2).wait_recv()
            self.middle(1).wait_recv()
            out[:, there] = self.rz[2].astype(F32) + self.rm[1].astype(F32)

        @pl.when(p.outer)
        def _():
            self.forward().wait_recv()
            out[:, here] = out[:, here] + self.rz[0].astype(F32)
            self.back().wait_recv()
            out[:, there] = self.rz[1].astype(F32)

        @pl.when(p.inner)
        def _():
            for j in range(2):
                self.relay(j).wait_send()
            self.forward().wait_send()

    def sent_on(self, j):
        @pl.when(self.p.outer)
        def _():
            self.outward(j).wait_send()

        @pl.when(self.p.inner)
        def _():
            (self.back() if j == 2 else self.middle(j)).wait_send()

    def sent(self, *which):
        for k in which:
            self.across(k).wait_send()


def pair_scatter_scratch(n, rows, half):
    return [
        pltpu.VMEM((4, rows, half), BF),
        pltpu.VMEM((n, 4, rows, half), BF),
        pltpu.VMEM((3, rows, half), BF),
        pltpu.VMEM((n, 3, rows, half), BF),
        pltpu.VMEM((n, 4, rows, half), BF),
        pltpu.VMEM((rows, half), F32),
        pltpu.SemaphoreType.DMA((n, 11)),
        pltpu.SemaphoreType.DMA((n, 11)),
    ]


class Columns:
    def __init__(self, p, jobs, buffer, sems):
        self.p, self.jobs, self.buffer, self.sems, self.at = p, jobs, buffer, sems, 0
        for n in range(min(2, len(jobs))):
            self.copies(n, "start")

    def copies(self, n, act):
        array, k, flip = self.jobs[n]
        pair, _, tokens, local = array.shape
        rows = self.buffer.shape[2]
        start = self.p.block(k, 1 - self.p.x if flip else self.p.x) * rows
        cols = pl.ds(pl.multiple_of(start % local, rows), rows)
        for q in range(pair):
            copy = pltpu.make_async_copy(
                array.at[q, start // local, :, cols],
                self.buffer.at[n % 2, pl.ds(q * tokens, tokens), :],
                self.sems.at[n % 2, q],
            )
            getattr(copy, act)()

    def times(self, right):
        return self.times_next(right, True, True)

    def times_next(self, right, first, last):
        if first:
            self.at += 1
            self.copies(self.at - 1, "wait")
        n = self.at - 1
        tokens = self.jobs[n][0].shape[0] * self.jobs[n][0].shape[2]
        product = contract_tokens(self.buffer[n % 2, :tokens, :], right)
        if last and n + 2 < len(self.jobs):
            self.copies(n + 2, "start")
        return product


ORDER = (FAR, NEAR, MATE, OWN)


class Spread:
    def __init__(self, p, view, ss, rs):
        self.p = p
        self.view, self.ss, self.rs = view, ss, rs

    def to_core(self):
        block = self.view(self.p.me)
        return remote(block, block, self.ss.at[0], self.rs.at[0], self.p.core)

    def to_side(self):
        block = self.view(self.p.me)
        return remote(block, block, self.ss.at[1], self.rs.at[1], self.p.side)

    def on_to_core(self):
        block = self.view(self.p.side_owner)
        return remote(block, block, self.ss.at[2], self.rs.at[2], self.p.core)

    def start(self):
        self.to_side().start()
        self.to_core().start()

    def forward(self):
        self.to_side().wait_recv()
        self.on_to_core().start()

    def finish(self):
        self.to_core().wait_recv()
        self.on_to_core().wait_recv()
        self.to_core().wait_send()
        self.to_side().wait_send()
        self.on_to_core().wait_send()


def lanes_of(column):
    return jnp.broadcast_to(column, (column.shape[0], 128)).T[:8]


def column_of(lanes):
    return jnp.broadcast_to(lanes[:1], (128, lanes.shape[1])).T[:, :1]


def block_forward(
    stream, masks, conv_weight, first_gain, gain, in_weight, out_weight, gate_weight, up_weight,
    down_weight, collective,
):
    tokens, local = stream.shape
    rows, width = gate_weight.shape
    half = width // 2
    three = in_weight.shape[1]
    owners, pair = 4, 2
    features = owners * local
    tile = tokens // 4
    plan = [("in", rows // 4)] * 4 + [("out", rows)]
    plan += [(name, rows // 4) for name in ("gate", "up", "down") for _ in range(4)]
    n_chunks = len(plan)

    def kernel(*refs):
        stream_ref, masks_ref, conv_ref, first_gain_ref, gain_ref = refs[:5]
        in_ref, out_ref, gate_ref, up_ref, down_ref = refs[5:10]
        in_all, out_all, gate_all, up_all, down_all = refs[10:15]
        normed_all, projected_all, convolved_all, gated_all, mid_all = refs[15:20]
        hidden_all, silu_all, slope_all, mixed_all, middle, squares = refs[20:26]
        first_squares, refs = refs[26], refs[:26] + refs[27:]
        x, in_vm, out_vm, gate_vm, up_vm, projected, mixed, convolved, gated = refs[26:35]
        to_core, sums, from_y, near_squares, mid, results, relay = refs[35:42]
        halo, first_near, first_ss, first_rs = refs[55:]
        chunk_ss, chunk_rs, x_ss, x_rs, mid_ss, mid_rs, move_ss, move_rs = refs[42:50]
        square_ss, square_rs, halo_sem, store_sem, result_sem = refs[50:55]

        p = Place()
        p.core = (p.zh, p.zl, p.x, p.y, 1 - p.c)
        p.side = (p.zh, p.zl, p.x, 1 - p.y, p.c)
        diagonal = (p.zh, p.zl, p.x, 1 - p.y, 1 - p.c)
        p.me, p.side_owner = 2 * p.y + p.c, 2 * (1 - p.y) + p.c
        place = 2 * p.z + p.x
        last = 2 * 4 - 1

        def device_at(s):
            return (s // 4, s // 2 % 2, s % 2, p.y, p.c)

        following, previous = device_at(lax.rem(place + 1, 8)), device_at(lax.rem(place + 7, 8))
        p.enter(p.core, p.side, diagonal, following, previous)

        chunks = []
        firsts = {}
        targets = {
            "in": (in_ref, in_vm), "out": (out_ref, out_vm), "gate": (gate_ref, gate_vm),
            "up": (up_ref, up_vm), "down": (down_ref, down_all),
        }
        for c, (name, count) in enumerate(plan):
            first = firsts.get(name, 0)
            firsts[name] = first + count
            source, target = targets[name]
            if name in ("in", "out"):
                chunk = line_gather_chunk(
                    p, source, target, chunk_ss.at[c], chunk_rs.at[c], first, count, rows
                )
            else:
                held = relay.at[("gate", "up", "down").index(name)]
                chunk = pair_gather_chunk(
                    p, source, target, held, chunk_ss.at[c], chunk_rs.at[c], first, count, rows
                )
            chunks.append(chunk)

        def pump(step):
            for c in range(3) if step == 0 else [step + 2]:
                if c < n_chunks:
                    chunks[c][0]()
            for stage in range(1, 5):
                if 0 <= step - stage < n_chunks:
                    chunks[step - stage][stage]()

        stores = []

        def store(source, target):
            copy = pltpu.make_async_copy(source, target, store_sem.at[1 + len(stores)])
            copy.start()
            stores.append(copy)

        spread_x = Spread(p, lambda owner: x.at[owner], x_ss, x_rs)

        def project(t):
            here = pl.ds(t * tile, tile)
            value = sum(
                dot(x[j, here, :], in_vm[j * local : (j + 1) * local, :]) for j in range(owners)
            )
            projected[here, :] = value
            mixed[pl.ds(8 + t * tile, tile), :] = value[:, :local] * value[:, 2 * local :]

        def halo_copy():
            return remote(
                mixed.at[pl.ds(tokens, 8), :], halo, halo_sem.at[0], halo_sem.at[1], following
            )

        def send_halo():
            @pl.when(place < last)
            def _():
                halo_copy().start()

        def take_halo():
            @pl.when(place > 0)
            def _():
                halo_copy().wait_recv()

            @pl.when(place == 0)
            def _():
                halo[...] = jnp.zeros_like(halo)

            mixed[:8, :] = halo[...]

        def convolve(t):
            here = pl.ds(t * tile, tile)
            value = (
                conv_ref[0:1, :] * mixed[pl.ds(8 + t * tile, tile), :]
                + masks_ref[0, here, :] * conv_ref[1:2, :] * mixed[pl.ds(7 + t * tile, tile), :]
                + masks_ref[1, here, :] * conv_ref[2:3, :] * mixed[pl.ds(6 + t * tile, tile), :]
            )
            convolved[here, :] = value
            gated[here, :] = (projected[here, local : 2 * local] * value).astype(BF)

        owner = [
            2 * (1 - p.y) + 1 - p.c, 2 * (1 - p.y) + p.c, 2 * p.y + 1 - p.c, 2 * p.y + p.c
        ]

        def core_copy(b, t):
            return remote(
                to_core.at[b, t], sums.at[b, t], move_ss.at[b, t], move_rs.at[b, t], p.core
            )

        def side_copy(t):
            return remote(sums.at[0, t], from_y.at[t], move_ss.at[2, t], move_rs.at[2, t], p.side)

        def mixer_out(n):
            out_rows = pl.ds(pl.multiple_of(owner[n] * local, local), local)
            for t in range(4):
                here = pl.ds(t * tile, tile)
                value = contract_cols(gated[here, :], out_vm[out_rows, :])
                b = n // 2
                if n % 2 == 0:
                    to_core[b, t] = value.astype(BF)
                    core_copy(b, t).start()
                else:
                    core_copy(b, t).wait_recv()
                    value = value + sums[b, t].astype(F32)
                    if b == 0:
                        sums[b, t] = value.astype(BF)
                        side_copy(t).start()
                    else:
                        middle[here, :] = stream_ref[here, :] + value

        def residual(t):
            here = pl.ds(t * tile, tile)
            side_copy(t).wait_recv()
            value = middle[here, :] + from_y[t].astype(F32)
            middle[here, :] = value
            squares[:, here] = lanes_of(jnp.sum(value * value, axis=1, keepdims=True))

        def square_copies(mine, near, send_sems, recv_sems):
            return [
                remote(mine, near.at[i], send_sems.at[i], recv_sems.at[i], device)
                for i, device in enumerate((p.core, p.side, diagonal))
            ]

        def sum_squares(mine, near, *sems):
            for copy in square_copies(mine, near, *sems):
                copy.wait_recv()
                copy.wait_send()
            mine[...] = mine[...] + near[0] + near[1] + near[2]

        first = (first_squares, first_near, first_ss, first_rs)
        second = (squares, near_squares, square_ss, square_rs)

        def first_sums():
            for t in range(4):
                here = pl.ds(t * tile, tile)
                value = stream_ref[here, :]
                first_squares[:, here] = lanes_of(jnp.sum(value * value, axis=1, keepdims=True))
            for copy in square_copies(*first):
                copy.start()

        def first_norm():
            sum_squares(*first)
            for t in range(4):
                here = pl.ds(t * tile, tile)
                inverse = lax.rsqrt(first_squares[:, here] / features + epsilon)
                value = stream_ref[here, :] * column_of(inverse) * first_gain_ref[...]
                x[p.me, here, :] = value.astype(BF)

        def own_tile(t):
            return lambda who: mid.at[p.zl, who, pl.ds(t * tile, tile), :]

        def mate_tile(t):
            return lambda who: mid.at[1 - p.zl, who, pl.ds(t * tile, tile), :]

        spread_own = [Spread(p, own_tile(t), mid_ss.at[0, t], mid_rs.at[0, t]) for t in range(4)]
        spread_mate = [Spread(p, mate_tile(t), mid_ss.at[1, t], mid_rs.at[1, t]) for t in range(4)]

        def mate_send(t):
            block = own_tile(t)(p.me)
            return remote(block, block, mid_ss.at[0, t, 3], mid_rs.at[0, t, 3], p.mate)

        def normalize_mid(t):
            here = pl.ds(t * tile, tile)
            inverse = lax.rsqrt(squares[:, here] / features + epsilon)
            value = middle[here, :] * column_of(inverse) * gain_ref[...]
            mid[p.zl, p.me, here, :] = value.astype(BF)
            mate_send(t).start()
            spread_own[t].start()

        def pass_on(t):
            spread_own[t].forward()
            mate_send(t).wait_recv()
            spread_mate[t].start()

        def result_stores(m, act):
            start = pl.multiple_of(tile_place(m) * tile, tile)
            for i, ref in enumerate((hidden_all, silu_all, slope_all)):
                copy = pltpu.make_async_copy(
                    results.at[m % 2, i], ref.at[pl.ds(start, tile), :], result_sem.at[m % 2, i]
                )
                getattr(copy, act)()

        def tile_place(m):
            return (p.zl if m < 4 else 1 - p.zl) * 4 + m % 4

        def hidden_units(m):
            q = p.zl if m < 4 else 1 - p.zl
            here = pl.ds(m % 4 * tile, tile)
            (spread_own if m < 4 else spread_mate)[m % 4].finish()
            if m >= 2:
                result_stores(m - 2, "wait")
            for part in range(2):
                cols = pl.ds(part * half // 2, half // 2)
                value = sum(
                    dot(mid[q, j, here, :], gate_vm[j * local : (j + 1) * local, cols])
                    for j in range(owners)
                )
                upward = sum(
                    dot(mid[q, j, here, :], up_vm[j * local : (j + 1) * local, cols])
                    for j in range(owners)
                )
                sigmoid = jax.nn.sigmoid(value)
                silu = value * sigmoid
                results[m % 2, 0, :, cols] = (silu * upward).astype(BF)
                results[m % 2, 1, :, cols] = silu.astype(BF)
                results[m % 2, 2, :, cols] = (upward * (sigmoid + silu * (1.0 - sigmoid))).astype(BF)
            result_stores(m, "start")

        pump(0)
        first_sums()
        first_norm()
        spread_x.start()
        pump(1)
        pump(2)
        spread_x.forward()
        pump(3)
        pump(4)
        pump(5)
        spread_x.finish()
        pump(6)
        pump(7)
        store(x, normed_all)
        store(in_vm, in_all)
        project(3)
        send_halo()
        project(2)
        pump(8)
        project(1)
        project(0)
        store(projected, projected_all)
        store(out_vm, out_all)
        pump(9)
        take_halo()
        for t in range(4):
            convolve(t)
        store(convolved, convolved_all)
        store(mixed, mixed_all)
        store(gated, gated_all)
        mixer_out(0)
        mixer_out(1)
        pump(10)
        mixer_out(2)
        mixer_out(3)
        pump(11)
        residual(0)
        residual(1)
        pump(12)
        store(gate_vm, gate_all)
        residual(2)
        residual(3)
        for copy in square_copies(*second):
            copy.start()
        pump(13)
        sum_squares(*second)
        for t in range(4):
            normalize_mid(t)
        pump(14)
        pass_on(0)
        pass_on(1)
        pump(15)
        pass_on(2)
        pass_on(3)
        pump(16)
        store(up_vm, up_all)
        hidden_units(0)
        hidden_units(1)
        pump(17)
        hidden_units(2)
        for t in range(4):
            spread_mate[t].forward()
        pump(18)
        hidden_units(3)
        hidden_units(4)
        hidden_units(5)
        pump(19)
        hidden_units(6)
        hidden_units(7)
        store(mid, mid_all)
        pump(20)
        result_stores(6, "wait")
        result_stores(7, "wait")
        for copy in stores:
            copy.wait()
        for t in range(4):
            core_copy(0, t).wait_send()
            core_copy(1, t).wait_send()
            side_copy(t).wait_send()
            mate_send(t).wait_send()

        @pl.when(place < last)
        def _():
            halo_copy().wait_send()

    def array(*shape, dtype=BF):
        return jax.ShapeDtypeStruct(shape, dtype)

    units = array(pair * tokens, half)
    outs = [
        (array(8 * rows, three), ANY), (array(8 * rows, local), ANY),
        (array(8 * rows, half), ANY), (array(8 * rows, half), ANY), (array(8 * rows, half), ANY),
        (array(owners, tokens, local), ANY), (array(tokens, three, dtype=F32), ANY),
        (array(tokens, local, dtype=F32), ANY), (array(tokens, local), ANY),
        (array(pair, owners, tokens, local), ANY),
        (units, ANY), (units, ANY), (units, ANY),
        (array(8 + tokens, local, dtype=F32), ANY),
        (array(tokens, local, dtype=F32), VMEM), (array(8, tokens, dtype=F32), VMEM),
        (array(8, tokens, dtype=F32), VMEM),
    ]
    return pl.pallas_call(
        kernel,
        out_shape=[o[0] for o in outs],
        in_specs=[VMEM] * 5 + [ANY] * 5,
        out_specs=[o[1] for o in outs],
        scratch_shapes=[
            pltpu.VMEM((owners, tokens, local), BF),
            pltpu.VMEM((8 * rows, three), BF),
            pltpu.VMEM((8 * rows, local), BF),
            pltpu.VMEM((8 * rows, half), BF),
            pltpu.VMEM((8 * rows, half), BF),
            pltpu.VMEM((tokens, three), F32),
            pltpu.VMEM((8 + tokens, local), F32),
            pltpu.VMEM((tokens, local), F32),
            pltpu.VMEM((tokens, local), BF),
            pltpu.VMEM((2, 4, tile, local), BF),
            pltpu.VMEM((2, 4, tile, local), BF),
            pltpu.VMEM((4, tile, local), BF),
            pltpu.VMEM((3, 8, tokens), F32),
            pltpu.VMEM((pair, owners, tokens, local), BF),
            pltpu.VMEM((2, 3, tile, half), BF),
            pltpu.VMEM((3, 3, rows, half), BF),
            pltpu.SemaphoreType.DMA((n_chunks, 12)),
            pltpu.SemaphoreType.DMA((n_chunks, 10)),
            pltpu.SemaphoreType.DMA((3,)),
            pltpu.SemaphoreType.DMA((3,)),
            pltpu.SemaphoreType.DMA((2, 4, 4)),
            pltpu.SemaphoreType.DMA((2, 4, 4)),
            pltpu.SemaphoreType.DMA((3, 4)),
            pltpu.SemaphoreType.DMA((3, 4)),
            pltpu.SemaphoreType.DMA((3,)),
            pltpu.SemaphoreType.DMA((3,)),
            pltpu.SemaphoreType.DMA((2,)),
            pltpu.SemaphoreType.DMA((12,)),
            pltpu.SemaphoreType.DMA((2, 3)),
            pltpu.VMEM((8, local), F32),
            pltpu.VMEM((3, 8, tokens), F32),
            pltpu.SemaphoreType.DMA((3,)),
            pltpu.SemaphoreType.DMA((3,)),
        ],
        compiler_params=pltpu.CompilerParams(
            collective_id=collective, has_side_effects=True, vmem_limit_bytes=62 << 20
        ),
        cost_estimate=pl.CostEstimate(flops=0, bytes_accessed=600 << 20, transcendentals=0),
        name="block_forward",
    )(
        stream, masks, conv_weight, first_gain, gain, in_weight, out_weight, gate_weight, up_weight,
        down_weight,
    )


def feed_forward_backward(
    out_rows, normed, hidden, silu, slope, gate, up, down, middle, out_grad, squares, gain, collective
):
    pair, owners, tokens, local = normed.shape
    total, half = hidden.shape
    rows = owners * local // 8
    tile = total // 8
    piece = total // 4

    def kernel(*refs):
        out_ref, normed_ref, hidden_ref, silu_ref, slope_ref, gate_ref, up_ref, down_ref = refs[:8]
        middle_ref, out_grad_ref, squares_ref, gain_ref = refs[8:12]
        middle_grad, branch_all, gain_grad, partials, down_grad_all, gate_grad_all, up_rows = refs[12:19]
        gate_rows, weights, cols, early, to_core, sums, from_y, from_mate, lanes = refs[19:28]
        near_lanes, residual, weight_grad, cols_sem, early_sem, weights_sem, move_ss, move_rs = refs[28:36]
        lanes_ss, lanes_rs, branch_ss, branch_rs, tile_sem = refs[36:41]
        sx, rx, sz, rz, rm, held, ss, rs = refs[41:]
        p = Place()
        p.core = (p.zh, p.zl, p.x, p.y, 1 - p.c)
        p.side = (p.zh, p.zl, p.x, 1 - p.y, p.c)
        diagonal = (p.zh, p.zl, p.x, 1 - p.y, 1 - p.c)
        p.me, p.side_owner = 2 * p.y + p.c, 2 * (1 - p.y) + p.c

        down_load = pltpu.make_async_copy(down_ref, weights, weights_sem.at[0])
        down_load.start()

        def tile_loads(m, act):
            start = m % (8 // pair) * tile
            copies = [
                (
                    out_ref.at[m // (8 // pair), j, pl.ds(start, tile), :],
                    early.at[m % 2, pl.ds(j * tile, tile), :],
                )
                for j in range(owners)
            ]
            copies += [
                (
                    ref.at[pl.ds(m * tile, tile), pl.ds(part * local, local)],
                    early.at[2 + m % 2, pl.ds((2 * i + part) * tile, tile), :],
                )
                for i, ref in enumerate((silu_ref, slope_ref))
                for part in range(2)
            ]
            for i, (source, target) in enumerate(copies):
                getattr(pltpu.make_async_copy(source, target, early_sem.at[m % 2, i]), act)()

        quarter = tokens // 4
        D = (out_ref, normed_ref)
        jobs = [(D[0], k, True) for k in ORDER]
        jobs += [(D[0], FAR, False), (D[0], NEAR, False), (D[0], MATE, False)]
        jobs += [(D[1], FAR, True), (D[1], NEAR, True), (D[0], OWN, False)]
        jobs += [(D[1], MATE, True), (D[1], OWN, True)]
        jobs += [(D[1], k, False) for k in ORDER]
        feed = Columns(p, jobs, cols, cols_sem)
        tile_loads(0, "start")
        tile_loads(1, "start")
        p.enter(p.core, p.side, diagonal)

        dm = PairScatter(
            p, lambda k, x: feed.times(hidden_ref[...]), sx, rx.at[0], sz, rz.at[0],
            rm.at[0], held, weight_grad, ss.at[0], rs.at[0],
        )
        gm = PairScatter(
            p, lambda k, x: feed.times(gate_rows[...]), sx, rx.at[1], sz, rz.at[1],
            rm.at[1], held, weight_grad, ss.at[1], rs.at[1],
        )

        def rows_backward(m):
            tile_loads(m, "wait")
            here = pl.ds(m * tile, tile)
            hidden_grad = sum(
                dot(
                    early[m % 2, j * tile : (j + 1) * tile, :],
                    weights[j * local : (j + 1) * local, :],
                )
                for j in range(owners)
            )
            for part in range(2):
                units = pl.ds(part * local, local)
                value = hidden_grad[:, part * local : (part + 1) * local]
                for i, ref in enumerate((up_rows, gate_rows)):
                    first = (2 * i + part) * tile
                    factor = early[2 + m % 2, first : first + tile, :]
                    ref[here, units] = (value * factor.astype(F32)).astype(BF)
            if m + 2 < 8:
                tile_loads(m + 2, "start")

        owner = [
            2 * (1 - p.y) + 1 - p.c, 2 * (1 - p.y) + p.c, 2 * p.y + 1 - p.c, 2 * p.y + p.c
        ]

        def weight_loads(n, act):
            start = pl.multiple_of(owner[n] * local, local)
            for i, ref in enumerate((gate_ref, up_ref)):
                copy = pltpu.make_async_copy(
                    ref.at[pl.ds(start, local), :],
                    weights.at[pl.ds((n % 2 * 2 + i) * local, local), :],
                    weights_sem.at[1 + n % 2 * 2 + i],
                )
                getattr(copy, act)()

        def piece_rows(t):
            place = p.zl if t >= 2 else 1 - p.zl
            return pl.ds(pl.multiple_of(place * tokens + t % 2 * piece, piece), piece)

        def core_copy(b, t):
            return remote(
                to_core.at[t], sums.at[b, t], move_ss.at[b, t], move_rs.at[b, t], p.core
            )

        def side_copy(t):
            return remote(sums.at[0, t], from_y.at[t], move_ss.at[2, t], move_rs.at[2, t], p.side)

        def mate_copy(t):
            return remote(sums.at[1, t], from_mate.at[t], move_ss.at[3, t], move_rs.at[3, t], p.mate)

        def partial_sum(n, t):
            here = piece_rows(t)
            first = n % 2 * 2 * local
            return contract_cols(gate_rows[here, :], weights[first : first + local, :]) + contract_cols(
                up_rows[here, :], weights[first + local : first + 2 * local, :]
            )

        def partial_block(n):
            weight_loads(n, "wait")
            for t in range(4):
                value = partial_sum(n, t)
                b = n // 2
                if n % 2 == 0:
                    if b == 1:
                        core_copy(0, t).wait_send()
                    to_core[t] = value.astype(BF)
                    core_copy(b, t).start()
                else:
                    core_copy(b, t).wait_recv()
                    sums[b, t] = (value + sums[b, t].astype(F32)).astype(BF)
                    if b == 0:
                        side_copy(t).start()
            if n + 2 < 4:
                weight_loads(n + 2, "start")

        def to_mate(t):
            side_copy(t).wait_recv()
            sums[1, t] = (sums[1, t].astype(F32) + from_y[t].astype(F32)).astype(BF)
            mate_copy(t).start()

        def final(t):
            side_copy(t).wait_recv()
            mate_copy(t - 2).wait_recv()
            middle_grad[pl.ds((t - 2) * piece, piece), :] = (
                sums[1, t].astype(F32) + from_y[t].astype(F32) + from_mate[t - 2].astype(F32)
            )

        def lane_copies():
            return [
                remote(lanes, near_lanes.at[i], lanes_ss.at[i], lanes_rs.at[i], device)
                for i, device in enumerate((p.core, p.side, diagonal))
            ]

        inverse_lanes = lax.rsqrt(squares_ref[...] / (owners * local) + epsilon)

        def residual_loads(n, act):
            here = pl.ds(n % 4 * quarter, quarter)
            for i, ref in enumerate((middle_ref, out_grad_ref)):
                copy = pltpu.make_async_copy(ref.at[here, :], residual.at[n % 2, i], tile_sem.at[n % 2, i])
                getattr(copy, act)()

        def row_sums():
            total = jnp.zeros((1, local), F32)
            for t in range(4):
                here = pl.ds(t * quarter, quarter)
                residual_loads(t, "wait")
                product = middle_grad[here, :] * residual[t % 2, 0]
                residual_loads(t + 2, "start")
                lanes[:, here] = lanes_of(
                    jnp.sum(product * gain_ref[...], axis=1, keepdims=True)
                )
                inverse = column_of(inverse_lanes[:, t * quarter : (t + 1) * quarter])
                total = total + jnp.sum(product * inverse, axis=0, keepdims=True)
            gain_grad[...] = total
            for copy in lane_copies():
                copy.start()

        spreads = [
            Spread(
                p,
                lambda who, t=t: early.at[who, pl.ds(t * quarter, quarter), :],
                branch_ss.at[t],
                branch_rs.at[t],
            )
            for t in range(4)
        ]

        def residual_grad():
            for copy in lane_copies():
                copy.wait_recv()
            sums_all = (lanes[...] + near_lanes[0] + near_lanes[1] + near_lanes[2]) / (owners * local)
            scale_all = inverse_lanes * inverse_lanes * inverse_lanes * sums_all
            for t in range(4):
                here = pl.ds(t * quarter, quarter)
                part = slice(t * quarter, (t + 1) * quarter)
                residual_loads(4 + t, "wait")
                value = (
                    residual[t % 2, 1]
                    + column_of(inverse_lanes[:, part]) * gain_ref[...] * middle_grad[here, :]
                    - residual[t % 2, 0] * column_of(scale_all[:, part])
                )
                middle_grad[here, :] = value
                early[p.me, here, :] = value.astype(BF)
                spreads[t].start()
                if t + 2 < 4:
                    residual_loads(6 + t, "start")

        def out_store(m, j):
            start = m % (8 // pair) * tile
            return pltpu.make_async_copy(
                to_core.at[j % 2, pl.ds(0, tile), :],
                partials.at[m // (8 // pair), j, pl.ds(start, tile), :],
                tile_sem.at[2, j % 2],
            )

        def out_partial(m):
            for j in range(owners):
                value = contract_cols(
                    hidden_ref[pl.ds(m * tile, tile), :], weights[j * local : (j + 1) * local, :]
                )
                if m > 0 or j >= 2:
                    out_store(m if j >= 2 else m - 1, (j - 2) % owners).wait()
                to_core[j % 2, :tile, :] = value.astype(BF)
                out_store(m, j).start()

        for k in ORDER:
            dm.send_across(k)
        down_load.wait()
        for m in range(3):
            rows_backward(m)
        dm.send_on(FAR, 0)
        for m in range(3, 7):
            rows_backward(m)
        dm.send_on(NEAR, 1)
        rows_backward(7)
        weight_loads(0, "start")
        weight_loads(1, "start")
        dm.send_relay(0)
        partial_block(0)
        partial_block(1)
        dm.mate_rows()
        dm.send_relay(1)
        dm.send_forward()
        dm.sent(FAR)
        gm.send_across(FAR)
        dm.sent(NEAR)
        gm.send_across(NEAR)
        partial_block(2)
        partial_block(3)
        down_again = pltpu.make_async_copy(down_ref, weights, weights_sem.at[0])
        down_again.start()
        to_mate(0)
        dm.own_rows()
        dm.sent(MATE)
        gm.send_across(MATE)
        dm.sent(OWN)
        gm.send_across(OWN)
        to_mate(1)
        dm.send_back()
        dm.sent_on(0)
        gm.send_on(FAR, 0)
        dm.sent_on(1)
        gm.send_on(NEAR, 1)
        residual_loads(0, "start")
        residual_loads(1, "start")
        down_again.wait()
        for t in range(4):
            core_copy(1, t).wait_send()
        for m in range(8):
            out_partial(m)
        dm.sent_on(2)
        gm.mate_rows()
        final(2)
        final(3)
        row_sums()
        gm.send_relay(0)
        residual_grad()
        dm.finish()
        down_store = pltpu.make_async_copy(weight_grad, down_grad_all, weights_sem.at[1])
        down_store.start()
        gm.send_relay(1)
        gm.send_forward()
        down_store.wait()
        gm.own_rows()
        gm.send_back()
        for t in range(4):
            spreads[t].forward()
        gm.finish()
        gate_store = pltpu.make_async_copy(weight_grad, gate_grad_all, weights_sem.at[1])
        gate_store.start()
        for t in range(4):
            spreads[t].finish()
        gather_done = pltpu.make_async_copy(early, branch_all, early_sem.at[0, 0])
        gather_done.start()
        for j in range(3):
            gm.sent_on(j)
        gm.sent(*ORDER)
        for t in range(4):
            side_copy(t).wait_send()
        for t in range(2):
            mate_copy(t).wait_send()
        for copy in lane_copies():
            copy.wait_send()
        out_store(7, 2).wait()
        out_store(7, 3).wait()
        gather_done.wait()
        gate_store.wait()

    def array(*shape, dtype=F32):
        return jax.ShapeDtypeStruct(shape, dtype)

    return pl.pallas_call(
        kernel,
        out_shape=[
            array(tokens, local),
            array(owners, tokens, local, dtype=BF),
            array(1, local),
            array(pair, owners, tokens, local, dtype=BF),
            array(rows, 2 * half),
            array(rows, 2 * half),
            array(total, half, dtype=BF),
        ],
        in_specs=[ANY, ANY, VMEM, ANY, ANY, ANY, ANY, ANY, ANY, ANY, VMEM, VMEM],
        out_specs=[VMEM, ANY, VMEM, ANY, ANY, ANY, VMEM],
        scratch_shapes=[
            pltpu.VMEM((total, half), BF),
            pltpu.VMEM((owners * local, half), BF),
            pltpu.VMEM((2, total, rows), BF),
            pltpu.VMEM((owners, tokens, local), BF),
            pltpu.VMEM((4, piece, local), BF),
            pltpu.VMEM((2, 4, piece, local), BF),
            pltpu.VMEM((4, piece, local), BF),
            pltpu.VMEM((2, piece, local), BF),
            pltpu.VMEM((8, tokens), F32),
            pltpu.VMEM((3, 8, tokens), F32),
            pltpu.VMEM((2, 2, tokens // 4, local), F32),
            pltpu.VMEM((rows, 2 * half), F32),
            pltpu.SemaphoreType.DMA((2, pair)),
            pltpu.SemaphoreType.DMA((2, 8)),
            pltpu.SemaphoreType.DMA((5,)),
            pltpu.SemaphoreType.DMA((4, 4)),
            pltpu.SemaphoreType.DMA((4, 4)),
            pltpu.SemaphoreType.DMA((3,)),
            pltpu.SemaphoreType.DMA((3,)),
            pltpu.SemaphoreType.DMA((4, 3)),
            pltpu.SemaphoreType.DMA((4, 3)),
            pltpu.SemaphoreType.DMA((3, 2)),
        ]
        + pair_scatter_scratch(2, rows, half),
        compiler_params=pltpu.CompilerParams(
            collective_id=collective, has_side_effects=True, vmem_limit_bytes=62 << 20
        ),
        cost_estimate=pl.CostEstimate(flops=0, bytes_accessed=300 << 20, transcendentals=0),
        name="feed_forward_backward",
    )(
        out_rows, normed, hidden, silu, slope, gate, up, down, middle, out_grad, squares, gain
    )


class LineScatter:
    def __init__(self, p, product, sx, rx, sz, rz, rm, held, out, ss, rs):
        self.p, self.product = p, product
        self.sx, self.rx, self.sz, self.rz, self.rm = sx, rx, sz, rz, rm
        self.held, self.out, self.ss, self.rs = held, out, ss, rs

    def across(self, k):
        return remote(self.sx.at[k], self.rx.at[k], self.ss.at[k], self.rs.at[k], self.p.across)

    def outward(self, j):
        return remote(self.sz.at[j], self.rz.at[j], self.ss.at[4 + j], self.rs.at[4 + j], self.p.mate)

    def middle(self, j):
        return remote(self.sz.at[j], self.rm.at[j], self.ss.at[7 + j], self.rs.at[7 + j], self.p.mid)

    def back(self):
        return remote(self.sz.at[2], self.rz.at[0], self.ss.at[4], self.rs.at[4], self.p.mate)

    def send_across(self, k):
        self.sx[k] = self.product(k, 1 - self.p.x).astype(BF)
        self.across(k).start()

    def summed(self, k):
        total = self.product(k, self.p.x)
        self.across(k).wait_recv()
        return total + self.rx[k].astype(F32)

    def send_on(self, k, j):
        total = self.summed(k)

        @pl.when(self.p.outer)
        def _():
            self.sz[j] = total.astype(BF)
            self.outward(j).start()

        @pl.when(self.p.inner)
        def _():
            self.outward(j).wait_recv()
            self.sz[j] = (total + self.rz[j].astype(F32)).astype(BF)
            self.middle(j).start()

    def mate_rows(self):
        total = self.summed(MATE)

        @pl.when(self.p.outer)
        def _():
            self.sz[2] = total.astype(BF)
            self.outward(2).start()

        @pl.when(self.p.inner)
        def _():
            self.held[...] = total

    def own_rows(self):
        self.out[...] = self.summed(OWN)

    def send_back(self):
        @pl.when(self.p.inner)
        def _():
            self.middle(0).wait_recv()
            self.sz[2] = (self.held[...] + self.rm[0].astype(F32)).astype(BF)
            self.back().start()

    def finish(self):
        @pl.when(self.p.inner)
        def _():
            self.outward(2).wait_recv()
            self.middle(1).wait_recv()
            self.out[...] = self.out[...] + self.rz[2].astype(F32) + self.rm[1].astype(F32)
            for j in range(2):
                self.middle(j).wait_send()
            self.back().wait_send()

        @pl.when(self.p.outer)
        def _():
            self.back().wait_recv()
            self.out[...] = self.out[...] + self.rz[0].astype(F32)
            for j in range(3):
                self.outward(j).wait_send()

        for k in range(4):
            self.across(k).wait_send()


def mixer_backward(
    normed_mid, up_rows, branch, whole_out, in_matrix, projected, convolved, mixed, gated, normed_in,
    masks, conv_weight, stream, middle_grad, gain, inverse, gain_mid_grad, collective,
):
    pair, owners, tokens, local = normed_mid.shape
    total, half = up_rows.shape
    rows = owners * local // 8
    three = in_matrix.shape[1]
    tile = tokens // 4
    groups = three // local

    def kernel(*refs):
        normed_mid_ref, up_rows_ref, branch_ref, out_ref, in_ref, projected_ref, convolved_ref = refs[:7]
        mixed_ref, gated_ref, normed_in_ref, masks_ref, conv_ref, stream_ref = refs[7:13]
        middle_ref, gain_ref, inverse_ref, gain_mid_ref = refs[13:17]
        stream_grad, small_sums, up_grad, out_grad, in_grad = refs[17:22]
        conv_grad, rows_grad, stage, stage_mixed, weights, to_core, sums, from_y, lanes, near_lanes = refs[22:32]
        smalls, cols, stage_sem, in_sem, move_ss, move_rs, lanes_ss, lanes_rs = refs[32:40]
        small_ss, small_rs, halo_sem, cols_sem = refs[40:44]
        branch_sem = refs[59]
        sx, rx, sz, rz, rm, held, ss, rs = refs[44:52]
        lx, lrx, lz, lrz, lrm, lss, lrs = refs[52:59]
        lheld = held.at[:, pl.ds(0, local)]

        p = Place()
        p.core = (p.zh, p.zl, p.x, p.y, 1 - p.c)
        p.side = (p.zh, p.zl, p.x, 1 - p.y, p.c)
        diagonal = (p.zh, p.zl, p.x, 1 - p.y, 1 - p.c)
        place = 2 * p.z + p.x
        last = 7

        def device_at(s):
            return (s // 4, s // 2 % 2, s % 2, p.y, p.c)

        others = [lax.rem(place + d, 8) for d in range(1, 8)]

        jobs = []
        for t in range(4):
            jobs.append(((projected_ref, 1), (convolved_ref, 0), t))
        for t in range(4):
            jobs.append(((projected_ref, 0), (projected_ref, 2), t))
        for _ in range(2):
            for t in range(4):
                jobs.append(((stream_ref, 0), (middle_ref, 0), t))
        taken = []

        def stage_copies(n, act):
            for i, (ref, group) in enumerate(jobs[n][:2]):
                copy = pltpu.make_async_copy(
                    ref.at[pl.ds(jobs[n][2] * tile, tile), pl.ds(group * local, local)],
                    stage.at[n % 2, i],
                    stage_sem.at[n % 2, i],
                )
                getattr(copy, act)()

        def mixed_load(t):
            return pltpu.make_async_copy(
                mixed_ref.at[pl.ds(t * tile, tile + 8), :], stage_mixed.at[t % 2], stage_sem.at[t % 2, 2]
            )

        def branch_slot(t, j):
            return to_core.at[j] if t % 2 == 0 else lz.at[j // 3, j % 3]

        def branch_loads(t, act):
            for j in range(owners):
                copy = pltpu.make_async_copy(
                    branch_ref.at[0, j, pl.ds(t * tile, tile), :], branch_slot(t, j), branch_sem.at[t % 2, j]
                )
                getattr(copy, act)()

        def staged():
            n = len(taken)
            taken.append(n)
            stage_copies(n, "wait")
            values = stage[n % 2, 0], stage[n % 2, 1]
            return values

        def staged_done():
            n = len(taken) - 1
            if n + 2 < len(jobs):
                stage_copies(n + 2, "start")

        def out_loads(act):
            for j in range(owners):
                copy = pltpu.make_async_copy(
                    out_ref.at[pl.ds(j * local, local), :], weights.at[j], in_sem.at[j]
                )
                getattr(copy, act)()

        out_loads("start")
        stage_copies(0, "start")
        stage_copies(1, "start")
        branch_loads(0, "start")
        branch_loads(1, "start")
        mixed_load(0).start()
        mixed_load(1).start()
        feed_jobs = [(normed_mid_ref, k, True) for k in ORDER]
        feed_jobs += [(normed_mid_ref, FAR, False)]
        feed_jobs += [(branch_ref, k, True) for k in ORDER]
        feed_jobs += [(normed_mid_ref, NEAR, False)]
        feed_jobs += [(normed_in_ref, FAR, True), (normed_in_ref, NEAR, True)]
        feed_jobs += [(normed_mid_ref, MATE, False)]
        feed_jobs += [(normed_in_ref, MATE, True), (normed_in_ref, OWN, True)]
        feed_jobs += [(normed_mid_ref, OWN, False)]
        feed_jobs += [(branch_ref, k, False) for k in ORDER]
        feed_jobs += [(normed_in_ref, k, False) for k in ORDER]
        feed = Columns(p, feed_jobs, cols, cols_sem)
        owner = [
            2 * (1 - p.y) + 1 - p.c, 2 * (1 - p.y) + p.c, 2 * p.y + 1 - p.c, 2 * p.y + p.c
        ]
        p.enter_all([device_at(s) for s in others] + [p.core, p.side, diagonal])

        um = PairScatter(
            p, lambda k, x: feed.times(up_rows_ref[...]), sx, rx.at[0], sz, rz.at[0], rm.at[0], held,
            up_grad, ss.at[0], rs.at[0],
        )

        om = LineScatter(
            p, lambda k, x: feed.times(gated_ref[...]), lx.at[0], lrx.at[0], lz.at[0], lrz.at[0], lrm.at[0], lheld,
            out_grad, lss.at[0], lrs.at[0],
        )
        ims = [
            LineScatter(
                p, lambda k, x, g=g: feed.times_next(rows_grad[g], g == 0, g == groups - 1),
                lx.at[1 + g], lrx.at[1 + g], lz.at[1 + g], lrz.at[1 + g], lrm.at[1 + g],
                lheld, in_grad.at[:, pl.ds(g * local, local)], lss.at[1 + g], lrs.at[1 + g],
            )
            for g in range(groups)
        ]

        def halo_copy():
            return remote(
                conv_grad.at[pl.ds(0, 8), :],
                conv_grad.at[pl.ds(tokens, 8), :],
                halo_sem.at[0],
                halo_sem.at[1],
                device_at(others[6]),
            )

        taps = [jnp.zeros((1, local), F32) for _ in range(3)]

        def gated_backward(t):
            here = pl.ds(t * tile, tile)
            branch_loads(t, "wait")
            gated_grad = sum(
                dot(branch_slot(t, j)[...], weights[j])
                for j in range(owners)
            )
            if t + 2 < 4:
                branch_loads(t + 2, "start")
            out_gate, conv = staged()
            mixed_load(t).wait()
            near = stage_mixed.at[t % 2]
            rows_grad[1, here, :] = (gated_grad * conv).astype(BF)
            value = gated_grad * out_gate
            conv_grad[here, :] = value
            staged_done()
            taps[0] += jnp.sum(value * near[pl.ds(8, tile), :], axis=0, keepdims=True)
            taps[1] += jnp.sum(
                masks_ref[here, 0:1] * value * near[pl.ds(7, tile), :],
                axis=0, keepdims=True,
            )
            taps[2] += jnp.sum(
                masks_ref[here, 1:2] * value * near[pl.ds(6, tile), :],
                axis=0, keepdims=True,
            )
            if t + 2 < 4:
                mixed_load(t + 2).start()

        def send_halo():
            @pl.when(place > 0)
            def _():
                halo_copy().start()

        def take_halo():
            @pl.when(place < last)
            def _():
                halo_copy().wait_recv()

            @pl.when(place == last)
            def _():
                conv_grad[tokens:, :] = jnp.zeros((8, local), F32)

        def conv_backward(t):
            here = pl.ds(t * tile, tile)
            in_gate, carried = staged()
            value = (
                conv_ref[0:1, :] * conv_grad[here, :]
                + masks_ref[here, 2:3] * conv_ref[1:2, :] * conv_grad[pl.ds(1 + t * tile, tile), :]
                + masks_ref[here, 3:4] * conv_ref[2:3, :] * conv_grad[pl.ds(2 + t * tile, tile), :]
            )
            rows_grad[0, here, :] = (value * carried).astype(BF)
            rows_grad[2, here, :] = (value * in_gate).astype(BF)
            staged_done()

        def in_loads(n, act):
            start = pl.multiple_of(owner[n] * local, local)
            for g in range(groups):
                copy = pltpu.make_async_copy(
                    in_ref.at[pl.ds(start, local), pl.ds(g * local, local)], weights.at[g], in_sem.at[g]
                )
                getattr(copy, act)()

        def core_copy(b, t):
            return remote(to_core.at[t], sums.at[b, t], move_ss.at[b, t], move_rs.at[b, t], p.core)

        def side_copy(t):
            return remote(sums.at[0, t], from_y.at[t], move_ss.at[2, t], move_rs.at[2, t], p.side)

        def partial_block(n):
            in_loads(n, "wait")
            b = n // 2
            for t in range(4):
                here = pl.ds(t * tile, tile)
                value = sum(
                    contract_cols(rows_grad[g, here, :], weights[g])
                    for g in range(groups)
                )
                if n % 2 == 0:
                    if b == 1:
                        core_copy(0, t).wait_send()
                    to_core[t] = value.astype(BF)
                    core_copy(b, t).start()
                else:
                    core_copy(b, t).wait_recv()
                    value = value + sums[b, t].astype(F32)
                    if b == 0:
                        sums[b, t] = value.astype(BF)
                        side_copy(t).start()
                    else:
                        stream_grad[here, :] = value
            if n + 1 < 4:
                in_loads(n + 1, "start")

        def lane_copies():
            return [
                remote(lanes, near_lanes.at[i], lanes_ss.at[i], lanes_rs.at[i], device)
                for i, device in enumerate((p.core, p.side, diagonal))
            ]

        def small_copies():
            return [
                remote(
                    smalls.at[place], smalls.at[place], small_ss.at[d], small_rs.at[place], device_at(s)
                )
                for d, s in enumerate(others)
            ]

        def row_sums():
            total_gain = jnp.zeros((1, local), F32)
            for t in range(4):
                here = pl.ds(t * tile, tile)
                side_copy(t).wait_recv()
                value = stream_grad[here, :] + from_y[t].astype(F32)
                stream_grad[here, :] = value
                values = staged()[0]
                staged_done()
                product = value * values
                lanes[:, here] = lanes_of(jnp.sum(product * gain_ref[...], axis=1, keepdims=True))
                inverse_here = column_of(inverse_ref[:, here])
                total_gain = total_gain + jnp.sum(product * inverse_here, axis=0, keepdims=True)
            for copy in lane_copies():
                copy.start()
            smalls[place] = jnp.concatenate(
                taps + [total_gain, gain_mid_ref[...], jnp.zeros((3, local), F32)], axis=0
            )
            for copy in small_copies():
                copy.start()

        def input_grad():
            for copy in lane_copies():
                copy.wait_recv()
            sums_all = (lanes[...] + near_lanes[0] + near_lanes[1] + near_lanes[2]) / (owners * local)
            scale_all = inverse_ref[...] * inverse_ref[...] * inverse_ref[...] * sums_all
            for t in range(4):
                here = pl.ds(t * tile, tile)
                values, residual = staged()
                stream_grad[here, :] = (
                    residual
                    + column_of(inverse_ref[:, here]) * gain_ref[...] * stream_grad[here, :]
                    - values * column_of(scale_all[:, t * tile : (t + 1) * tile])
                )
                staged_done()

        def sum_smalls():
            for s in others:
                block = smalls.at[s]
                remote(block, block, small_ss.at[0], small_rs.at[s], p.mate).wait_recv()
            value = smalls[0]
            for s in range(1, 8):
                value = value + smalls[s]
            small_sums[...] = value

        for k in ORDER:
            um.send_across(k)
        out_loads("wait")
        for t in range(4):
            gated_backward(t)
            if t == 0:
                send_halo()
        in_loads(0, "start")
        um.send_on(FAR, 0)
        take_halo()
        for t in range(4):
            conv_backward(t)
        for k in ORDER:
            om.send_across(k)
        um.send_on(NEAR, 1)
        um.send_relay(0)
        partial_block(0)
        partial_block(1)
        for k in (FAR, NEAR):
            for m in ims:
                m.send_across(k)
        um.mate_rows()
        um.send_relay(1)
        um.send_forward()
        partial_block(2)
        partial_block(3)
        for k in (MATE, OWN):
            for m in ims:
                m.send_across(k)
        um.own_rows()
        um.send_back()
        om.send_on(FAR, 0)
        om.send_on(NEAR, 1)
        om.mate_rows()
        om.own_rows()
        om.send_back()
        um.finish()
        for m in ims:
            m.send_on(FAR, 0)
        row_sums()
        for m in ims:
            m.send_on(NEAR, 1)
        input_grad()
        om.finish()
        for m in ims:
            m.mate_rows()
            m.send_back()
        sum_smalls()
        for m in ims:
            m.own_rows()
        for m in ims:
            m.finish()
        for j in range(3):
            um.sent_on(j)
        um.sent(*ORDER)
        for t in range(4):
            core_copy(1, t).wait_send()
            side_copy(t).wait_send()
        for copy in lane_copies() + small_copies():
            copy.wait_send()

        @pl.when(place > 0)
        def _():
            halo_copy().wait_send()

    def array(*shape):
        return jax.ShapeDtypeStruct(shape, F32)

    n = 1 + groups
    return pl.pallas_call(
        kernel,
        out_shape=[
            array(tokens, local),
            array(8, local),
            array(rows, 2 * half),
            array(rows, local),
            array(rows, three),
        ],
        in_specs=[ANY, VMEM, ANY, ANY, ANY, ANY, ANY, ANY, VMEM, ANY, VMEM, VMEM, ANY, ANY]
        + [VMEM] * 3,
        out_specs=[VMEM] * 5,
        scratch_shapes=[
            pltpu.VMEM((tokens + 8, local), F32),
            pltpu.VMEM((groups, tokens, local), BF),
            pltpu.VMEM((2, 2, tile, local), F32),
            pltpu.VMEM((2, tile + 8, local), F32),
            pltpu.VMEM((owners, local, local), BF),
            pltpu.VMEM((4, tile, local), BF),
            pltpu.VMEM((2, 4, tile, local), BF),
            pltpu.VMEM((4, tile, local), BF),
            pltpu.VMEM((8, tokens), F32),
            pltpu.VMEM((3, 8, tokens), F32),
            pltpu.VMEM((8, 8, local), F32),
            pltpu.VMEM((2, total, rows), BF),
            pltpu.SemaphoreType.DMA((2, 3)),
            pltpu.SemaphoreType.DMA((owners,)),
            pltpu.SemaphoreType.DMA((3, 4)),
            pltpu.SemaphoreType.DMA((3, 4)),
            pltpu.SemaphoreType.DMA((3,)),
            pltpu.SemaphoreType.DMA((3,)),
            pltpu.SemaphoreType.DMA((7,)),
            pltpu.SemaphoreType.DMA((8,)),
            pltpu.SemaphoreType.DMA((2,)),
            pltpu.SemaphoreType.DMA((2, pair)),
        ]
        + pair_scatter_scratch(1, rows, half)
        + [
            pltpu.VMEM((n, 4, rows, local), BF),
            pltpu.VMEM((n, 4, rows, local), BF),
            pltpu.VMEM((n, 3, rows, local), BF),
            pltpu.VMEM((n, 3, rows, local), BF),
            pltpu.VMEM((n, 2, rows, local), BF),
            pltpu.SemaphoreType.DMA((n, 9)),
            pltpu.SemaphoreType.DMA((n, 9)),
            pltpu.SemaphoreType.DMA((2, owners)),
        ],
        compiler_params=pltpu.CompilerParams(
            collective_id=collective, has_side_effects=True, vmem_limit_bytes=62 << 20
        ),
        cost_estimate=pl.CostEstimate(flops=0, bytes_accessed=300 << 20, transcendentals=0),
        name="mixer_backward",
    )(
        normed_mid, up_rows, branch[None], whole_out, in_matrix, projected, convolved, mixed, gated,
        normed_in[None], masks, conv_weight, stream, middle_grad, gain, inverse, gain_mid_grad,
    )


SEQ = ("zh", "zl", "x")
TP = ("y", "c")
PAIR = ("zl", "y", "c")


def after(value, *others):
    return lax.optimization_barrier((value, *others))[0]


def gather_pair_rows(rows):
    blocks = lax.all_gather(rows, PAIR, axis=0)
    return blocks.reshape(lax.axis_size("zl"), lax.axis_size(TP), *rows.shape)


def paired_on_device(
    stream,
    norm1_gain,
    in_weight,
    conv_weight,
    out_weight,
    norm2_gain,
    gate_weight,
    up_weight,
    down_weight,
    doc_starts,
    out_grad,
):
    tokens, local = stream.shape
    rows_here = in_weight.shape[0]
    positions = lax.axis_index(SEQ) * tokens + jnp.arange(tokens, dtype=jnp.int32)
    mask_one, mask_two = lag_masks(doc_starts, positions)
    (
        in_matrix, whole_out, whole_gate, whole_up, whole_down, normed_in, projected, convolved, gated,
        normed_mid, hidden, silu, slope, mixed, middle, squares, first_squares,
    ) = block_forward(
        stream,
        jnp.stack([mask_one, mask_two]),
        conv_weight,
        norm1_gain[None],
        norm2_gain[None],
        in_weight.reshape(rows_here, 3 * local),
        out_weight,
        gate_weight,
        up_weight,
        down_weight,
        0,
    )
    out_full = gather_pair_rows(out_grad.astype(BF))
    mean_square = squares[0] / (local * lax.axis_size(TP)) + epsilon
    rms_mid = jnp.sqrt(mean_square)
    first_mean = first_squares / (local * lax.axis_size(TP)) + epsilon
    rms_in, inverse_in = jnp.sqrt(first_mean[0]), lax.rsqrt(first_mean)
    middle_grad, branch_blocks, gain_mid_grad, ffn_partial, down_weight_grad, gate_weight_grad, up_rows = (
        feed_forward_backward(
            out_full, normed_mid, hidden, silu, slope, whole_gate, whole_up, whole_down, middle, out_grad,
            squares, norm2_gain[None], 4,
        )
    )
    result = middle + lax.psum_scatter(
        ffn_partial.reshape(-1, local), PAIR, scatter_dimension=0, tiled=True
    ).astype(F32)
    next_one, next_two = lag_masks(doc_starts, positions + 1)[0], lag_masks(doc_starts, positions + 2)[1]
    count = tokens * lax.axis_size(SEQ)
    masks = jnp.concatenate(
        [
            mask_one,
            mask_two,
            jnp.where(positions[:, None] + 1 < count, next_one, 0.0),
            jnp.where(positions[:, None] + 2 < count, next_two, 0.0),
        ],
        axis=1,
    )
    stream_grad, small_sums, up_weight_grad, out_weight_grad, in_weight_grad = mixer_backward(
        normed_mid, up_rows, branch_blocks, whole_out, in_matrix, projected, convolved, mixed, gated,
        normed_in, masks, conv_weight, stream, middle_grad, norm1_gain[None],
        inverse_in, gain_mid_grad, 5,
    )
    conv_total, gain_in_total, gain_mid_total = small_sums[:3], small_sums[3], small_sums[4]
    return (
        result,
        stream_grad,
        gain_in_total,
        in_weight_grad.reshape(rows_here, 3, local),
        conv_total,
        out_weight_grad,
        gain_mid_total,
        gate_weight_grad,
        up_weight_grad,
        down_weight_grad,
        jnp.stack([rms_in, rms_mid]),
    )


def solution(mesh):
    seq, tp = mesh.shape["seq"], mesh.shape["tp"]
    if (seq, tp) == (8, 4):
        shape, names = (2, 2, 2, 2, 2), ("zh", "zl", "x", "y", "c")
        mesh = Mesh(mesh.devices.reshape(shape), names)
        body, rows, cols = paired_on_device, SEQ, TP
    else:
        body, rows, cols = on_device, "seq", "tp"
    return jax.shard_map(
        body,
        mesh=mesh,
        in_specs=(
            P(rows, cols),
            P(cols),
            P(rows, None, cols),
            P(None, cols),
            P(rows, cols),
            P(cols),
            P(rows, cols),
            P(rows, cols),
            P(rows, cols),
            P(),
            P(rows, cols),
        ),
        out_specs=(
            P(rows, cols),
            P(rows, cols),
            P(cols),
            P(rows, None, cols),
            P(None, cols),
            P(rows, cols),
            P(cols),
            P(rows, cols),
            P(rows, cols),
            P(rows, cols),
            P(None, rows),
        ),
        check_vma=False,
    )
```

```python
import jax
import jax.numpy as jnp
from jax import lax
from jax.experimental import pallas as pl
from jax.experimental.pallas import tpu as pltpu
from jax.sharding import Mesh, PartitionSpec as P

epsilon = 1e-05


def from_behind(shard, axis, by):
    count = lax.axis_size(axis)
    pairs = [(i, i + by) for i in range(count) if 0 <= i + by < count]
    return lax.ppermute(shard, axis, pairs)


def doc_count(doc_starts, positions):
    return jnp.sum((doc_starts[None, :] <= positions[:, None]).astype(jnp.int32), axis=1)


def lag_masks(doc_starts, positions):
    current = doc_count(doc_starts, positions)
    one = (positions >= 1) & (doc_count(doc_starts, positions - 1) == current)
    two = (positions >= 2) & (doc_count(doc_starts, positions - 2) == current)
    return (one.astype(jnp.float32)[:, None], two.astype(jnp.float32)[:, None])


def contract_rows(left, right):
    return lax.dot_general(
        left, right, (((0,), (0,)), ((), ())), preferred_element_type=jnp.float32
    )


def contract_cols(left, right):
    return lax.dot_general(
        left, right, (((1,), (1,)), ((), ())), preferred_element_type=jnp.float32
    )


def reduce_tp(partial_rows):
    return lax.psum_scatter(
        partial_rows.astype(jnp.bfloat16), "tp", scatter_dimension=1, tiled=True
    ).astype(jnp.float32)


def reduce_seq(partial_grad):
    return lax.psum_scatter(
        partial_grad.astype(jnp.bfloat16), "seq", scatter_dimension=0, tiled=True
    ).astype(jnp.float32)


def gather_grads(grad_rows):
    return lax.all_gather(grad_rows, "tp", axis=1, tiled=True)


def normalize(values, gain):
    width = gain.shape[0] * lax.axis_size("tp")
    squares = lax.psum(jnp.sum(values * values, axis=1, keepdims=True), "tp")
    inverse = lax.rsqrt(squares / width + epsilon)
    normed = lax.all_gather(
        (values * inverse * gain).astype(jnp.bfloat16), "tp", axis=1, tiled=True
    )
    return (normed, inverse, jnp.sqrt(squares[:, 0] / width + epsilon))


def norm_backward(values, gain, inverse, grad_rows):
    width = gain.shape[0] * lax.axis_size("tp")
    gained = gain * grad_rows
    total = lax.psum(jnp.sum(values * gained, axis=1, keepdims=True), "tp")
    grad_values = inverse * gained - values * inverse**3 * (total / width)
    grad_gain = jnp.sum(grad_rows * values * inverse, axis=0)
    return (grad_values, grad_gain)


def on_device(
    stream,
    norm1_gain,
    in_weight,
    conv_weight,
    out_weight,
    norm2_gain,
    gate_weight,
    up_weight,
    down_weight,
    doc_starts,
    out_grad,
):
    tokens = stream.shape[0]
    local = stream.shape[1]
    rows_here = in_weight.shape[0]
    whole_in, whole_out, whole_gate, whole_up, whole_down = (
        lax.all_gather(in_weight, "seq", axis=0, tiled=True),
        lax.all_gather(out_weight, "seq", axis=0, tiled=True),
        lax.all_gather(gate_weight, "seq", axis=0, tiled=True),
        lax.all_gather(up_weight, "seq", axis=0, tiled=True),
        lax.all_gather(down_weight, "seq", axis=0, tiled=True),
    )
    width = whole_out.shape[0]
    in_matrix = whole_in.reshape(width, 3 * local)
    positions = lax.axis_index("seq") * tokens + jnp.arange(tokens, dtype=jnp.int32)
    mask_one, mask_two = lag_masks(doc_starts, positions)
    normed_in, inverse_in, rms_in = normalize(stream, norm1_gain)
    projected = jnp.dot(normed_in, in_matrix, preferred_element_type=jnp.float32)
    in_gate = projected[:, :local]
    out_gate = projected[:, local : 2 * local]
    carried = projected[:, 2 * local :]
    mixed = in_gate * carried
    previous = from_behind(mixed[-2:], "seq", 1)
    extended = jnp.concatenate([previous, mixed], axis=0)
    convolved = (
        conv_weight[0] * mixed
        + mask_one * conv_weight[1] * extended[1:-1]
        + mask_two * conv_weight[2] * extended[:-2]
    )
    gated = (out_gate * convolved).astype(jnp.bfloat16)
    middle = stream + reduce_tp(contract_cols(gated, whole_out))
    normed_mid, inverse_mid, rms_mid = normalize(middle, norm2_gain)
    gate = jnp.dot(normed_mid, whole_gate, preferred_element_type=jnp.float32)
    upward = jnp.dot(normed_mid, whole_up, preferred_element_type=jnp.float32)
    hidden = (jax.nn.silu(gate) * upward).astype(jnp.bfloat16)
    result = middle + reduce_tp(contract_cols(hidden, whole_down))
    out_full = gather_grads(out_grad.astype(jnp.bfloat16))
    hidden_grad = jnp.dot(out_full, whole_down, preferred_element_type=jnp.float32)
    sigmoid_gate = jax.nn.sigmoid(gate)
    gate_rows = (hidden_grad * upward * sigmoid_gate * (1.0 + gate * (1.0 - sigmoid_gate))).astype(
        jnp.bfloat16
    )
    up_rows = (hidden_grad * gate * sigmoid_gate).astype(jnp.bfloat16)
    normed_mid_grad = reduce_tp(
        contract_cols(gate_rows, whole_gate) + contract_cols(up_rows, whole_up)
    )
    middle_norm_grad, gain_mid_grad = norm_backward(
        middle, norm2_gain, inverse_mid, normed_mid_grad
    )
    middle_grad = out_grad + middle_norm_grad
    branch_full = gather_grads(middle_grad.astype(jnp.bfloat16))
    gated_grad = jnp.dot(branch_full, whole_out, preferred_element_type=jnp.float32)
    out_gate_grad = gated_grad * convolved
    conv_grad = gated_grad * out_gate
    lag_one = mask_one * conv_grad
    lag_two = mask_two * conv_grad
    next_one, next_two = from_behind((lag_one[:2], lag_two[:2]), "seq", -1)
    after_one = jnp.concatenate([lag_one, next_one], axis=0)
    after_two = jnp.concatenate([lag_two, next_two], axis=0)
    mixed_grad = (
        conv_weight[0] * conv_grad
        + conv_weight[1] * after_one[1 : tokens + 1]
        + conv_weight[2] * after_two[2:]
    )
    tap_grads = jnp.stack(
        [
            jnp.sum(conv_grad * mixed, axis=0),
            jnp.sum(lag_one * extended[1:-1], axis=0),
            jnp.sum(lag_two * extended[:-2], axis=0),
        ]
    )
    projected_grad = jnp.concatenate(
        [mixed_grad * carried, out_gate_grad, mixed_grad * in_gate], axis=1
    ).astype(jnp.bfloat16)
    normed_in_grad = reduce_tp(contract_cols(projected_grad, in_matrix))
    stream_norm_grad, gain_in_grad = norm_backward(stream, norm1_gain, inverse_in, normed_in_grad)
    stream_grad = middle_grad + stream_norm_grad
    conv_total, gain_in_total, gain_mid_total = lax.psum(
        (tap_grads, gain_in_grad, gain_mid_grad), "seq"
    )
    down_weight_grad = reduce_seq(contract_rows(out_full, hidden))
    gate_weight_grad = reduce_seq(contract_rows(normed_mid, gate_rows))
    up_weight_grad = reduce_seq(contract_rows(normed_mid, up_rows))
    out_weight_grad = reduce_seq(contract_rows(branch_full, gated))
    in_weight_grad = reduce_seq(contract_rows(normed_in, projected_grad)).reshape(
        rows_here, 3, local
    )
    rms_values = jnp.stack([rms_in, rms_mid])
    return (
        result,
        stream_grad,
        gain_in_total,
        in_weight_grad,
        conv_total,
        out_weight_grad,
        gain_mid_total,
        gate_weight_grad,
        up_weight_grad,
        down_weight_grad,
        rms_values,
    )


MESH = pl.DeviceIdType.MESH
BF = jnp.bfloat16
F32 = jnp.float32
ANY = pl.BlockSpec(memory_space=pl.ANY)
VMEM = pl.BlockSpec(memory_space=pltpu.VMEM)
OWN, MATE, NEAR, FAR = 0, 1, 2, 3


def dot(left, right):
    return jnp.dot(left, right, preferred_element_type=F32)


def remote(src, dst, send_sem, recv_sem, device):
    return pltpu.make_async_remote_copy(
        src_ref=src,
        dst_ref=dst,
        send_sem=send_sem,
        recv_sem=recv_sem,
        device_id=device,
        device_id_type=MESH,
    )


class Place:
    def __init__(self):
        self.zh, self.zl = lax.axis_index("zh"), lax.axis_index("zl")
        self.x, self.y, self.c = lax.axis_index("x"), lax.axis_index("y"), lax.axis_index("c")
        self.z = 2 * self.zh + self.zl
        self.inner = (self.z == 1) | (self.z == 2)
        self.outer = (self.z == 0) | (self.z == 3)
        self.rows = [self.z, 2 * self.zh + 1 - self.zl, 2 - self.zh, 3 - 3 * self.zh]
        self.mate = (self.zh, 1 - self.zl, self.x, self.y, self.c)
        self.mid = (1 - self.zh, 1 - self.zl, self.x, self.y, self.c)
        self.across = (self.zh, self.zl, 1 - self.x, self.y, self.c)

    def block(self, which, x):
        return self.rows[which] * 2 + x

    def enter_all(self, devices):
        barrier = pltpu.get_barrier_semaphore()
        for device in devices:
            pl.semaphore_signal(barrier, inc=1, device_id=device, device_id_type=MESH)
        pl.semaphore_wait(barrier, len(devices))

    def enter(self, *others):
        barrier = pltpu.get_barrier_semaphore()

        def greet(device):
            pl.semaphore_signal(barrier, inc=1, device_id=device, device_id_type=MESH)

        greet(self.mate)
        greet(self.across)
        for device in others:
            greet(device)

        @pl.when(self.inner)
        def _():
            greet(self.mid)

        @pl.when(self.inner)
        def _():
            pl.semaphore_wait(barrier, 3 + len(others))

        @pl.when(self.outer)
        def _():
            pl.semaphore_wait(barrier, 2 + len(others))


def pair_gather_chunk(p, weight, out, relay, ss, rs, first, count, rows):
    half = out.shape[1]
    here = pl.ds(first, count)
    own = weight.at[here, pl.ds(pl.multiple_of(p.zl * half, half), half)]
    other = weight.at[here, pl.ds(pl.multiple_of((1 - p.zl) * half, half), half)]

    def block(which, x):
        return out.at[pl.ds(pl.multiple_of(p.block(which, x) * rows + first, count), count), :]

    held = [relay.at[i, here, :] for i in range(3)]

    def send(slot, src, dst, recv, device):
        return remote(src, dst, ss.at[slot], rs.at[recv], device)

    def arrived(recv, dst):
        remote(dst, dst, ss.at[0], rs.at[recv], p.mate).wait_recv()

    local = pltpu.make_async_copy(own, block(OWN, p.x), ss.at[11])
    across = [
        send(7 + k, own if k == OWN else block(k, p.x), block(k, p.x), 6 + k, p.across)
        for k in range(4)
    ]
    to_mate = send(0, other, block(OWN, p.x), 0, p.mate)
    outer_own = send(1, own, held[0], 3, p.mate)
    mid_other = send(3, other, block(OWN, p.x), 1, p.mid)
    mid_own = send(4, own, held[1], 4, p.mid)
    mid_far = send(5, held[0], block(MATE, p.x), 2, p.mid)
    mid_far_own = send(6, block(MATE, p.x), held[2], 5, p.mid)
    back_near = send(1, held[1], block(NEAR, p.x), 1, p.mate)
    back_far = send(2, held[2], block(FAR, p.x), 2, p.mate)

    def begin():
        @pl.when(p.inner)
        def _():
            mid_other.start()
            mid_own.start()

        to_mate.start()

        @pl.when(p.outer)
        def _():
            outer_own.start()

        across[OWN].start()
        local.start()

    def mate_here():
        arrived(0, block(MATE, p.x))

        @pl.when(p.inner)
        def _():
            arrived(3, held[0])
            mid_far.start()
            mid_far_own.start()
            arrived(4, held[1])
            back_near.start()

        across[MATE].start()

    def near_here():
        arrived(1, block(NEAR, p.x))
        across[NEAR].start()

        @pl.when(p.inner)
        def _():
            arrived(5, held[2])
            back_far.start()

    def far_here():
        arrived(2, block(FAR, p.x))
        across[FAR].start()

    def finish():
        for k in range(4):
            arrived(6 + k, block(k, 1 - p.x))
            across[k].wait_send()
        local.wait()
        to_mate.wait_send()

        @pl.when(p.inner)
        def _():
            for copy in (mid_other, mid_own, mid_far, mid_far_own, back_near, back_far):
                copy.wait_send()

        @pl.when(p.outer)
        def _():
            outer_own.wait_send()

    return [begin, mate_here, near_here, far_here, finish]


def line_gather_chunk(p, weight, out, ss, rs, first, count, rows):
    own = weight.at[pl.ds(first, count), :]

    def block(which, x):
        return out.at[pl.ds(pl.multiple_of(p.block(which, x) * rows + first, count), count), :]

    def send(slot, src, dst, recv, device):
        return remote(src, dst, ss.at[slot], rs.at[recv], device)

    def arrived(recv, dst):
        remote(dst, dst, ss.at[0], rs.at[recv], p.mate).wait_recv()

    local = pltpu.make_async_copy(own, block(OWN, p.x), ss.at[9])
    across = [
        send(k, own if k == OWN else block(k, p.x), block(k, p.x), 3 + k, p.across)
        for k in range(4)
    ]
    to_mate = send(4, own, block(OWN, p.x), MATE - 1, p.mate)
    to_mid = send(5, own, block(OWN, p.x), NEAR - 1, p.mid)
    mid_far = send(6, block(MATE, p.x), block(MATE, p.x), FAR - 1, p.mid)
    back_near = send(7, block(NEAR, p.x), block(NEAR, p.x), NEAR - 1, p.mate)
    back_far = send(8, block(FAR, p.x), block(FAR, p.x), FAR - 1, p.mate)

    def begin():
        @pl.when(p.inner)
        def _():
            to_mid.start()

        to_mate.start()
        across[OWN].start()
        local.start()

    def mate_here():
        arrived(MATE - 1, block(MATE, p.x))

        @pl.when(p.inner)
        def _():
            mid_far.start()

        across[MATE].start()

    def near_here():
        arrived(NEAR - 1, block(NEAR, p.x))

        @pl.when(p.inner)
        def _():
            back_near.start()

        across[NEAR].start()

    def far_here():
        arrived(FAR - 1, block(FAR, p.x))

        @pl.when(p.inner)
        def _():
            back_far.start()

        across[FAR].start()

    def finish():
        for k in range(4):
            arrived(3 + k, block(k, 1 - p.x))
            across[k].wait_send()
        local.wait()
        to_mate.wait_send()

        @pl.when(p.inner)
        def _():
            for copy in (to_mid, mid_far, back_near, back_far):
                copy.wait_send()

    return [begin, mate_here, near_here, far_here, finish]


def contract_tokens(left, right):
    return lax.dot_general(left, right, (((0,), (0,)), ((), ())), preferred_element_type=F32)


class PairScatter:
    def __init__(self, p, product, sx, rx, sz, rz, rm, held, out, ss, rs):
        self.p, self.product = p, product
        self.sx, self.rx, self.sz, self.rz, self.rm = sx, rx, sz, rz, rm
        self.held, self.out, self.ss, self.rs = held, out, ss, rs
        self.half = sz.shape[2]

    def across(self, k):
        return remote(self.sx.at[k], self.rx.at[k], self.ss.at[k], self.rs.at[k], self.p.across)

    def outward(self, j):
        return remote(self.sz.at[j], self.rz.at[j], self.ss.at[4 + j], self.rs.at[4 + j], self.p.mate)

    def middle(self, j):
        return remote(self.sz.at[j], self.rm.at[j], self.ss.at[7 + j], self.rs.at[7 + j], self.p.mid)

    def relay(self, j):
        return remote(
            self.rz.at[j], self.rm.at[2 + j], self.ss.at[9 + j], self.rs.at[9 + j], self.p.mid
        )

    def forward(self):
        return remote(self.rm.at[0], self.rz.at[0], self.ss.at[4], self.rs.at[4], self.p.mate)

    def back(self):
        return remote(self.sz.at[2], self.rz.at[1], self.ss.at[5], self.rs.at[5], self.p.mate)

    def cols_of(self, place):
        return pl.ds(pl.multiple_of(place * self.half, self.half), self.half)

    def send_across(self, k, *sent):
        self.sx[k] = self.product(k, 1 - self.p.x).astype(BF)
        self.sent(*sent)
        self.across(k).start()

    def summed(self, k):
        total = self.product(k, self.p.x)
        self.across(k).wait_recv()
        return total + self.rx[k].astype(F32)

    def send_on(self, k, j):
        self.sz[j] = self.summed(k).astype(BF)

        @pl.when(self.p.outer)
        def _():
            self.outward(j).start()

        @pl.when(self.p.inner)
        def _():
            self.middle(j).start()

    def send_relay(self, j):
        @pl.when(self.p.inner)
        def _():
            self.outward(j).wait_recv()
            self.relay(j).start()

    def mate_rows(self):
        total = self.summed(MATE)

        @pl.when(self.p.outer)
        def _():
            self.sz[2] = total.astype(BF)
            self.outward(2).start()

        @pl.when(self.p.inner)
        def _():
            self.held[...] = total

    def send_forward(self):
        @pl.when(self.p.inner)
        def _():
            self.middle(0).wait_recv()
            self.forward().start()

    def own_rows(self):
        self.out[:, self.cols_of(self.p.zl)] = self.summed(OWN)

    def send_back(self):
        @pl.when(self.p.inner)
        def _():
            self.relay(0).wait_recv()
            self.sz[2] = (self.held[...] + self.rm[2].astype(F32)).astype(BF)
            self.back().start()

    def finish(self):
        p, out = self.p, self.out
        here, there = self.cols_of(p.zl), self.cols_of(1 - p.zl)

        @pl.when(p.inner)
        def _():
            self.relay(1).wait_recv()
            out[:, here] = out[:, here] + self.rm[3].astype(F32)
            self.outward(2).wait_recv()
            self.middle(1).wait_recv()
            out[:, there] = self.rz[2].astype(F32) + self.rm[1].astype(F32)

        @pl.when(p.outer)
        def _():
            self.forward().wait_recv()
            out[:, here] = out[:, here] + self.rz[0].astype(F32)
            self.back().wait_recv()
            out[:, there] = self.rz[1].astype(F32)

        @pl.when(p.inner)
        def _():
            for j in range(2):
                self.relay(j).wait_send()
            self.forward().wait_send()

    def sent_on(self, j):
        @pl.when(self.p.outer)
        def _():
            self.outward(j).wait_send()

        @pl.when(self.p.inner)
        def _():
            (self.back() if j == 2 else self.middle(j)).wait_send()

    def sent(self, *which):
        for k in which:
            self.across(k).wait_send()


def pair_scatter_scratch(n, rows, half):
    return [
        pltpu.VMEM((4, rows, half), BF),
        pltpu.VMEM((n, 4, rows, half), BF),
        pltpu.VMEM((3, rows, half), BF),
        pltpu.VMEM((n, 3, rows, half), BF),
        pltpu.VMEM((n, 4, rows, half), BF),
        pltpu.VMEM((rows, half), F32),
        pltpu.SemaphoreType.DMA((n, 11)),
        pltpu.SemaphoreType.DMA((n, 11)),
    ]


class Columns:
    def __init__(self, p, jobs, buffer, sems):
        self.p, self.jobs, self.buffer, self.sems, self.at = p, jobs, buffer, sems, 0
        for n in range(min(2, len(jobs))):
            self.copies(n, "start")

    def copies(self, n, act):
        array, k, flip = self.jobs[n]
        pair, _, tokens, local = array.shape
        rows = self.buffer.shape[2]
        start = self.p.block(k, 1 - self.p.x if flip else self.p.x) * rows
        cols = pl.ds(pl.multiple_of(start % local, rows), rows)
        for q in range(pair):
            copy = pltpu.make_async_copy(
                array.at[q, start // local, :, cols],
                self.buffer.at[n % 2, pl.ds(q * tokens, tokens), :],
                self.sems.at[n % 2, q],
            )
            getattr(copy, act)()

    def times(self, right):
        return self.times_next(right, True, True)

    def times_next(self, right, first, last):
        if first:
            self.at += 1
            self.copies(self.at - 1, "wait")
        n = self.at - 1
        tokens = self.jobs[n][0].shape[0] * self.jobs[n][0].shape[2]
        product = contract_tokens(self.buffer[n % 2, :tokens, :], right)
        if last and n + 2 < len(self.jobs):
            self.copies(n + 2, "start")
        return product


ORDER = (FAR, NEAR, MATE, OWN)


class Spread:
    def __init__(self, p, view, ss, rs):
        self.p = p
        self.view, self.ss, self.rs = view, ss, rs

    def to_core(self):
        block = self.view(self.p.me)
        return remote(block, block, self.ss.at[0], self.rs.at[0], self.p.core)

    def to_side(self):
        block = self.view(self.p.me)
        return remote(block, block, self.ss.at[1], self.rs.at[1], self.p.side)

    def on_to_core(self):
        block = self.view(self.p.side_owner)
        return remote(block, block, self.ss.at[2], self.rs.at[2], self.p.core)

    def start(self):
        self.to_side().start()
        self.to_core().start()

    def forward(self):
        self.to_side().wait_recv()
        self.on_to_core().start()

    def finish(self):
        self.to_core().wait_recv()
        self.on_to_core().wait_recv()
        self.to_core().wait_send()
        self.to_side().wait_send()
        self.on_to_core().wait_send()


def lanes_of(column):
    return jnp.broadcast_to(column, (column.shape[0], 128)).T[:8]


def column_of(lanes):
    return jnp.broadcast_to(lanes[:1], (128, lanes.shape[1])).T[:, :1]


def block_forward(
    stream, masks, conv_weight, first_gain, gain, in_weight, out_weight, gate_weight, up_weight,
    down_weight, collective,
):
    tokens, local = stream.shape
    rows, width = gate_weight.shape
    half = width // 2
    three = in_weight.shape[1]
    owners, pair = 4, 2
    features = owners * local
    tile = tokens // 4
    plan = [("in", rows // 4)] * 4 + [("out", rows)]
    plan += [(name, rows // 4) for name in ("gate", "up", "down") for _ in range(4)]
    n_chunks = len(plan)

    def kernel(*refs):
        stream_ref, masks_ref, conv_ref, first_gain_ref, gain_ref = refs[:5]
        in_ref, out_ref, gate_ref, up_ref, down_ref = refs[5:10]
        in_all, out_all, gate_all, up_all, down_all = refs[10:15]
        normed_all, projected_all, convolved_all, gated_all, mid_all = refs[15:20]
        hidden_all, silu_all, slope_all, mixed_all, middle, squares = refs[20:26]
        first_squares, refs = refs[26], refs[:26] + refs[27:]
        x, in_vm, out_vm, gate_vm, up_vm, projected, mixed, convolved, gated = refs[26:35]
        to_core, sums, from_y, near_squares, mid, results, relay = refs[35:42]
        halo, first_near, first_ss, first_rs = refs[55:]
        chunk_ss, chunk_rs, x_ss, x_rs, mid_ss, mid_rs, move_ss, move_rs = refs[42:50]
        square_ss, square_rs, halo_sem, store_sem, result_sem = refs[50:55]

        p = Place()
        p.core = (p.zh, p.zl, p.x, p.y, 1 - p.c)
        p.side = (p.zh, p.zl, p.x, 1 - p.y, p.c)
        diagonal = (p.zh, p.zl, p.x, 1 - p.y, 1 - p.c)
        p.me, p.side_owner = 2 * p.y + p.c, 2 * (1 - p.y) + p.c
        place = 2 * p.z + p.x
        last = 2 * 4 - 1

        def device_at(s):
            return (s // 4, s // 2 % 2, s % 2, p.y, p.c)

        following, previous = device_at(lax.rem(place + 1, 8)), device_at(lax.rem(place + 7, 8))
        p.enter(p.core, p.side, diagonal, following, previous)

        chunks = []
        firsts = {}
        targets = {
            "in": (in_ref, in_vm), "out": (out_ref, out_vm), "gate": (gate_ref, gate_vm),
            "up": (up_ref, up_vm), "down": (down_ref, down_all),
        }
        for c, (name, count) in enumerate(plan):
            first = firsts.get(name, 0)
            firsts[name] = first + count
            source, target = targets[name]
            if name in ("in", "out"):
                chunk = line_gather_chunk(
                    p, source, target, chunk_ss.at[c], chunk_rs.at[c], first, count, rows
                )
            else:
                held = relay.at[("gate", "up", "down").index(name)]
                chunk = pair_gather_chunk(
                    p, source, target, held, chunk_ss.at[c], chunk_rs.at[c], first, count, rows
                )
            chunks.append(chunk)

        def pump(step):
            for c in range(3) if step == 0 else [step + 2]:
                if c < n_chunks:
                    chunks[c][0]()
            for stage in range(1, 5):
                if 0 <= step - stage < n_chunks:
                    chunks[step - stage][stage]()

        stores = []

        def store(source, target):
            copy = pltpu.make_async_copy(source, target, store_sem.at[1 + len(stores)])
            copy.start()
            stores.append(copy)

        spread_x = Spread(p, lambda owner: x.at[owner], x_ss, x_rs)

        def project(t):
            here = pl.ds(t * tile, tile)
            value = sum(
                dot(x[j, here, :], in_vm[j * local : (j + 1) * local, :]) for j in range(owners)
            )
            projected[here, :] = value
            mixed[pl.ds(8 + t * tile, tile), :] = value[:, :local] * value[:, 2 * local :]

        def halo_copy():
            return remote(
                mixed.at[pl.ds(tokens, 8), :], halo, halo_sem.at[0], halo_sem.at[1], following
            )

        def send_halo():
            @pl.when(place < last)
            def _():
                halo_copy().start()

        def take_halo():
            @pl.when(place > 0)
            def _():
                halo_copy().wait_recv()

            @pl.when(place == 0)
            def _():
                halo[...] = jnp.zeros_like(halo)

            mixed[:8, :] = halo[...]

        def convolve(t):
            here = pl.ds(t * tile, tile)
            value = (
                conv_ref[0:1, :] * mixed[pl.ds(8 + t * tile, tile), :]
                + masks_ref[0, here, :] * conv_ref[1:2, :] * mixed[pl.ds(7 + t * tile, tile), :]
                + masks_ref[1, here, :] * conv_ref[2:3, :] * mixed[pl.ds(6 + t * tile, tile), :]
            )
            convolved[here, :] = value
            gated[here, :] = (projected[here, local : 2 * local] * value).astype(BF)

        owner = [
            2 * (1 - p.y) + 1 - p.c, 2 * (1 - p.y) + p.c, 2 * p.y + 1 - p.c, 2 * p.y + p.c
        ]

        def core_copy(b, t):
            return remote(
                to_core.at[b, t], sums.at[b, t], move_ss.at[b, t], move_rs.at[b, t], p.core
            )

        def side_copy(t):
            return remote(sums.at[0, t], from_y.at[t], move_ss.at[2, t], move_rs.at[2, t], p.side)

        def mixer_out(n):
            out_rows = pl.ds(pl.multiple_of(owner[n] * local, local), local)
            for t in range(4):
                here = pl.ds(t * tile, tile)
                value = contract_cols(gated[here, :], out_vm[out_rows, :])
                b = n // 2
                if n % 2 == 0:
                    to_core[b, t] = value.astype(BF)
                    core_copy(b, t).start()
                else:
                    core_copy(b, t).wait_recv()
                    value = value + sums[b, t].astype(F32)
                    if b == 0:
                        sums[b, t] = value.astype(BF)
                        side_copy(t).start()
                    else:
                        middle[here, :] = stream_ref[here, :] + value

        def residual(t):
            here = pl.ds(t * tile, tile)
            side_copy(t).wait_recv()
            value = middle[here, :] + from_y[t].astype(F32)
            middle[here, :] = value
            squares[:, here] = lanes_of(jnp.sum(value * value, axis=1, keepdims=True))

        def square_copies(mine, near, send_sems, recv_sems):
            return [
                remote(mine, near.at[i], send_sems.at[i], recv_sems.at[i], device)
                for i, device in enumerate((p.core, p.side, diagonal))
            ]

        def sum_squares(mine, near, *sems):
            for copy in square_copies(mine, near, *sems):
                copy.wait_recv()
                copy.wait_send()
            mine[...] = mine[...] + near[0] + near[1] + near[2]

        first = (first_squares, first_near, first_ss, first_rs)
        second = (squares, near_squares, square_ss, square_rs)

        def first_sums():
            for t in range(4):
                here = pl.ds(t * tile, tile)
                value = stream_ref[here, :]
                first_squares[:, here] = lanes_of(jnp.sum(value * value, axis=1, keepdims=True))
            for copy in square_copies(*first):
                copy.start()

        def first_norm():
            sum_squares(*first)
            for t in range(4):
                here = pl.ds(t * tile, tile)
                inverse = lax.rsqrt(first_squares[:, here] / features + epsilon)
                value = stream_ref[here, :] * column_of(inverse) * first_gain_ref[...]
                x[p.me, here, :] = value.astype(BF)

        def own_tile(t):
            return lambda who: mid.at[p.zl, who, pl.ds(t * tile, tile), :]

        def mate_tile(t):
            return lambda who: mid.at[1 - p.zl, who, pl.ds(t * tile, tile), :]

        spread_own = [Spread(p, own_tile(t), mid_ss.at[0, t], mid_rs.at[0, t]) for t in range(4)]
        spread_mate = [Spread(p, mate_tile(t), mid_ss.at[1, t], mid_rs.at[1, t]) for t in range(4)]

        def mate_send(t):
            block = own_tile(t)(p.me)
            return remote(block, block, mid_ss.at[0, t, 3], mid_rs.at[0, t, 3], p.mate)

        def normalize_mid(t):
            here = pl.ds(t * tile, tile)
            inverse = lax.rsqrt(squares[:, here] / features + epsilon)
            value = middle[here, :] * column_of(inverse) * gain_ref[...]
            mid[p.zl, p.me, here, :] = value.astype(BF)
            mate_send(t).start()
            spread_own[t].start()

        def pass_on(t):
            spread_own[t].forward()
            mate_send(t).wait_recv()
            spread_mate[t].start()

        def result_stores(m, act):
            start = pl.multiple_of(tile_place(m) * tile, tile)
            for i, ref in enumerate((hidden_all, silu_all, slope_all)):
                copy = pltpu.make_async_copy(
                    results.at[m % 2, i], ref.at[pl.ds(start, tile), :], result_sem.at[m % 2, i]
                )
                getattr(copy, act)()

        def tile_place(m):
            return (p.zl if m < 4 else 1 - p.zl) * 4 + m % 4

        def hidden_units(m):
            q = p.zl if m < 4 else 1 - p.zl
            here = pl.ds(m % 4 * tile, tile)
            (spread_own if m < 4 else spread_mate)[m % 4].finish()
            if m >= 2:
                result_stores(m - 2, "wait")
            for part in range(2):
                cols = pl.ds(part * half // 2, half // 2)
                value = sum(
                    dot(mid[q, j, here, :], gate_vm[j * local : (j + 1) * local, cols])
                    for j in range(owners)
                )
                upward = sum(
                    dot(mid[q, j, here, :], up_vm[j * local : (j + 1) * local, cols])
                    for j in range(owners)
                )
                sigmoid = jax.nn.sigmoid(value)
                silu = value * sigmoid
                results[m % 2, 0, :, cols] = (silu * upward).astype(BF)
                results[m % 2, 1, :, cols] = silu.astype(BF)
                results[m % 2, 2, :, cols] = (upward * (sigmoid + silu * (1.0 - sigmoid))).astype(BF)
            result_stores(m, "start")

        pump(0)
        first_sums()
        first_norm()
        spread_x.start()
        pump(1)
        pump(2)
        spread_x.forward()
        pump(3)
        pump(4)
        pump(5)
        spread_x.finish()
        pump(6)
        pump(7)
        store(x, normed_all)
        store(in_vm, in_all)
        project(3)
        send_halo()
        project(2)
        pump(8)
        project(1)
        project(0)
        store(projected, projected_all)
        store(out_vm, out_all)
        pump(9)
        take_halo()
        for t in range(4):
            convolve(t)
        store(convolved, convolved_all)
        store(mixed, mixed_all)
        store(gated, gated_all)
        mixer_out(0)
        mixer_out(1)
        pump(10)
        mixer_out(2)
        mixer_out(3)
        pump(11)
        residual(0)
        residual(1)
        pump(12)
        store(gate_vm, gate_all)
        residual(2)
        residual(3)
        for copy in square_copies(*second):
            copy.start()
        pump(13)
        sum_squares(*second)
        for t in range(4):
            normalize_mid(t)
        pump(14)
        pass_on(0)
        pass_on(1)
        pump(15)
        pass_on(2)
        pass_on(3)
        pump(16)
        store(up_vm, up_all)
        hidden_units(0)
        hidden_units(1)
        pump(17)
        hidden_units(2)
        for t in range(4):
            spread_mate[t].forward()
        pump(18)
        hidden_units(3)
        hidden_units(4)
        hidden_units(5)
        pump(19)
        hidden_units(6)
        hidden_units(7)
        store(mid, mid_all)
        pump(20)
        result_stores(6, "wait")
        result_stores(7, "wait")
        for copy in stores:
            copy.wait()
        for t in range(4):
            core_copy(0, t).wait_send()
            core_copy(1, t).wait_send()
            side_copy(t).wait_send()
            mate_send(t).wait_send()

        @pl.when(place < last)
        def _():
            halo_copy().wait_send()

    def array(*shape, dtype=BF):
        return jax.ShapeDtypeStruct(shape, dtype)

    units = array(pair * tokens, half)
    outs = [
        (array(8 * rows, three), ANY), (array(8 * rows, local), ANY),
        (array(8 * rows, half), ANY), (array(8 * rows, half), ANY), (array(8 * rows, half), ANY),
        (array(owners, tokens, local), ANY), (array(tokens, three, dtype=F32), ANY),
        (array(tokens, local, dtype=F32), ANY), (array(tokens, local), ANY),
        (array(pair, owners, tokens, local), ANY),
        (units, ANY), (units, ANY), (units, ANY),
        (array(8 + tokens, local, dtype=F32), ANY),
        (array(tokens, local, dtype=F32), VMEM), (array(8, tokens, dtype=F32), VMEM),
        (array(8, tokens, dtype=F32), VMEM),
    ]
    return pl.pallas_call(
        kernel,
        out_shape=[o[0] for o in outs],
        in_specs=[VMEM] * 5 + [ANY] * 5,
        out_specs=[o[1] for o in outs],
        scratch_shapes=[
            pltpu.VMEM((owners, tokens, local), BF),
            pltpu.VMEM((8 * rows, three), BF),
            pltpu.VMEM((8 * rows, local), BF),
            pltpu.VMEM((8 * rows, half), BF),
            pltpu.VMEM((8 * rows, half), BF),
            pltpu.VMEM((tokens, three), F32),
            pltpu.VMEM((8 + tokens, local), F32),
            pltpu.VMEM((tokens, local), F32),
            pltpu.VMEM((tokens, local), BF),
            pltpu.VMEM((2, 4, tile, local), BF),
            pltpu.VMEM((2, 4, tile, local), BF),
            pltpu.VMEM((4, tile, local), BF),
            pltpu.VMEM((3, 8, tokens), F32),
            pltpu.VMEM((pair, owners, tokens, local), BF),
            pltpu.VMEM((2, 3, tile, half), BF),
            pltpu.VMEM((3, 3, rows, half), BF),
            pltpu.SemaphoreType.DMA((n_chunks, 12)),
            pltpu.SemaphoreType.DMA((n_chunks, 10)),
            pltpu.SemaphoreType.DMA((3,)),
            pltpu.SemaphoreType.DMA((3,)),
            pltpu.SemaphoreType.DMA((2, 4, 4)),
            pltpu.SemaphoreType.DMA((2, 4, 4)),
            pltpu.SemaphoreType.DMA((3, 4)),
            pltpu.SemaphoreType.DMA((3, 4)),
            pltpu.SemaphoreType.DMA((3,)),
            pltpu.SemaphoreType.DMA((3,)),
            pltpu.SemaphoreType.DMA((2,)),
            pltpu.SemaphoreType.DMA((12,)),
            pltpu.SemaphoreType.DMA((2, 3)),
            pltpu.VMEM((8, local), F32),
            pltpu.VMEM((3, 8, tokens), F32),
            pltpu.SemaphoreType.DMA((3,)),
            pltpu.SemaphoreType.DMA((3,)),
        ],
        compiler_params=pltpu.CompilerParams(
            collective_id=collective, has_side_effects=True, vmem_limit_bytes=62 << 20
        ),
        cost_estimate=pl.CostEstimate(flops=0, bytes_accessed=600 << 20, transcendentals=0),
        name="block_forward",
    )(
        stream, masks, conv_weight, first_gain, gain, in_weight, out_weight, gate_weight, up_weight,
        down_weight,
    )


def feed_forward_backward(
    out_rows, normed, hidden, silu, slope, gate, up, down, middle, out_grad, squares, gain, collective
):
    pair, owners, tokens, local = normed.shape
    total, half = hidden.shape
    rows = owners * local // 8
    tile = total // 8
    piece = total // 4

    def kernel(*refs):
        out_ref, normed_ref, hidden_ref, silu_ref, slope_ref, gate_ref, up_ref, down_ref = refs[:8]
        middle_ref, out_grad_ref, squares_ref, gain_ref = refs[8:12]
        middle_grad, branch_all, gain_grad, partials, down_grad_all, gate_grad_all, up_blocks = refs[12:19]
        gate_rows, weights, cols, early, to_core, sums, from_y, from_mate, lanes = refs[19:28]
        near_lanes, residual, weight_grad, cols_sem, early_sem, weights_sem, move_ss, move_rs = refs[28:36]
        lanes_ss, lanes_rs, branch_ss, branch_rs, tile_sem = refs[36:41]
        up_rows, up_ss, up_rs, free_sem = refs[41:45]
        sx, rx, sz, rz, rm, held, ss, rs = refs[45:]
        p = Place()
        p.core = (p.zh, p.zl, p.x, p.y, 1 - p.c)
        p.side = (p.zh, p.zl, p.x, 1 - p.y, p.c)
        diagonal = (p.zh, p.zl, p.x, 1 - p.y, 1 - p.c)
        p.me, p.side_owner = 2 * p.y + p.c, 2 * (1 - p.y) + p.c

        down_load = pltpu.make_async_copy(down_ref, weights, weights_sem.at[0])
        down_load.start()

        def tile_loads(m, act):
            start = m % (8 // pair) * tile
            copies = [
                (
                    out_ref.at[m // (8 // pair), j, pl.ds(start, tile), :],
                    early.at[m % 2, pl.ds(j * tile, tile), :],
                )
                for j in range(owners)
            ]
            copies += [
                (
                    ref.at[pl.ds(m * tile, tile), pl.ds(part * local, local)],
                    early.at[2 + m % 2, pl.ds((2 * i + part) * tile, tile), :],
                )
                for i, ref in enumerate((silu_ref, slope_ref))
                for part in range(2)
            ]
            for i, (source, target) in enumerate(copies):
                getattr(pltpu.make_async_copy(source, target, early_sem.at[m % 2, i]), act)()

        quarter = tokens // 4
        D = (out_ref, normed_ref)
        jobs = [(D[0], k, True) for k in ORDER]
        jobs += [(D[0], FAR, False), (D[0], NEAR, False), (D[0], MATE, False)]
        jobs += [(D[1], FAR, True), (D[1], NEAR, True), (D[0], OWN, False)]
        jobs += [(D[1], MATE, True), (D[1], OWN, True)]
        jobs += [(D[1], FAR, False), (D[1], NEAR, False), (D[1], FAR, True), (D[1], NEAR, True)]
        jobs += [(D[1], MATE, False), (D[1], MATE, True), (D[1], OWN, True), (D[1], OWN, False)]
        jobs += [(D[1], k, False) for k in ORDER]
        feed = Columns(p, jobs, cols, cols_sem)
        tile_loads(0, "start")
        tile_loads(1, "start")
        p.enter(p.core, p.side, diagonal)

        dm = PairScatter(
            p, lambda k, x: feed.times(hidden_ref[...]), sx, rx.at[0], sz, rz.at[0],
            rm.at[0], held, weight_grad, ss.at[0], rs.at[0],
        )
        gm = PairScatter(
            p, lambda k, x: feed.times(gate_rows[...]), sx, rx.at[1], sz, rz.at[1],
            rm.at[1], held, weight_grad, ss.at[1], rs.at[1],
        )

        um = PairScatter(
            p, lambda k, x: feed.times(up_rows[...]), sx, rx.at[0], sz, None, None, None, None,
            up_ss, up_rs,
        )

        def up_store(k):
            return pltpu.make_async_copy(rx.at[0, k], up_blocks.at[k], up_ss.at[4 + k])

        def rows_backward(m):
            tile_loads(m, "wait")
            here = pl.ds(m * tile, tile)
            hidden_grad = sum(
                dot(
                    early[m % 2, j * tile : (j + 1) * tile, :],
                    weights[j * local : (j + 1) * local, :],
                )
                for j in range(owners)
            )
            for part in range(2):
                units = pl.ds(part * local, local)
                value = hidden_grad[:, part * local : (part + 1) * local]
                for i, ref in enumerate((up_rows, gate_rows)):
                    first = (2 * i + part) * tile
                    factor = early[2 + m % 2, first : first + tile, :]
                    ref[here, units] = (value * factor.astype(F32)).astype(BF)
            if m + 2 < 8:
                tile_loads(m + 2, "start")

        owner = [
            2 * (1 - p.y) + 1 - p.c, 2 * (1 - p.y) + p.c, 2 * p.y + 1 - p.c, 2 * p.y + p.c
        ]

        def weight_loads(n, act):
            start = pl.multiple_of(owner[n] * local, local)
            for i, ref in enumerate((gate_ref, up_ref)):
                copy = pltpu.make_async_copy(
                    ref.at[pl.ds(start, local), :],
                    weights.at[pl.ds((n % 2 * 2 + i) * local, local), :],
                    weights_sem.at[1 + n % 2 * 2 + i],
                )
                getattr(copy, act)()

        def piece_rows(t):
            place = p.zl if t >= 2 else 1 - p.zl
            return pl.ds(pl.multiple_of(place * tokens + t % 2 * piece, piece), piece)

        def core_copy(b, t):
            return remote(
                to_core.at[t], sums.at[b, t], move_ss.at[b, t], move_rs.at[b, t], p.core
            )

        def side_copy(t):
            return remote(sums.at[0, t], from_y.at[t], move_ss.at[2, t], move_rs.at[2, t], p.side)

        def mate_copy(t):
            return remote(sums.at[1, t], from_mate.at[t], move_ss.at[3, t], move_rs.at[3, t], p.mate)

        def partial_sum(n, t):
            here = piece_rows(t)
            first = n % 2 * 2 * local
            return contract_cols(gate_rows[here, :], weights[first : first + local, :]) + contract_cols(
                up_rows[here, :], weights[first + local : first + 2 * local, :]
            )

        def partial_block(n):
            weight_loads(n, "wait")
            for t in range(4):
                value = partial_sum(n, t)
                b = n // 2
                if n % 2 == 0:
                    if b == 1:
                        core_copy(0, t).wait_send()
                    to_core[t] = value.astype(BF)
                    core_copy(b, t).start()
                else:
                    core_copy(b, t).wait_recv()
                    sums[b, t] = (value + sums[b, t].astype(F32)).astype(BF)
                    if b == 0:
                        side_copy(t).start()
            if n + 2 < 4:
                weight_loads(n + 2, "start")

        def to_mate(t):
            side_copy(t).wait_recv()
            sums[1, t] = (sums[1, t].astype(F32) + from_y[t].astype(F32)).astype(BF)
            mate_copy(t).start()

        def final(t):
            side_copy(t).wait_recv()
            mate_copy(t - 2).wait_recv()
            middle_grad[pl.ds((t - 2) * piece, piece), :] = (
                sums[1, t].astype(F32) + from_y[t].astype(F32) + from_mate[t - 2].astype(F32)
            )

        def lane_copies():
            return [
                remote(lanes, near_lanes.at[i], lanes_ss.at[i], lanes_rs.at[i], device)
                for i, device in enumerate((p.core, p.side, diagonal))
            ]

        inverse_lanes = lax.rsqrt(squares_ref[...] / (owners * local) + epsilon)

        def residual_loads(n, act):
            here = pl.ds(n % 4 * quarter, quarter)
            for i, ref in enumerate((middle_ref, out_grad_ref)):
                copy = pltpu.make_async_copy(ref.at[here, :], residual.at[n % 2, i], tile_sem.at[n % 2, i])
                getattr(copy, act)()

        def row_sums():
            total = jnp.zeros((1, local), F32)
            for t in range(4):
                here = pl.ds(t * quarter, quarter)
                residual_loads(t, "wait")
                product = middle_grad[here, :] * residual[t % 2, 0]
                residual_loads(t + 2, "start")
                lanes[:, here] = lanes_of(
                    jnp.sum(product * gain_ref[...], axis=1, keepdims=True)
                )
                inverse = column_of(inverse_lanes[:, t * quarter : (t + 1) * quarter])
                total = total + jnp.sum(product * inverse, axis=0, keepdims=True)
            gain_grad[...] = total
            for copy in lane_copies():
                copy.start()

        spreads = [
            Spread(
                p,
                lambda who, t=t: early.at[who, pl.ds(t * quarter, quarter), :],
                branch_ss.at[t],
                branch_rs.at[t],
            )
            for t in range(4)
        ]

        def residual_grad():
            for copy in lane_copies():
                copy.wait_recv()
            sums_all = (lanes[...] + near_lanes[0] + near_lanes[1] + near_lanes[2]) / (owners * local)
            scale_all = inverse_lanes * inverse_lanes * inverse_lanes * sums_all
            for t in range(4):
                here = pl.ds(t * quarter, quarter)
                part = slice(t * quarter, (t + 1) * quarter)
                residual_loads(4 + t, "wait")
                value = (
                    residual[t % 2, 1]
                    + column_of(inverse_lanes[:, part]) * gain_ref[...] * middle_grad[here, :]
                    - residual[t % 2, 0] * column_of(scale_all[:, part])
                )
                middle_grad[here, :] = value
                early[p.me, here, :] = value.astype(BF)
                spreads[t].start()
                if t + 2 < 4:
                    residual_loads(6 + t, "start")

        def out_store(m, j):
            start = m % (8 // pair) * tile
            return pltpu.make_async_copy(
                to_core.at[j % 2, pl.ds(0, tile), :],
                partials.at[m // (8 // pair), j, pl.ds(start, tile), :],
                tile_sem.at[2, j % 2],
            )

        def out_partial(m):
            for j in range(owners):
                value = contract_cols(
                    hidden_ref[pl.ds(m * tile, tile), :], weights[j * local : (j + 1) * local, :]
                )
                if m > 0 or j >= 2:
                    out_store(m if j >= 2 else m - 1, (j - 2) % owners).wait()
                to_core[j % 2, :tile, :] = value.astype(BF)
                out_store(m, j).start()

        for k in ORDER:
            dm.send_across(k)
        down_load.wait()
        for m in range(3):
            rows_backward(m)
        dm.send_on(FAR, 0)
        for m in range(3, 7):
            rows_backward(m)
        dm.send_on(NEAR, 1)
        rows_backward(7)
        weight_loads(0, "start")
        weight_loads(1, "start")
        dm.send_relay(0)
        partial_block(0)
        partial_block(1)
        dm.mate_rows()
        dm.send_relay(1)
        dm.send_forward()
        dm.sent(FAR)
        gm.send_across(FAR)
        dm.sent(NEAR)
        gm.send_across(NEAR)
        partial_block(2)
        partial_block(3)
        down_again = pltpu.make_async_copy(down_ref, weights, weights_sem.at[0])
        down_again.start()
        to_mate(0)
        dm.own_rows()
        pl.semaphore_signal(free_sem, inc=1, device_id=p.across, device_id_type=MESH)
        dm.sent(MATE)
        gm.send_across(MATE)
        dm.sent(OWN)
        gm.send_across(OWN)
        to_mate(1)
        dm.send_back()
        dm.sent_on(0)
        gm.send_on(FAR, 0)
        dm.sent_on(1)
        gm.send_on(NEAR, 1)
        pl.semaphore_wait(free_sem, 1)
        gm.sent(FAR)
        um.send_across(FAR)
        gm.sent(NEAR)
        um.send_across(NEAR)
        residual_loads(0, "start")
        residual_loads(1, "start")
        down_again.wait()
        for t in range(4):
            core_copy(1, t).wait_send()
        for m in range(8):
            out_partial(m)
        dm.sent_on(2)
        gm.mate_rows()
        gm.sent(MATE)
        um.send_across(MATE)
        final(2)
        final(3)
        row_sums()
        gm.send_relay(0)
        gm.sent(OWN)
        um.send_across(OWN)
        residual_grad()
        dm.finish()
        down_store = pltpu.make_async_copy(weight_grad, down_grad_all, weights_sem.at[1])
        down_store.start()
        gm.send_relay(1)
        gm.send_forward()
        down_store.wait()
        gm.own_rows()
        gm.send_back()
        for t in range(4):
            spreads[t].forward()
        gm.finish()
        gate_store = pltpu.make_async_copy(weight_grad, gate_grad_all, weights_sem.at[1])
        gate_store.start()
        for t in range(4):
            spreads[t].finish()
        gather_done = pltpu.make_async_copy(early, branch_all, early_sem.at[0, 0])
        gather_done.start()
        for k in ORDER:
            total_rows = um.summed(k)
            rx[0, k] = total_rows.astype(BF)
            up_store(k).start()
        for j in range(3):
            gm.sent_on(j)
        um.sent(*ORDER)
        for k in ORDER:
            up_store(k).wait()
        for t in range(4):
            side_copy(t).wait_send()
        for t in range(2):
            mate_copy(t).wait_send()
        for copy in lane_copies():
            copy.wait_send()
        out_store(7, 2).wait()
        out_store(7, 3).wait()
        gather_done.wait()
        gate_store.wait()

    def array(*shape, dtype=F32):
        return jax.ShapeDtypeStruct(shape, dtype)

    return pl.pallas_call(
        kernel,
        out_shape=[
            array(tokens, local),
            array(owners, tokens, local, dtype=BF),
            array(1, local),
            array(pair, owners, tokens, local, dtype=BF),
            array(rows, 2 * half),
            array(rows, 2 * half),
            array(4, rows, half, dtype=BF),
        ],
        in_specs=[ANY, ANY, VMEM, ANY, ANY, ANY, ANY, ANY, ANY, ANY, VMEM, VMEM],
        out_specs=[VMEM, ANY, VMEM, ANY, ANY, ANY, ANY],
        scratch_shapes=[
            pltpu.VMEM((total, half), BF),
            pltpu.VMEM((owners * local, half), BF),
            pltpu.VMEM((2, total, rows), BF),
            pltpu.VMEM((owners, tokens, local), BF),
            pltpu.VMEM((4, piece, local), BF),
            pltpu.VMEM((2, 4, piece, local), BF),
            pltpu.VMEM((4, piece, local), BF),
            pltpu.VMEM((2, piece, local), BF),
            pltpu.VMEM((8, tokens), F32),
            pltpu.VMEM((3, 8, tokens), F32),
            pltpu.VMEM((2, 2, tokens // 4, local), F32),
            pltpu.VMEM((rows, 2 * half), F32),
            pltpu.SemaphoreType.DMA((2, pair)),
            pltpu.SemaphoreType.DMA((2, 8)),
            pltpu.SemaphoreType.DMA((5,)),
            pltpu.SemaphoreType.DMA((4, 4)),
            pltpu.SemaphoreType.DMA((4, 4)),
            pltpu.SemaphoreType.DMA((3,)),
            pltpu.SemaphoreType.DMA((3,)),
            pltpu.SemaphoreType.DMA((4, 3)),
            pltpu.SemaphoreType.DMA((4, 3)),
            pltpu.SemaphoreType.DMA((3, 2)),
            pltpu.VMEM((total, half), BF),
            pltpu.SemaphoreType.DMA((8,)),
            pltpu.SemaphoreType.DMA((4,)),
            pltpu.SemaphoreType.REGULAR,
        ]
        + pair_scatter_scratch(2, rows, half),
        compiler_params=pltpu.CompilerParams(
            collective_id=collective, has_side_effects=True, vmem_limit_bytes=62 << 20
        ),
        cost_estimate=pl.CostEstimate(flops=0, bytes_accessed=300 << 20, transcendentals=0),
        name="feed_forward_backward",
    )(
        out_rows, normed, hidden, silu, slope, gate, up, down, middle, out_grad, squares, gain
    )


class LineScatter:
    def __init__(self, p, product, sx, rx, sz, rz, rm, held, out, ss, rs):
        self.p, self.product = p, product
        self.sx, self.rx, self.sz, self.rz, self.rm = sx, rx, sz, rz, rm
        self.held, self.out, self.ss, self.rs = held, out, ss, rs

    def across(self, k):
        return remote(self.sx.at[k], self.rx.at[k], self.ss.at[k], self.rs.at[k], self.p.across)

    def outward(self, j):
        return remote(self.sz.at[j], self.rz.at[j], self.ss.at[4 + j], self.rs.at[4 + j], self.p.mate)

    def middle(self, j):
        return remote(self.sz.at[j], self.rm.at[j], self.ss.at[7 + j], self.rs.at[7 + j], self.p.mid)

    def back(self):
        return remote(self.sz.at[2], self.rz.at[0], self.ss.at[4], self.rs.at[4], self.p.mate)

    def send_across(self, k):
        self.sx[k] = self.product(k, 1 - self.p.x).astype(BF)
        self.across(k).start()

    def summed(self, k):
        total = self.product(k, self.p.x)
        self.across(k).wait_recv()
        return total + self.rx[k].astype(F32)

    def send_on(self, k, j):
        total = self.summed(k)

        @pl.when(self.p.outer)
        def _():
            self.sz[j] = total.astype(BF)
            self.outward(j).start()

        @pl.when(self.p.inner)
        def _():
            self.outward(j).wait_recv()
            self.sz[j] = (total + self.rz[j].astype(F32)).astype(BF)
            self.middle(j).start()

    def mate_rows(self):
        total = self.summed(MATE)

        @pl.when(self.p.outer)
        def _():
            self.sz[2] = total.astype(BF)
            self.outward(2).start()

        @pl.when(self.p.inner)
        def _():
            self.held[...] = total

    def own_rows(self):
        self.out[...] = self.summed(OWN)

    def send_back(self):
        @pl.when(self.p.inner)
        def _():
            self.middle(0).wait_recv()
            self.sz[2] = (self.held[...] + self.rm[0].astype(F32)).astype(BF)
            self.back().start()

    def finish(self):
        @pl.when(self.p.inner)
        def _():
            self.outward(2).wait_recv()
            self.middle(1).wait_recv()
            self.out[...] = self.out[...] + self.rz[2].astype(F32) + self.rm[1].astype(F32)
            for j in range(2):
                self.middle(j).wait_send()
            self.back().wait_send()

        @pl.when(self.p.outer)
        def _():
            self.back().wait_recv()
            self.out[...] = self.out[...] + self.rz[0].astype(F32)
            for j in range(3):
                self.outward(j).wait_send()

        for k in range(4):
            self.across(k).wait_send()


def mixer_backward(
    up_blocks, branch, whole_out, in_matrix, projected, convolved, mixed, gated, normed_in,
    masks, conv_weight, stream, middle_grad, gain, inverse, gain_mid_grad, partials, middle, collective,
):
    owners, tokens, local = branch.shape
    rows, half = up_blocks.shape[1:]
    three = in_matrix.shape[1]
    tile = tokens // 4
    groups = three // local

    def kernel(*refs):
        refs = (None,) + refs
        up_ref, branch_ref, out_ref, in_ref, projected_ref, convolved_ref = refs[1:7]
        mixed_ref, gated_ref, normed_in_ref, masks_ref, conv_ref, stream_ref = refs[7:13]
        middle_ref, gain_ref, inverse_ref, gain_mid_ref = refs[13:17]
        partials_ref, residual_ref = refs[17:19]
        refs = refs[:17] + refs[19:]
        stream_grad, small_sums, up_grad, out_grad, in_grad = refs[17:22]
        result_all = refs[22]
        refs = refs[:22] + refs[23:]
        conv_grad, rows_grad, stage, stage_mixed, weights, to_core, sums, from_y, lanes, near_lanes = refs[22:32]
        smalls, cols, stage_sem, in_sem, move_ss, move_rs, lanes_ss, lanes_rs = refs[32:40]
        small_ss, small_rs, halo_sem, cols_sem = refs[40:44]
        branch_sem = refs[59]
        res_sums, res_y, res_mate, res_own, res_ss, res_rs, res_sem = refs[60:]
        own_block, up_sem, sz, rz, rm, held, ss, rs = refs[44:52]
        lx, lrx, lz, lrz, lrm, lss, lrs = refs[52:59]

        p = Place()
        p.core = (p.zh, p.zl, p.x, p.y, 1 - p.c)
        p.side = (p.zh, p.zl, p.x, 1 - p.y, p.c)
        diagonal = (p.zh, p.zl, p.x, 1 - p.y, 1 - p.c)
        place = 2 * p.z + p.x
        last = 7

        def device_at(s):
            return (s // 4, s // 2 % 2, s % 2, p.y, p.c)

        others = [lax.rem(place + d, 8) for d in range(1, 8)]

        jobs = []
        for t in range(4):
            jobs.append(((projected_ref, 1), (convolved_ref, 0), t))
        for t in range(4):
            jobs.append(((projected_ref, 0), (projected_ref, 2), t))
        for _ in range(2):
            for t in range(4):
                jobs.append(((stream_ref, 0), (middle_ref, 0), t))
        taken = []

        def stage_copies(n, act):
            for i, (ref, group) in enumerate(jobs[n][:2]):
                copy = pltpu.make_async_copy(
                    ref.at[pl.ds(jobs[n][2] * tile, tile), pl.ds(group * local, local)],
                    stage.at[n % 2, i],
                    stage_sem.at[n % 2, i],
                )
                getattr(copy, act)()

        def mixed_load(t):
            return pltpu.make_async_copy(
                mixed_ref.at[pl.ds(t * tile, tile + 8), :], stage_mixed.at[t % 2], stage_sem.at[t % 2, 2]
            )

        def branch_slot(t, j):
            return to_core.at[j] if t % 2 == 0 else lz.at[j // 3, j % 3]

        def branch_loads(t, act):
            for j in range(owners):
                copy = pltpu.make_async_copy(
                    branch_ref.at[0, j, pl.ds(t * tile, tile), :], branch_slot(t, j), branch_sem.at[t % 2, j]
                )
                getattr(copy, act)()

        def staged():
            n = len(taken)
            taken.append(n)
            stage_copies(n, "wait")
            values = stage[n % 2, 0], stage[n % 2, 1]
            return values

        def staged_done():
            n = len(taken) - 1
            if n + 2 < len(jobs):
                stage_copies(n + 2, "start")

        def out_loads(act):
            for j in range(owners):
                copy = pltpu.make_async_copy(
                    out_ref.at[pl.ds(j * local, local), :], weights.at[j], in_sem.at[j]
                )
                getattr(copy, act)()

        for k in ORDER:
            pltpu.make_async_copy(
                up_ref.at[k], own_block if k == OWN else sz.at[(None, 2, 1, 0)[k]], up_sem.at[k]
            ).start()
        out_loads("start")
        stage_copies(0, "start")
        stage_copies(1, "start")
        branch_loads(0, "start")
        branch_loads(1, "start")
        mixed_load(0).start()
        mixed_load(1).start()
        feed_jobs = [(branch_ref, k, True) for k in ORDER]
        feed_jobs += [(normed_in_ref, k, True) for k in ORDER]
        feed_jobs += [(branch_ref, k, False) for k in ORDER]
        feed_jobs += [(normed_in_ref, k, False) for k in ORDER]
        feed = Columns(p, feed_jobs, cols, cols_sem)
        owner = [
            2 * (1 - p.y) + 1 - p.c, 2 * (1 - p.y) + p.c, 2 * p.y + 1 - p.c, 2 * p.y + p.c
        ]
        p.enter_all([device_at(s) for s in others] + [p.core, p.side, diagonal])

        um = PairScatter(p, None, None, None, sz, rz, rm, None, up_grad, ss, rs)

        def up_load(k):
            target = own_block if k == OWN else sz.at[(None, 2, 1, 0)[k]]
            return pltpu.make_async_copy(up_ref.at[k], target, up_sem.at[k])

        def up_send(k, j):
            up_load(k).wait()

            @pl.when(p.outer)
            def _():
                um.outward(j).start()

            if j < 2:

                @pl.when(p.inner)
                def _():
                    um.middle(j).start()

        def up_back():
            @pl.when(p.inner)
            def _():
                um.relay(0).wait_recv()
                sz[2] = (sz[2].astype(F32) + rm[2].astype(F32)).astype(BF)
                um.back().start()

        om = LineScatter(
            p, lambda k, x: feed.times(gated_ref[...]), lx.at[0], lrx.at[0], lz.at[0], lrz.at[0], lrm.at[0], held,
            out_grad, lss.at[0], lrs.at[0],
        )
        ims = [
            LineScatter(
                p, lambda k, x, g=g: feed.times_next(rows_grad[g], g == 0, g == groups - 1),
                lx.at[1 + g], lrx.at[1 + g], lz.at[1 + g], lrz.at[1 + g], lrm.at[1 + g],
                held, in_grad.at[:, pl.ds(g * local, local)], lss.at[1 + g], lrs.at[1 + g],
            )
            for g in range(groups)
        ]

        def halo_copy():
            return remote(
                conv_grad.at[pl.ds(0, 8), :],
                conv_grad.at[pl.ds(tokens, 8), :],
                halo_sem.at[0],
                halo_sem.at[1],
                device_at(others[6]),
            )

        taps = [jnp.zeros((1, local), F32) for _ in range(3)]

        def gated_backward(t):
            here = pl.ds(t * tile, tile)
            branch_loads(t, "wait")
            gated_grad = sum(
                dot(branch_slot(t, j)[...], weights[j])
                for j in range(owners)
            )
            if t + 2 < 4:
                branch_loads(t + 2, "start")
            out_gate, conv = staged()
            mixed_load(t).wait()
            near = stage_mixed.at[t % 2]
            rows_grad[1, here, :] = (gated_grad * conv).astype(BF)
            value = gated_grad * out_gate
            conv_grad[here, :] = value
            staged_done()
            taps[0] += jnp.sum(value * near[pl.ds(8, tile), :], axis=0, keepdims=True)
            taps[1] += jnp.sum(
                masks_ref[here, 0:1] * value * near[pl.ds(7, tile), :],
                axis=0, keepdims=True,
            )
            taps[2] += jnp.sum(
                masks_ref[here, 1:2] * value * near[pl.ds(6, tile), :],
                axis=0, keepdims=True,
            )
            if t + 2 < 4:
                mixed_load(t + 2).start()

        def send_halo():
            @pl.when(place > 0)
            def _():
                halo_copy().start()

        def take_halo():
            @pl.when(place < last)
            def _():
                halo_copy().wait_recv()

            @pl.when(place == last)
            def _():
                conv_grad[tokens:, :] = jnp.zeros((8, local), F32)

        def conv_backward(t):
            here = pl.ds(t * tile, tile)
            in_gate, carried = staged()
            value = (
                conv_ref[0:1, :] * conv_grad[here, :]
                + masks_ref[here, 2:3] * conv_ref[1:2, :] * conv_grad[pl.ds(1 + t * tile, tile), :]
                + masks_ref[here, 3:4] * conv_ref[2:3, :] * conv_grad[pl.ds(2 + t * tile, tile), :]
            )
            rows_grad[0, here, :] = (value * carried).astype(BF)
            rows_grad[2, here, :] = (value * in_gate).astype(BF)
            staged_done()

        def in_loads(n, act):
            start = pl.multiple_of(owner[n] * local, local)
            for g in range(groups):
                copy = pltpu.make_async_copy(
                    in_ref.at[pl.ds(start, local), pl.ds(g * local, local)], weights.at[g], in_sem.at[g]
                )
                getattr(copy, act)()

        def core_copy(b, t):
            return remote(to_core.at[t], sums.at[b, t], move_ss.at[b, t], move_rs.at[b, t], p.core)

        def side_copy(t):
            return remote(sums.at[0, t], from_y.at[t], move_ss.at[2, t], move_rs.at[2, t], p.side)

        def partial_block(n):
            in_loads(n, "wait")
            b = n // 2
            for t in range(4):
                here = pl.ds(t * tile, tile)
                value = sum(
                    contract_cols(rows_grad[g, here, :], weights[g])
                    for g in range(groups)
                )
                if n % 2 == 0:
                    if b == 1:
                        core_copy(0, t).wait_send()
                    to_core[t] = value.astype(BF)
                    core_copy(b, t).start()
                else:
                    core_copy(b, t).wait_recv()
                    value = value + sums[b, t].astype(F32)
                    if b == 0:
                        sums[b, t] = value.astype(BF)
                        side_copy(t).start()
                    else:
                        stream_grad[here, :] = value
            if n + 1 < 4:
                in_loads(n + 1, "start")

        piece = tokens // 2

        def res_source(j, t):
            place = p.zl if t >= 2 else 1 - p.zl
            return partials_ref.at[place, j, pl.ds(t % 2 * piece, piece), :]

        def res_core(b, t):
            return remote(
                res_source(owner[2 * b], t), res_sums.at[b, t], res_ss.at[b, t], res_rs.at[b, t], p.core
            )

        def res_side(t):
            return remote(res_sums.at[0, t], res_y.at[t], res_ss.at[2, t], res_rs.at[2, t], p.side)

        def res_send(t):
            return remote(res_sums.at[1, t], res_mate.at[t], res_ss.at[3, t], res_rs.at[3, t], p.mate)

        def res_load(n):
            source = res_source(owner[2 * (n // 4) + 1], n % 4)
            return pltpu.make_async_copy(source, res_own.at[n % 2], res_sem.at[n % 2])

        def res_residual(i):
            here = pl.ds(i * tile, tile)
            return pltpu.make_async_copy(residual_ref.at[here, :], stage.at[i % 2, i // 2], res_sem.at[2 + i])

        def res_store(i):
            here = pl.ds(i * tile, tile)
            return pltpu.make_async_copy(stage.at[i % 2, i // 2], result_all.at[here, :], res_sem.at[6 + i])

        def res_add(n, *others):
            res_load(n).wait()
            b, t = n // 4, n % 4
            res_core(b, t).wait_recv()
            for part in range(2):
                here = pl.ds(part * tile, tile)
                value = res_own[n % 2, here, :].astype(F32) + res_sums[b, t, here, :].astype(F32)
                for other in others:
                    value = value + other[here, :].astype(F32)
                if n < 6:
                    res_sums[b, t, here, :] = value.astype(BF)
                else:
                    i = (n - 6) * 2 + part
                    res_residual(i).wait()
                    slot = stage.at[part, n - 6]
                    slot[...] = slot[...] + value
                    res_store(i).start()
            if n + 2 < 8:
                res_load(n + 2).start()

        def res_to_side(t):
            res_add(t)
            res_side(t).start()

        def res_to_mate(t):
            res_side(t).wait_recv()
            res_add(4 + t, res_y.at[t])
            res_send(t).start()

        def res_final(t):
            res_side(t).wait_recv()
            res_send(t - 2).wait_recv()
            res_add(4 + t, res_y.at[t], res_mate.at[t - 2])

        def lane_copies():
            return [
                remote(lanes, near_lanes.at[i], lanes_ss.at[i], lanes_rs.at[i], device)
                for i, device in enumerate((p.core, p.side, diagonal))
            ]

        def small_copies():
            return [
                remote(
                    smalls.at[place], smalls.at[place], small_ss.at[d], small_rs.at[place], device_at(s)
                )
                for d, s in enumerate(others)
            ]

        def row_sums():
            total_gain = jnp.zeros((1, local), F32)
            for t in range(4):
                here = pl.ds(t * tile, tile)
                side_copy(t).wait_recv()
                value = stream_grad[here, :] + from_y[t].astype(F32)
                stream_grad[here, :] = value
                values = staged()[0]
                staged_done()
                product = value * values
                lanes[:, here] = lanes_of(jnp.sum(product * gain_ref[...], axis=1, keepdims=True))
                inverse_here = column_of(inverse_ref[:, here])
                total_gain = total_gain + jnp.sum(product * inverse_here, axis=0, keepdims=True)
            for copy in lane_copies():
                copy.start()
            smalls[place] = jnp.concatenate(
                taps + [total_gain, gain_mid_ref[...], jnp.zeros((3, local), F32)], axis=0
            )
            for copy in small_copies():
                copy.start()

        def input_grad():
            for copy in lane_copies():
                copy.wait_recv()
            sums_all = (lanes[...] + near_lanes[0] + near_lanes[1] + near_lanes[2]) / (owners * local)
            scale_all = inverse_ref[...] * inverse_ref[...] * inverse_ref[...] * sums_all
            for t in range(4):
                here = pl.ds(t * tile, tile)
                values, residual = staged()
                stream_grad[here, :] = (
                    residual
                    + column_of(inverse_ref[:, here]) * gain_ref[...] * stream_grad[here, :]
                    - values * column_of(scale_all[:, t * tile : (t + 1) * tile])
                )
                staged_done()

        def sum_smalls():
            for s in others:
                block = smalls.at[s]
                remote(block, block, small_ss.at[0], small_rs.at[s], p.mate).wait_recv()
            value = smalls[0]
            for s in range(1, 8):
                value = value + smalls[s]
            small_sums[...] = value

        for b in range(2):
            for t in range(4):
                res_core(b, t).start()
        res_load(0).start()
        res_load(1).start()
        up_send(FAR, 0)
        up_send(NEAR, 1)
        up_send(MATE, 2)
        out_loads("wait")
        for t in range(4):
            gated_backward(t)
            if t == 0:
                send_halo()
            else:
                res_to_side(t - 1)
        in_loads(0, "start")
        res_to_side(3)
        um.send_relay(0)
        take_halo()
        for t in range(4):
            conv_backward(t)
        for k in ORDER:
            om.send_across(k)
        for k in (FAR, NEAR):
            for m in ims:
                m.send_across(k)
        um.send_relay(1)
        um.send_forward()
        res_to_mate(0)
        res_to_mate(1)
        partial_block(0)
        partial_block(1)
        for k in (MATE, OWN):
            for m in ims:
                m.send_across(k)
        up_load(OWN).wait()
        up_grad[:, um.cols_of(p.zl)] = own_block[...].astype(F32)
        up_back()
        partial_block(2)
        partial_block(3)
        om.send_on(FAR, 0)
        om.send_on(NEAR, 1)
        om.mate_rows()
        om.own_rows()
        om.send_back()
        um.finish()
        for m in ims:
            m.send_on(FAR, 0)
        row_sums()
        for m in ims:
            m.send_on(NEAR, 1)
        input_grad()
        for i in range(4):
            res_residual(i).start()
        om.finish()
        for m in ims:
            m.mate_rows()
            m.send_back()
        res_final(2)
        res_final(3)
        sum_smalls()
        for m in ims:
            m.own_rows()
        for m in ims:
            m.finish()
        for i in range(4):
            res_store(i).wait()
        for t in range(4):
            res_core(0, t).wait_send()
            res_core(1, t).wait_send()
            res_side(t).wait_send()
        for t in range(2):
            res_send(t).wait_send()
        for j in range(3):
            um.sent_on(j)
        for t in range(4):
            core_copy(1, t).wait_send()
            side_copy(t).wait_send()
        for copy in lane_copies() + small_copies():
            copy.wait_send()

        @pl.when(place > 0)
        def _():
            halo_copy().wait_send()

    def array(*shape):
        return jax.ShapeDtypeStruct(shape, F32)

    n = 1 + groups
    return pl.pallas_call(
        kernel,
        out_shape=[
            array(tokens, local),
            array(8, local),
            array(rows, 2 * half),
            array(rows, local),
            array(rows, three),
            array(tokens, local),
        ],
        in_specs=[ANY, ANY, ANY, ANY, ANY, ANY, ANY, VMEM, ANY, VMEM, VMEM, ANY, ANY]
        + [VMEM] * 3
        + [ANY, ANY],
        out_specs=[VMEM] * 5 + [ANY],
        scratch_shapes=[
            pltpu.VMEM((tokens + 8, local), F32),
            pltpu.VMEM((groups, tokens, local), BF),
            pltpu.VMEM((2, 2, tile, local), F32),
            pltpu.VMEM((2, tile + 8, local), F32),
            pltpu.VMEM((owners, local, local), BF),
            pltpu.VMEM((4, tile, local), BF),
            pltpu.VMEM((2, 4, tile, local), BF),
            pltpu.VMEM((4, tile, local), BF),
            pltpu.VMEM((8, tokens), F32),
            pltpu.VMEM((3, 8, tokens), F32),
            pltpu.VMEM((8, 8, local), F32),
            pltpu.VMEM((2, tokens, rows), BF),
            pltpu.SemaphoreType.DMA((2, 3)),
            pltpu.SemaphoreType.DMA((owners,)),
            pltpu.SemaphoreType.DMA((3, 4)),
            pltpu.SemaphoreType.DMA((3, 4)),
            pltpu.SemaphoreType.DMA((3,)),
            pltpu.SemaphoreType.DMA((3,)),
            pltpu.SemaphoreType.DMA((7,)),
            pltpu.SemaphoreType.DMA((8,)),
            pltpu.SemaphoreType.DMA((2,)),
            pltpu.SemaphoreType.DMA((2, 1)),
            pltpu.VMEM((rows, half), BF),
            pltpu.SemaphoreType.DMA((4,)),
            pltpu.VMEM((3, rows, half), BF),
            pltpu.VMEM((3, rows, half), BF),
            pltpu.VMEM((4, rows, half), BF),
            pltpu.VMEM((rows, local), F32),
            pltpu.SemaphoreType.DMA((11,)),
            pltpu.SemaphoreType.DMA((11,)),
            pltpu.VMEM((n, 4, rows, local), BF),
            pltpu.VMEM((n, 4, rows, local), BF),
            pltpu.VMEM((n, 3, rows, local), BF),
            pltpu.VMEM((n, 3, rows, local), BF),
            pltpu.VMEM((n, 2, rows, local), BF),
            pltpu.SemaphoreType.DMA((n, 9)),
            pltpu.SemaphoreType.DMA((n, 9)),
            pltpu.SemaphoreType.DMA((2, owners)),
            pltpu.VMEM((2, 4, tokens // 2, local), BF),
            pltpu.VMEM((4, tokens // 2, local), BF),
            pltpu.VMEM((2, tokens // 2, local), BF),
            pltpu.VMEM((2, tokens // 2, local), BF),
            pltpu.SemaphoreType.DMA((4, 4)),
            pltpu.SemaphoreType.DMA((4, 4)),
            pltpu.SemaphoreType.DMA((10,)),
        ],
        compiler_params=pltpu.CompilerParams(
            collective_id=collective, has_side_effects=True, vmem_limit_bytes=62 << 20
        ),
        cost_estimate=pl.CostEstimate(flops=0, bytes_accessed=300 << 20, transcendentals=0),
        name="mixer_backward",
    )(
        up_blocks, branch[None], whole_out, in_matrix, projected, convolved, mixed, gated,
        normed_in[None], masks, conv_weight, stream, middle_grad, gain, inverse, gain_mid_grad, partials,
        middle,
    )


SEQ = ("zh", "zl", "x")
TP = ("y", "c")
PAIR = ("zl", "y", "c")


def after(value, *others):
    return lax.optimization_barrier((value, *others))[0]


def gather_pair_rows(rows):
    blocks = lax.all_gather(rows, PAIR, axis=0)
    return blocks.reshape(lax.axis_size("zl"), lax.axis_size(TP), *rows.shape)


def paired_on_device(
    stream,
    norm1_gain,
    in_weight,
    conv_weight,
    out_weight,
    norm2_gain,
    gate_weight,
    up_weight,
    down_weight,
    doc_starts,
    out_grad,
):
    tokens, local = stream.shape
    rows_here = in_weight.shape[0]
    positions = lax.axis_index(SEQ) * tokens + jnp.arange(tokens, dtype=jnp.int32)
    mask_one, mask_two = lag_masks(doc_starts, positions)
    (
        in_matrix, whole_out, whole_gate, whole_up, whole_down, normed_in, projected, convolved, gated,
        normed_mid, hidden, silu, slope, mixed, middle, squares, first_squares,
    ) = block_forward(
        stream,
        jnp.stack([mask_one, mask_two]),
        conv_weight,
        norm1_gain[None],
        norm2_gain[None],
        in_weight.reshape(rows_here, 3 * local),
        out_weight,
        gate_weight,
        up_weight,
        down_weight,
        0,
    )
    out_full = gather_pair_rows(out_grad.astype(BF))
    mean_square = squares[0] / (local * lax.axis_size(TP)) + epsilon
    rms_mid = jnp.sqrt(mean_square)
    first_mean = first_squares / (local * lax.axis_size(TP)) + epsilon
    rms_in, inverse_in = jnp.sqrt(first_mean[0]), lax.rsqrt(first_mean)
    middle_grad, branch_blocks, gain_mid_grad, ffn_partial, down_weight_grad, gate_weight_grad, up_blocks = (
        feed_forward_backward(
            out_full, normed_mid, hidden, silu, slope, whole_gate, whole_up, whole_down, middle, out_grad,
            squares, norm2_gain[None], 4,
        )
    )
    next_one, next_two = lag_masks(doc_starts, positions + 1)[0], lag_masks(doc_starts, positions + 2)[1]
    count = tokens * lax.axis_size(SEQ)
    masks = jnp.concatenate(
        [
            mask_one,
            mask_two,
            jnp.where(positions[:, None] + 1 < count, next_one, 0.0),
            jnp.where(positions[:, None] + 2 < count, next_two, 0.0),
        ],
        axis=1,
    )
    stream_grad, small_sums, up_weight_grad, out_weight_grad, in_weight_grad, result = mixer_backward(
        up_blocks, branch_blocks, whole_out, in_matrix, projected, convolved, mixed, gated,
        normed_in, masks, conv_weight, stream, middle_grad, norm1_gain[None],
        inverse_in, gain_mid_grad, ffn_partial, middle, 5,
    )
    conv_total, gain_in_total, gain_mid_total = small_sums[:3], small_sums[3], small_sums[4]
    return (
        result,
        stream_grad,
        gain_in_total,
        in_weight_grad.reshape(rows_here, 3, local),
        conv_total,
        out_weight_grad,
        gain_mid_total,
        gate_weight_grad,
        up_weight_grad,
        down_weight_grad,
        jnp.stack([rms_in, rms_mid]),
    )


def solution(mesh):
    seq, tp = mesh.shape["seq"], mesh.shape["tp"]
    if (seq, tp) == (8, 4):
        shape, names = (2, 2, 2, 2, 2), ("zh", "zl", "x", "y", "c")
        mesh = Mesh(mesh.devices.reshape(shape), names)
        body, rows, cols = paired_on_device, SEQ, TP
    else:
        body, rows, cols = on_device, "seq", "tp"
    return jax.shard_map(
        body,
        mesh=mesh,
        in_specs=(
            P(rows, cols),
            P(cols),
            P(rows, None, cols),
            P(None, cols),
            P(rows, cols),
            P(cols),
            P(rows, cols),
            P(rows, cols),
            P(rows, cols),
            P(),
            P(rows, cols),
        ),
        out_specs=(
            P(rows, cols),
            P(rows, cols),
            P(cols),
            P(rows, None, cols),
            P(None, cols),
            P(rows, cols),
            P(cols),
            P(rows, cols),
            P(rows, cols),
            P(rows, cols),
            P(None, rows),
        ),
        check_vma=False,
    )
```
